32 devices in a mesh: depth: 8 (over z, x), height: 4 (over y, core).
Axes of the slice: x: 2, y: 2, z: 4, core: 2. Of those that a mesh axis runs over, the one named last changes fastest.
Arguments:
- images: float32 [1, 32, 16, 64], P(None, 'depth', 'height'), may hold values from -9 to 9
- labels: int32 [1, 32, 16, 64], P(None, 'depth', 'height'), may hold values from 0 to 2
- weights: float32 [837927], replicated, may hold values from -3 to 3
- first_moment: float32 [837927], replicated, may hold values from -0.0001 to 0.0001
- second_moment: float32 [837927], replicated, may hold values from 0 to 0.0001, as said below
Outputs:
- grad_norm: float32 [], replicated
- moment_first: float32 [837927], replicated
- moment_second: float32 [837927], replicated
- weights_new: float32 [837927], replicated
- weights_copy: bfloat16 [837927], replicated
The draws below stay inside these ranges and needn't reach their ends.
Inputs may be any that keep to these rules, and one draw needn't show every extreme that they name: `second_moment`: entries are positive.
All inputs are finite; a program needn't handle non-finite values.
Results may differ from the reference program's by a relative error of at most 0.0075.
Values may be sent and summed in bfloat16 or wider, within the bound.
No kernel may reach another device: no remote copies, remote signals or barrier semaphores. Data moves between devices by JAX's collectives and lax.ppermute only.
A program may use at most 192 MiB of HBM per device.

```python
import math
import jax
import jax.numpy as jnp
from jax import lax

C1 = 32
C2 = 64
C3 = 128
CG = 32
CLS = 3
WX = 64
CROPS = 1
STEP = 10
DEPTH = 32
HEIGHT = 16
PARAMS = 837927


CLIP_NORM = 0.005


def layout_drawn():
    norm_width = C1 + 4 * C2 + C3
    return [('conv_first', (27, C1, 1)), ('conv_second', (27, C2, C1)), ('conv_third', (27, C2, C2)), ('conv_coarse', (27, C3, C2)), ('conv_merge', (27, C2, C2 + C3)), ('conv_final', (27, C2, C2)), ('gate_skip', (CG, C2)), ('gate_coarse', (CG, C3)), ('gate_bias', (CG,)), ('gate_score', (CG,)), ('score_bias', (1,)), ('head_fine', (CLS, C2)), ('bias_fine', (CLS,)), ('head_coarse', (CLS, C3)), ('bias_coarse', (CLS,)), ('gains', (norm_width,)), ('shifts', (norm_width,))]


def segment_spread():
    table = {'gate_skip': C2 ** (-0.5), 'gate_coarse': C3 ** (-0.5), 'gate_bias': 0.5, 'gate_score': 2.0 * CG ** (-0.5), 'score_bias': 0.5, 'head_fine': 2.0 * C2 ** (-0.5), 'bias_fine': 0.3, 'head_coarse': 2.0 * C3 ** (-0.5), 'bias_coarse': 0.3, 'gains': 0.2, 'shifts': 0.3}
    spreads = []
    centers = []
    for entry_name, entry_shape in layout_drawn():
        length = math.prod(entry_shape)
        spread = table.get(entry_name, (27.0 * entry_shape[-1]) ** (-0.5))
        spreads.append(jnp.full((length,), spread, jnp.float32))
        centers.append(jnp.full((length,), 1.0 if entry_name == 'gains' else 0.0, jnp.float32))
    return (jnp.concatenate(spreads), jnp.concatenate(centers))


def draw_weights(key, part):
    key = jax.random.fold_in(key, 1)
    spreads, centers = segment_spread()
    noise_draw = jnp.clip(jax.random.normal(key, (PARAMS,), jnp.float32), -3.0, 3.0)
    return centers + spreads * noise_draw


def draw_first_moment(key, part):
    key = jax.random.fold_in(key, 2)
    typical = CLIP_NORM / math.sqrt(PARAMS)
    return 0.11 * typical * jnp.clip(jax.random.normal(key, (PARAMS,), jnp.float32), -3.0, 3.0)


def draw_second_moment(key, part):
    key = jax.random.fold_in(key, 3)
    typical = CLIP_NORM / math.sqrt(PARAMS)
    factor = jnp.exp(jax.random.uniform(key, (PARAMS,), jnp.float32, 0.0, math.log(4.0)))
    return 0.001 * typical * typical * factor


def draw_images(key, part):
    key = jax.random.fold_in(key, 4)
    shape_all = (CROPS, DEPTH, HEIGHT, WX)
    depth_pos = jnp.arange(DEPTH, dtype=jnp.float32)[None, :, None, None] / (DEPTH - 1)
    return (1.0 + 2.0 * depth_pos) * jnp.clip(jax.random.normal(key, shape_all, jnp.float32), -3.0, 3.0)


def draw_labels(key, part):
    key = jax.random.fold_in(key, 5)
    shape_all = (CROPS, DEPTH, HEIGHT, WX)
    uniform_int = jax.random.randint(key, shape_all, 0, 1000)
    depth_pos = jnp.arange(DEPTH, dtype=jnp.int32)[None, :, None, None]
    upper_cut = 850 - 300 * depth_pos // (DEPTH - 1)
    return (uniform_int >= 333).astype(jnp.int32) + (uniform_int >= upper_cut).astype(jnp.int32)


def setup_inputs(seed: int = 0) -> dict:
    keys = jax.random.split(jax.random.key(seed), 6)
    images = draw_images(jax.random.fold_in(keys[5], 71), 0)
    labels = draw_labels(jax.random.fold_in(keys[5], 71), 0)
    weights = draw_weights(jax.random.fold_in(keys[5], 71), 0)
    first_moment = draw_first_moment(jax.random.fold_in(keys[5], 71), 0)
    second_moment = draw_second_moment(jax.random.fold_in(keys[5], 71), 0)
    return {"images": images, "labels": labels, "weights": weights, "first_moment": first_moment, "second_moment": second_moment}


@jax.custom_vjp
def low(v):
    return lax.optimization_barrier(v.astype(jnp.bfloat16)).astype(jnp.float32)

@jax.custom_vjp
def low_back(v):
    return v

def low_keep(v):
    return (low(v), None)

def low_pass(kept, grad):
    return (grad,)

def back_keep(v):
    return (v, None)

def back_low(kept, grad):
    return (low(grad),)
low.defvjp(low_keep, low_pass)
low_back.defvjp(back_keep, back_low)
EPS_NORM = 1e-05
CLIP_NORM = 0.005
LEARN_RATE = 0.02
BETA_ONE = 0.9
BETA_TWO = 0.999
ADAM_EPS = 1e-08
DECAY_RATE = 0.01
PRECISE = lax.Precision.HIGHEST

def layout():
    norm_width = C1 + 4 * C2 + C3
    return [('conv_first', (27, C1, 1)), ('conv_second', (27, C2, C1)), ('conv_third', (27, C2, C2)), ('conv_coarse', (27, C3, C2)), ('conv_merge', (27, C2, C2 + C3)), ('conv_final', (27, C2, C2)), ('gate_skip', (CG, C2)), ('gate_coarse', (CG, C3)), ('gate_bias', (CG,)), ('gate_score', (CG,)), ('score_bias', (1,)), ('head_fine', (CLS, C2)), ('bias_fine', (CLS,)), ('head_coarse', (CLS, C3)), ('bias_coarse', (CLS,)), ('gains', (norm_width,)), ('shifts', (norm_width,))]

def unpack(flat):
    pieces = {}
    offset = 0
    for entry_name, entry_shape in layout():
        length = math.prod(entry_shape)
        pieces[entry_name] = flat[offset:offset + length].reshape(entry_shape)
        offset += length
    return pieces

def norm_bounds():
    widths = [C1, C2, C2, C3, C2, C2]
    return [(sum(widths[:layer_id]), widths[layer_id]) for layer_id in range(6)]

def conv_whole(volume, kernel):
    padded = jnp.pad(volume, ((0, 0), (0, 0), (1, 1), (1, 1), (1, 1)))
    out_z, out_y, out_x = volume.shape[2:]
    result = jnp.zeros((kernel.shape[1],) + volume.shape[1:], jnp.float32)
    for tap_id in range(27):
        shift_z, shift_y, shift_x = (tap_id // 9, tap_id // 3 % 3, tap_id % 3)
        window = padded[:, :, shift_z:shift_z + out_z, shift_y:shift_y + out_y, shift_x:shift_x + out_x]
        result = result + jnp.einsum('oi,inzyx->onzyx', kernel[tap_id], window, precision=PRECISE)
    return result

def norm_act(conv_out, gain_part, bias_part):
    samples = conv_out[0].size
    average = lax.optimization_barrier(jnp.sum(conv_out, axis=(1, 2, 3, 4))) / samples
    squares = lax.optimization_barrier(jnp.sum(conv_out * conv_out, axis=(1, 2, 3, 4))) / samples
    inv_scale = lax.rsqrt(squares - average * average + EPS_NORM)
    normed = (conv_out - average[:, None, None, None, None]) * inv_scale[:, None, None, None, None]
    return jax.nn.silu(normed * gain_part[:, None, None, None, None] + bias_part[:, None, None, None, None])

def double_axis(volume, dim_id):
    inner_len = volume.shape[dim_id] - 2
    middle = lax.slice_in_dim(volume, 1, inner_len + 1, axis=dim_id)
    lower_half = 0.25 * lax.slice_in_dim(volume, 0, inner_len, axis=dim_id) + 0.75 * middle
    upper_half = 0.75 * middle + 0.25 * lax.slice_in_dim(volume, 2, inner_len + 2, axis=dim_id)
    stacked = jnp.stack([lower_half, upper_half], axis=dim_id + 1)
    return stacked.reshape(volume.shape[:dim_id] + (2 * inner_len,) + volume.shape[dim_id + 1:])

def upsample_padded(padded):
    for dim_id in (2, 3, 4):
        padded = double_axis(padded, dim_id)
    return padded

def pool_mean(volume):
    channels, crop_count, span_z, span_y, span_x = volume.shape
    grouped = volume.reshape(channels, crop_count, span_z // 2, 2, span_y // 2, 2, span_x // 2, 2)
    return lax.optimization_barrier(jnp.mean(grouped, axis=(3, 5, 7)))

def cross_entropy(logits, onehot):
    row_max = lax.optimization_barrier(jnp.max(logits, axis=0))
    log_total = row_max + jnp.log(lax.optimization_barrier(jnp.sum(jnp.exp(logits - row_max[None]), axis=0)))
    return log_total - lax.optimization_barrier(jnp.sum(logits * onehot, axis=0))

def forward_loss(flat, images, labels, class_weight):
    pieces = unpack(flat)
    bounds = norm_bounds()
    onehot = (labels[None] == jnp.arange(CLS)[:, None, None, None, None]).astype(jnp.float32)

    def norm_layer(volume, entry_name, layer_id):
        start_at, span_width = bounds[layer_id]
        conv_out = low_back(conv_whole(low(volume), low(pieces[entry_name])))
        return norm_act(conv_out, pieces['gains'][start_at:start_at + span_width], pieces['shifts'][start_at:start_at + span_width])
    first_act = norm_layer(images[None], 'conv_first', 0)
    second_act = norm_layer(first_act, 'conv_second', 1)
    third_act = norm_layer(second_act, 'conv_third', 2)
    coarse_act = norm_layer(pool_mean(third_act), 'conv_coarse', 3)
    edge_pad = ((0, 0), (0, 0), (1, 1), (1, 1), (1, 1))
    lifted = low(upsample_padded(jnp.pad(low(coarse_act), edge_pad, mode='edge')))
    skip_low = low(third_act)
    pre_gate = low_back(jnp.einsum('gc,cnzyx->gnzyx', low(pieces['gate_skip']), skip_low, precision=PRECISE) + jnp.einsum('gc,cnzyx->gnzyx', low(pieces['gate_coarse']), lifted, precision=PRECISE) + pieces['gate_bias'][:, None, None, None, None])
    inner_gate = jax.nn.silu(pre_gate)
    gate_alpha = jax.nn.sigmoid(jnp.einsum('g,gnzyx->nzyx', pieces['gate_score'], inner_gate, precision=PRECISE) + pieces['score_bias'][0])
    merged = jnp.concatenate([skip_low * gate_alpha[None], lifted], axis=0)
    merge_act = norm_layer(merged, 'conv_merge', 4)
    final_act = norm_layer(merge_act, 'conv_final', 5)
    fine_logits = low_back(jnp.einsum('kc,cnzyx->knzyx', low(pieces['head_fine']), low(final_act), precision=PRECISE) + pieces['bias_fine'][:, None, None, None, None])
    coarse_logits = low_back(jnp.einsum('kc,cnzyx->knzyx', low(pieces['head_coarse']), lifted, precision=PRECISE) + pieces['bias_coarse'][:, None, None, None, None])
    voxel_weight = lax.optimization_barrier(jnp.sum(class_weight[:, None, None, None, None] * onehot, axis=0))
    weighted = jnp.sum(voxel_weight * cross_entropy(fine_logits, onehot)) + 0.5 * jnp.sum(voxel_weight * cross_entropy(coarse_logits, onehot))
    return weighted / jnp.sum(voxel_weight)

def reference(images, labels, weights, first_moment, second_moment):
    onehot = (labels[None] == jnp.arange(CLS)[:, None, None, None, None]).astype(jnp.float32)
    counts = lax.optimization_barrier(jnp.sum(onehot, axis=(1, 2, 3, 4)))
    everything = jnp.sum(counts)
    class_weight = 2.0 * everything / (3.0 * counts + everything)

    def loss_of(flat):
        return forward_loss(flat, images, labels, class_weight)
    loss_value, pullback = jax.vjp(loss_of, weights)
    gradient = pullback(jnp.ones((), loss_value.dtype))[0]
    grad_norm = jnp.sqrt(jnp.sum(gradient * gradient))
    clipped = gradient * jnp.minimum(1.0, CLIP_NORM / (grad_norm + 1e-06))
    moment_one = BETA_ONE * first_moment + (1.0 - BETA_ONE) * clipped
    moment_two = BETA_TWO * second_moment + (1.0 - BETA_TWO) * clipped * clipped
    corrected_one = moment_one / (1.0 - BETA_ONE ** STEP)
    corrected_two = moment_two / (1.0 - BETA_TWO ** STEP)
    updated = weights - LEARN_RATE * (corrected_one / (jnp.sqrt(corrected_two) + ADAM_EPS) + DECAY_RATE * weights)
    return (grad_norm, moment_one, moment_two, updated, updated.astype(jnp.bfloat16))
```

```python
import functools
import math

import jax
import jax.numpy as jnp
from jax import lax
from jax.experimental import pallas as pl
from jax.experimental.pallas import tpu as pltpu
from jax.sharding import PartitionSpec as P

C1 = 32
C2 = 64
C3 = 128
CG = 32
CLS = 3
STEP = 10

EPS_NORM = 1e-05
CLIP_NORM = 0.005
LEARN_RATE = 0.02
BETA_ONE = 0.9
BETA_TWO = 0.999
ADAM_EPS = 1e-08
DECAY_RATE = 0.01

BF = jnp.bfloat16
F32 = jnp.float32
AXES = ("depth", "height")
WIDTHS = (C1, C2, C2, C3, C2, C2)
NORM_AT = (0, 32, 96, 160, 288, 352)
VOXELS = 18432
PAD = 160
ROWS = 6552
ROW_FIRST, ROW_SECOND, ROW_THIRD, ROW_COARSE = 0, 8, 440, 1304
ROW_MERGE, ROW_FINAL, ROW_GATE_SKIP, ROW_GATE_COARSE, ROW_TAIL = 3032, 5624, 6488, 6504, 6536
TAIL_AT = 836448
TAIL_LEN = 1479
T_GATE_BIAS, T_SCORE, T_SCORE_BIAS, T_HEAD_FINE, T_BIAS_FINE = 0, 32, 64, 65, 257
T_HEAD_COARSE, T_BIAS_COARSE, T_GAINS, T_SHIFTS = 260, 644, 647, 1063


class Sizes:
    def __init__(self, mesh_depth, mesh_height, local_z, local_y, width):
        self.D, self.H, self.lz, self.ly = mesh_depth, mesh_height, local_z, local_y
        self.planes = mesh_depth * local_z
        self.PY = mesh_height * local_y
        self.V = self.PY * width
        self.nb = self.V // 128
        self.half = self.nb // 2
        self.nbc = self.nb // 4
        self.Vc = self.V // 4
        self.total = self.planes * self.V
        self.G = 2
        while (self.planes // self.G + 2) * self.V > VOXELS:
            self.G *= 2
        self.Z = self.planes // self.G
        self.Zc = self.Z // 2
        self.ZP = -(-(self.Z + 4) // 16) * 16
        self.DP = self.planes - self.Z + self.ZP + 8
        self.two = self.G == 2
        self.share = 4 if mesh_depth * mesh_height // self.G % 4 == 0 else 1


def dot(left, right):
    return lax.dot_general(left, right, (((1,), (0,)), ((), ())), preferred_element_type=F32)


def dot_nt(left, right):
    return lax.dot_general(left, right, (((1,), (1,)), ((), ())), preferred_element_type=F32)


def ds(start, size, multiple=16):
    return pl.ds(start if isinstance(start, int) else pl.multiple_of(start, multiple), size)


def cols(k):
    return slice(k * 128, (k + 1) * 128)


def lanes(channels):
    return lax.broadcasted_iota(jnp.int32, (channels, 128), 1)


def sigmoid(value):
    return 0.5 * jnp.tanh(0.5 * value) + 0.5


def roll(value, steps):
    return pltpu.roll(value, steps % 128, axis=1)


def split_dot(value, matrix):
    high = value.astype(BF)
    low = (value - high.astype(F32)).astype(BF)
    return dot(high, matrix) + dot(low, matrix)


def norm_coefs(sums, gain, shift, channels, count):
    mean = jnp.sum(sums[:channels], axis=1, keepdims=True) / count
    square = jnp.sum(sums[channels : 2 * channels], axis=1, keepdims=True) / count
    inv = lax.rsqrt(square - mean * mean + EPS_NORM)
    full = (channels, 128)
    mean, inv = jnp.broadcast_to(mean, full), jnp.broadcast_to(inv, full)
    factor = inv * gain
    return mean, inv, factor, shift - mean * factor


def grad_coefs(sums, mean, inv, factor, channels, count):
    total = jnp.sum(sums[:channels], axis=1, keepdims=True) / count
    cross = jnp.sum(sums[channels : 2 * channels], axis=1, keepdims=True) / count
    slope = factor * cross * inv
    return slope, slope * mean - factor * total


def place_windows(p_ref, bases, rows, offset, blocks, seg):
    channels, count = blocks[0].shape[0], len(blocks)
    lane = lanes(channels)
    inner = lane & (seg - 1)
    for c in range(3):
        if c == 0:
            moved = [jnp.where(inner == 0, 0.0, roll(v, 1)) for v in blocks]
        elif c == 1:
            moved = blocks
        else:
            moved = [jnp.where(inner == seg - 1, 0.0, roll(v, 127)) for v in blocks]
        before = jnp.where(lane < seg, 0.0, roll(moved[-1], seg)).astype(BF)
        after = jnp.where(lane >= 128 - seg, 0.0, roll(moved[0], 128 - seg)).astype(BF)
        low = [v.astype(BF) for v in moved]
        extended = [before] + low + [after]
        for b in range(3):
            for k in range(count):
                for base in bases:
                    p_ref[ds(base + (3 * b + c) * rows + offset, channels), cols(k)] = extended[k + b]


def pack_wide(out, wide, rows):
    half = rows // 2
    out[:rows, :] = wide[:, :128]
    low = jnp.concatenate([wide[:half, 128:], wide[half:, 128:]], axis=1)
    out[rows : rows + half, :] = low


def unpack_wide(full, full_b, at, packed, start, rows):
    half = rows // 2
    full[at : at + rows, :] = packed[start : start + rows, :].astype(F32)
    low = packed[start + rows : start + rows + half, :].astype(F32)
    full_b[at : at + half, :] = low
    full_b[at + half : at + rows, :] = roll(low, 64)


def unrolled(count, times, body):
    while count % times:
        times -= 1

    def step(t, carry):
        for r in range(times):
            body(times * t + r)
        return carry

    if count == times:
        for i in range(count):
            body(i)
    else:
        lax.fori_loop(0, count // times, step, 0)


def fold_sums(values):
    total = values[0]
    for value in values[1:]:
        total = total + value
    return total


CHUNK = 4


class Far:
    def __init__(self, array, base=None):
        self.array, self.base = array, base


class Held:
    def __init__(self, array):
        self.array = array


class Copied:
    def __init__(self, source, target, sems, base):
        self.target, self.copies = target, []
        self.source, self.sems, self.base = source, sems, base

    def copy(self, c):
        if self.base is None:
            return pltpu.make_async_copy(self.source, self.target, self.sems.at[0])
        span = pl.ds(self.base + c * CHUNK, CHUNK)
        return pltpu.make_async_copy(self.source.at[span], self.target.at[span], self.sems.at[c])

    def __getitem__(self, at):
        return self.target[at]

    @property
    def shape(self):
        return self.target.shape


def need(c, *refs):
    for ref in refs:
        if isinstance(ref, Copied):
            ref.copy(c).wait()


def kernel_call(body, meta, ins, outs, scratch=(), far_outs=False, hbm_outs=(), room=12, us=10):
    def size(shape, dtype):
        return math.prod(shape[:-1]) * (-(-shape[-1] // 128) * 128) * jnp.dtype(dtype).itemsize

    scratch = list(scratch)
    own = len(scratch)
    hbm = range(len(outs)) if far_outs else hbm_outs
    held = [isinstance(a, Held) for a in ins]
    far = [a if isinstance(a, (Far, Held)) else None for a in ins]
    arrays = [
        a if f is None else pltpu.with_memory_space_constraint(a.array, pltpu.HBM) for a, f in zip(ins, far)
    ]
    far = [None if h else f for f, h in zip(far, held)]
    chunks = []
    for a in far:
        if a is not None:
            count = 1 if a.base is None else (a.array.shape[0] - 2 * a.base) // CHUNK
            chunks.append(count)
            scratch += [pltpu.VMEM(a.array.shape, a.array.dtype), pltpu.SemaphoreType.DMA((count,))]
    if far_outs:
        scratch += [pltpu.VMEM(*o) for o in outs] + [pltpu.SemaphoreType.DMA((len(outs),))]

    def wrapped(meta_ref, *refs):
        in_refs, out_refs = refs[: len(ins)], refs[len(ins) : len(ins) + len(outs)]
        own_refs, extra = refs[len(ins) + len(outs) :][:own], list(refs[len(ins) + len(outs) + own :])
        given, whole = [], []
        for a, h, ref in zip(far, held, in_refs):
            if h:
                continue
            if a is None:
                given.append(ref)
                continue
            target, sems = extra.pop(0), extra.pop(0)
            copied = Copied(ref, target, sems, a.base)
            if a.base is None:
                copied.copy(0).start()
                whole.append(copied)
                given.append(target)
            else:
                given.append(copied)
        for copied in given:
            if isinstance(copied, Copied):
                for c in range(copied.sems.shape[0]):
                    copied.copy(c).start()
        for copied in whole:
            copied.copy(0).wait()
        if not far_outs:
            body(meta_ref, *given, *out_refs, *own_refs)
            return
        buffers, sems = extra[:-1], extra[-1]
        body(meta_ref, *given, *buffers, *own_refs)
        copies = [
            pltpu.make_async_copy(source, target, sems.at[index])
            for index, (source, target) in enumerate(zip(buffers, out_refs))
        ]
        for copy in copies:
            copy.start()
        for copy in copies:
            copy.wait()

    vmem = sum(size(x.shape, x.dtype) for x in scratch if getattr(x, "memory_space", None) == pltpu.VMEM) + (room << 20)
    return pl.pallas_call(
        wrapped,
        out_shape=[pltpu.HBM(*o) if k in hbm else jax.ShapeDtypeStruct(*o) for k, o in enumerate(outs)],
        in_specs=[pl.BlockSpec(memory_space=pltpu.SMEM)]
        + [pl.BlockSpec(memory_space=pltpu.HBM if a or h else pltpu.VMEM) for a, h in zip(far, held)],
        out_specs=[pl.BlockSpec(memory_space=pltpu.HBM if k in hbm else pltpu.VMEM) for k in range(len(outs))],
        scratch_shapes=scratch,
        compiler_params=pltpu.CompilerParams(vmem_limit_bytes=min(vmem, 63 << 20)),
        cost_estimate=pl.CostEstimate(flops=us * 1000000000, bytes_accessed=1000, transcendentals=0),
    )(meta, *arrays)


def prep_body(z, meta, flat, tail, big, second, third, coarse, merge, final, b_second, b_third,
              b_coarse, b_merge, b_final, gate, gate_t, head, head_t, gains, shifts, stage, stage_b):
    def unroll(row, taps_out, width):
        count = taps_out * width // 128
        if width == 192:
            rows = count // 3
            one, two, three = (flat[pl.ds(row + j, rows, stride=3), :] for j in range(3))
            left = lanes(rows) < 64
            turned = roll(three, 64)
            stage[pl.ds(0, rows, stride=2), :] = one
            stage_b[pl.ds(0, rows, stride=2), :] = two
            stage[pl.ds(1, rows, stride=2), :] = jnp.where(left, roll(two, 64), turned)
            stage_b[pl.ds(1, rows, stride=2), :] = turned
        else:
            pack = 128 // width
            block = flat[row : row + count, :]
            for j in range(pack):
                stage[pl.ds(j, count, stride=pack), :] = roll(block, -j * width) if j else block

    def staged(at, count, width):
        if width <= 128:
            return stage[at : at + count, :width]
        return jnp.concatenate([stage[at : at + count, :], stage_b[at : at + count, : width - 128]], axis=1)

    def forward(out_c, in_c):
        return [
            jnp.concatenate(
                [staged((9 * a + t) * out_c, out_c, in_c) for t in range(9)],
                axis=1,
            )
            for a in range(3)
        ]

    def backward_plane(out_c, in_c, a):
        at = 26 - 9 * a
        return jnp.concatenate(
            [staged((at - t) * out_c, out_c, in_c) for t in range(9)], axis=0
        ).T

    def backward(out_c, in_c):
        return jnp.concatenate(
            [staged((26 - t) * out_c, out_c, in_c) for t in range(27)], axis=0
        ).T

    def double(ref, full, copies, step):
        rows, width = full.shape
        for r in range(copies):
            parts = []
            if r:
                parts.append(jnp.zeros((rows, r * step), F32))
            parts.append(full)
            if r < copies - 1:
                parts.append(jnp.zeros((rows, (copies - 1 - r) * step), F32))
            ref[r * rows : (r + 1) * rows, :] = jnp.concatenate(parts, axis=1).astype(BF)

    block = flat[0:8, :]
    for j in range(4):
        stage[pl.ds(j, 8, stride=4), :] = roll(block, -j * 32) if j else block
    taps = stage[0:32, :32].T.astype(BF)
    tall = jnp.concatenate([taps] * (z.Z + 2), axis=0)
    shape = ((z.Z + 2) * C1, 9 * z.ZP)
    source = lax.broadcasted_iota(jnp.int32, (32, 9 * z.ZP), 0)
    target = lax.broadcasted_iota(jnp.int32, (32, 9 * z.ZP), 1) // z.ZP
    gap = lax.rem(lax.broadcasted_iota(jnp.int32, shape, 1), z.ZP) - (
        lax.broadcasted_iota(jnp.int32, shape, 0) // C1
    )
    total = jnp.zeros(shape, F32)
    for a in range(3):
        spread = dot(tall, jnp.where(source == target + 5 + 9 * a, 1.0, 0.0).astype(BF))
        total = total + jnp.where(gap == a, spread, 0.0)
    big[...] = total.astype(BF)

    for row, ref, b_ref, width in (
        (ROW_SECOND, second, b_second, C1),
        (ROW_THIRD, third, b_third, C2),
        (ROW_FINAL, final, b_final, C2),
    ):
        unroll(row, 27 * C2, width)
        ref[...] = jnp.concatenate(forward(C2, width), axis=0).astype(BF)
        for a in range(3):
            b_ref[a * width : (a + 1) * width, :] = backward_plane(C2, width, a).astype(BF)
    unroll(ROW_COARSE, 27 * C3, C2)
    coarse[...] = jnp.concatenate(forward(C3, C2), axis=1).astype(BF)
    double(b_coarse, backward(C3, C2), 2, 9 * C3)
    unroll(ROW_MERGE, 27 * C2, C2 + C3)
    merge[...] = jnp.concatenate(forward(C2, C2 + C3), axis=0).astype(BF)
    b_merge[...] = backward(C2, C2 + C3).astype(BF)

    unroll(ROW_GATE_SKIP, CG, C2)
    gate_skip = stage[:CG, :C2]
    gate_coarse = flat[ROW_GATE_COARSE : ROW_GATE_COARSE + CG, :]
    lane = lanes(C3)

    def columns(at, channels):
        value = jnp.zeros((channels, 128), F32)
        for k in range(CLS):
            piece = tail[at + k * channels : at + (k + 1) * channels, :]
            value = jnp.where(lane[:channels] == k, piece, value)
        return value

    fine_cols = columns(T_HEAD_FINE, C2)
    coarse_cols = columns(T_HEAD_COARSE, C3)
    head_t[...] = fine_cols[:, :16].astype(BF)
    head[...] = fine_cols.T[:16, :].astype(BF)
    rows = jnp.concatenate(
        [
            jnp.concatenate([gate_skip, gate_coarse], axis=1),
            jnp.concatenate([jnp.zeros((16, C2), F32), coarse_cols.T[:16, :]], axis=1),
        ],
        axis=0,
    )
    gate[...] = rows.astype(BF)
    gate_t[...] = rows.T.astype(BF)
    gains[...] = tail[T_GAINS : T_GAINS + 416, :]
    shifts[...] = tail[T_SHIFTS : T_SHIFTS + 416, :]


def prepare(z, meta, flat, tail):
    outs = [
        (((z.Z + 2) * C1, 9 * z.ZP), BF),
        ((192, 9 * C1), BF),
        ((192, 9 * C2), BF),
        ((128, 27 * C2), BF),
        ((192, 9 * 192), BF),
        ((192, 9 * C2), BF),
        ((96, 9 * C2), BF),
        ((192, 9 * C2), BF),
        ((128, 36 * C3), BF),
        ((192, 27 * C2), BF),
        ((192, 9 * C2), BF),
        ((48, 192), BF),
        ((192, 48), BF),
        ((16, C2), BF),
        ((C2, 16), BF),
        ((416, 128), F32),
        ((416, 128), F32),
    ]
    names = (
        "big", "second", "third", "coarse", "merge", "final", "b_second", "b_third", "b_coarse",
        "b_merge", "b_final", "gate", "gate_t", "head", "head_t", "gains", "shifts",
    )
    out = kernel_call(
        lambda *refs: prep_body(z, *refs), meta, [flat, tail], outs,
        [pltpu.VMEM((27 * C3, 128), F32), pltpu.VMEM((27 * C2, 128), F32)], far_outs=True,
    )
    return dict(zip(names, out))


def layer_gain(gains, layer):
    return gains[NORM_AT[layer] : NORM_AT[layer] + WIDTHS[layer], :]


def send_planes(z, meta, h_refs, source, count, planes):
    if z.two:
        start = jnp.where(meta[0] == 0, planes - count, 0)
        for j in range(count):
            h_refs[0][j] = source(start + j).astype(BF)
    else:
        for j in range(count):
            h_refs[0][j] = source(j).astype(BF)
            h_refs[1][j] = source(planes - count + j).astype(BF)


UNROLL = CHUNK


def flow(z, build, consume, fetch=(), leave=None):
    build(0, 0, 0)

    def body(t, carry):
        need(t, *fetch)
        for r in range(UNROLL):
            zp = UNROLL * t + r
            build(zp + 1, (r + 1) % 2, None)
            consume(zp, r % 2)
        if leave:
            leave(t)
        return carry

    lax.fori_loop(0, z.Z // UNROLL, body, 0)
    build(z.Z + 1, 1, 1)
    consume(z.Z, 0)
    consume(z.Z + 1, 1)


def scatter(zp, result, width, parts, nb, finish):
    part_one, part_two = parts
    at = zp - 2 if isinstance(zp, int) else jnp.maximum(zp - 2, 0)
    for k in range(nb):
        finish(at, k, part_one[:, cols(k)] + result[2 * width :, cols(k)])
        part_one[:, cols(k)] = part_two[:, cols(k)] + result[width : 2 * width, cols(k)]
        part_two[:, cols(k)] = result[:width, cols(k)]


def add_sums(zp, st_ref, channels, first, second):
    first, second = fold_sums(first), fold_sums(second)
    if not isinstance(zp, int):
        first, second = jnp.where(zp >= 2, first, 0.0), jnp.where(zp >= 2, second, 0.0)
    st_ref[:channels, :] += first
    st_ref[channels : 2 * channels, :] += second


def convolve(z, weight, p_ref, parts, rows, channels, y_ref, st_ref, build, leave=None):
    st_ref[...] = jnp.zeros(st_ref.shape, F32)
    for part in parts:
        part[...] = jnp.zeros(part.shape, F32)

    def consume(zp, slot):
        result = dot(weight[...], p_ref[slot * rows : (slot + 1) * rows, :])
        values = []

        def finish(at, k, value):
            y_ref[at, :, cols(k)] = value
            values.append(value)

        scatter(zp, result, channels, parts, z.nb, finish)
        add_sums(zp, st_ref, channels, values, [v * v for v in values])

    flow(z, build, consume, leave=leave)


def first_body(z, meta, recv, big, y_ref, st_ref, p_ref, lab_ref, wide, rows):
    wide[...] = recv[...].astype(F32)
    rows[...] = jnp.zeros(rows.shape, F32)
    per = z.lz * z.ly
    for hh in range(z.H):
        for yy in range(z.ly):
            for zz in range(z.lz):
                rows[pl.ds((hh * z.ly + yy) * z.DP + 2 + zz, z.D, stride=z.lz), :] = wide[
                    pl.ds(hh * per + zz * z.ly + yy, z.D, stride=z.H * per), :
                ]
    lane = lanes(z.ZP)
    start = pl.multiple_of(meta[0] * z.Z // 8 * 8, 8)

    def source(y):
        if z.Z % 8 == 0:
            return rows[pl.ds(pl.multiple_of(y * z.DP + start, 8), z.ZP), :]
        block = rows[pl.ds(pl.multiple_of(y * z.DP + start, 8), z.ZP + 8), :]
        return jnp.where(lax.rem(meta[0], 2) == 0, block[: z.ZP], block[4 : z.ZP + 4])

    blocks = []
    hits = [jnp.zeros((1, 128), F32) for unused in range(CLS)]
    for k in range(z.nb):
        one, two = source(k), source(k + z.nb)
        blocks.append(jnp.where(lane < 64, one, roll(two, 64)))
        label = jnp.where(lane < 64, roll(one, 64), two)[2 : 2 + z.Z]
        for i in range(z.Z):
            lab_ref[i, :, cols(k)] = jnp.broadcast_to(label[i : i + 1], (8, 128))
        for c in range(CLS):
            hits[c] = hits[c] + jnp.sum(
                jnp.where(label == float(c), 1.0, 0.0), axis=0, keepdims=True
            )
    place_windows(p_ref, (0,), z.ZP, 0, blocks, 64)
    y_ref[...] = dot(big[...], p_ref[...])
    st_ref[...] = jnp.zeros(st_ref.shape, F32)

    def step(i):
        values = [y_ref[ds(C1 + i * C1, C1), cols(k)] for k in range(z.nb)]
        st_ref[:C1, :] += fold_sums(values)
        st_ref[C1 : 2 * C1, :] += fold_sums([v * v for v in values])

    unrolled(z.Z, 4, step)
    row = lax.broadcasted_iota(jnp.int32, (8, 128), 0)
    counts = jnp.zeros((8, 128), F32)
    for c in range(CLS):
        counts = jnp.where(row == c, hits[c], counts)
    st_ref[2 * C1 : 2 * C1 + 8, :] = counts


def second_body(z, meta, y1, sa, sb, gains, shifts, weight, y_ref, st_ref, *rest):
    h_refs, p_ref, parts = rest[:-3], rest[-3], rest[-2:]
    unused, unused, factor, level = norm_coefs(
        sa[...] + sb[...], layer_gain(gains, 0), layer_gain(shifts, 0), C1, z.total
    )

    def build(zp, slot, edge):
        blocks = []
        for k in range(z.nb):
            value = y1[ds(zp * C1, C1), cols(k)] * factor + level
            value = value * sigmoid(value)
            blocks.append(value if edge is None else jnp.where(meta[1 + edge] > 0, value, 0.0))
        place_windows(p_ref, (slot * 9 * C1,), C1, 0, blocks, 64)

    convolve(z, weight, p_ref, parts, 9 * C1, C2, y_ref, st_ref, build)
    send_planes(z, meta, h_refs, lambda i: y_ref[i], 1, z.Z)


def middle_body(z, layer, send, meta, y_in, lo, hi, sa, sb, gains, shifts, weight, y_ref, st_ref, *rest):
    h_refs, p_ref, parts = rest[:-3], rest[-3], rest[-2:]
    unused, unused, factor, level = norm_coefs(
        sa[...] + sb[...], layer_gain(gains, layer), layer_gain(shifts, layer), C2, z.total
    )

    def build(zp, slot, edge):
        if edge is None:
            get = lambda k: y_in[zp - 1, :, cols(k)]
        else:
            get = lambda k: (lo, hi)[edge][0, :, cols(k)].astype(F32)
        blocks = []
        for k in range(z.nb):
            value = get(k) * factor + level
            value = value * sigmoid(value)
            blocks.append(value if edge is None else jnp.where(meta[1 + edge] > 0, value, 0.0))
        place_windows(p_ref, (slot * 9 * C2,), C2, 0, blocks, 64)

    convolve(z, weight, p_ref, parts, 9 * C2, C2, y_ref, st_ref, build)
    send_planes(z, meta, h_refs, lambda i: y_ref[i], send, z.Z)


def pool_matrix(entries):
    row = lax.broadcasted_iota(jnp.int32, (256, 128), 0)
    col = lax.broadcasted_iota(jnp.int32, (256, 128), 1)
    same = (col // 32) == 2 * (lax.rem(row, 128) // 64) + row // 128
    return jnp.where(same, entries(lax.rem(row, 64), lax.rem(col, 32)), 0.0).astype(BF)


def mean_entries(fine, coarse):
    return jnp.where(fine // 2 == coarse, 0.125, 0.0)


def lift_entries(fine, coarse):
    near = fine // 2
    other = jnp.clip(jnp.where(lax.rem(fine, 2) == 0, near - 1, near + 1), 0, 31)
    return jnp.where(coarse == near, 0.75, 0.0) + jnp.where(coarse == other, 0.25, 0.0)


def coarse_body(z, meta, y3, lo, hi, sa, sb, gains, shifts, weight, skip, pooled, y_ref, st_ref, *rest):
    h_refs, p_ref = rest[:-1], rest[-1]
    unused, unused, factor, level = norm_coefs(
        sa[...] + sb[...], layer_gain(gains, 2), layer_gain(shifts, 2), C2, z.total
    )
    matrix = pool_matrix(mean_entries)

    def plane(jp, gets, valid, skip_at):
        sums = []
        for i in range(z.half):
            parts = []
            for index, get in enumerate(gets):
                for k in (2 * i, 2 * i + 1):
                    value = get(k) * factor + level
                    value = value * sigmoid(value)
                    if valid is not None:
                        value = jnp.where(valid > 0, value, 0.0)
                    if skip_at[index] is not None:
                        skip[skip_at[index], :, cols(k)] = value.astype(BF)
                    parts.append(value)
            sums.append(fold_sums(parts))
        blocks = []
        for kc in range(z.nbc):
            pair = jnp.concatenate([sums[kc], sums[kc + z.nbc]], axis=1)
            blocks.append(split_dot(pair, matrix))
        for kc in range(z.nbc):
            pooled[jp, :, cols(kc)] = blocks[kc].astype(BF)
        place_windows(p_ref, (jp * (9 * C2),), C2, 0, blocks, 32)

    plane(0, [lambda k: lo[0, :, cols(k)].astype(F32), lambda k: lo[1, :, cols(k)].astype(F32)],
          meta[1], (None, 0))
    plane(z.Zc + 1, [lambda k: hi[0, :, cols(k)].astype(F32), lambda k: hi[1, :, cols(k)].astype(F32)],
          meta[2], (z.Z + 1, None))

    def step(j):
        plane(j + 1, [lambda k: y3[2 * j, :, cols(k)], lambda k: y3[2 * j + 1, :, cols(k)]],
              None, (2 * j + 1, 2 * j + 2))

    unrolled(z.Zc, 4, step)
    st_ref[...] = jnp.zeros(st_ref.shape, F32)

    def conv(j):
        result = dot(weight[...], p_ref[ds(j * (9 * C2), 27 * C2), :])
        y_ref[j] = result
        values = [result[:, cols(k)] for k in range(z.nbc)]
        st_ref[:C3, :] += fold_sums(values)
        st_ref[C3 : 2 * C3, :] += fold_sums([v * v for v in values])

    unrolled(z.Zc, 8, conv)
    send_planes(z, meta, h_refs, lambda i: y_ref[i], 1, z.Zc)


def merge_body(z, meta, yc, lo, hi, sa, sb, gains, shifts, tail, skip, gate, weight,
               lifted_out, pre_out, logit_out, y_ref, st_ref, *rest):
    h_refs = rest[:-10]
    p_ref, t_ref, act, mixed, part_one, part_two, lifted, pre_ref, logit_ref, sems = rest[-10:]
    unused, unused, factor, level = norm_coefs(
        sa[...] + sb[...], layer_gain(gains, 3), layer_gain(shifts, 3), C3, z.total // 8
    )
    matrix = pool_matrix(lift_entries).astype(F32).T.astype(BF)
    n = z.half

    def coarse_act(get):
        out = []
        for k in range(z.nbc):
            value = get(k) * factor + level
            out.append((value * sigmoid(value)).astype(BF))
        return out

    for k, value in enumerate(coarse_act(lambda k: lo[0, :, cols(k)].astype(F32))):
        act[0, :, cols(k)] = value
    for k, value in enumerate(coarse_act(lambda k: hi[0, :, cols(k)].astype(F32))):
        act[z.Zc + 1, :, cols(k)] = value

    def own(j, carry):
        for k, value in enumerate(coarse_act(lambda k: yc[j, :, cols(k)])):
            act[j + 1, :, cols(k)] = value
        return carry

    lax.fori_loop(0, z.Zc, own, 0)

    @pl.when(meta[1] == 0)
    def low_edge():
        act[0] = act[1]

    @pl.when(meta[2] == 0)
    def high_edge():
        act[z.Zc + 1] = act[z.Zc]

    def spread(jp, slot):
        rows = [None] * n
        for k in range(z.nbc):
            both = dot(act[jp, :, cols(k)], matrix)
            rows[k], rows[k + z.nbc] = both[:, :128], both[:, 128:]
        lane = lanes(C3)
        first, last = rows[0], rows[n - 1]
        before = jnp.where(lane < 64, first, roll(last, 64))
        after = jnp.where(lane < 64, roll(first, 64), last)
        extended = [before] + rows + [after]
        for i in range(n):
            t_ref[slot, :, cols(2 * i)] = 0.25 * extended[i] + 0.75 * extended[i + 1]
            t_ref[slot, :, cols(2 * i + 1)] = 0.75 * extended[i + 1] + 0.25 * extended[i + 2]

    spread(0, 0)
    bias = tail[T_GATE_BIAS : T_GATE_BIAS + CG, :]
    score = tail[T_SCORE : T_SCORE + CG, :]
    score_bias = tail[T_SCORE_BIAS : T_SCORE_BIAS + 1, :]

    def build(zp, slot, edge):
        turn = zp % 2 if isinstance(zp, int) else 1 - (slot + 1) % 2
        wa, wb = (0.75, 0.25) if turn == 0 else (0.25, 0.75)
        old = (zp // 2) % 2 if isinstance(zp, int) else lax.rem(zp // 2, 2)
        new = 1 - old
        if turn == 0:
            spread(zp // 2 + 1, new)
        valid = None if edge is None else meta[1 + edge]
        base, row = slot * 9 * 192, slot * 192
        mixed[row : row + C2, :] = skip[zp]
        wide = []
        for k in range(z.nb):
            value = (wa * t_ref[old, :, cols(k)] + wb * t_ref[new, :, cols(k)]).astype(BF)
            mixed[row + C2 : row + 192, cols(k)] = value
            lifted[zp, :, cols(k)] = value
            value = value.astype(F32)
            wide.append(value if valid is None else jnp.where(valid > 0, value, 0.0))
        place_windows(p_ref, (base,), 192, C2, wide, 64)
        rows = dot(gate[...], mixed[row : row + 192, :])
        logit_ref[zp] = rows[CG:]
        gated = []
        for k in range(z.nb):
            pre = rows[:CG, cols(k)] + bias
            pre_ref[zp, :, cols(k)] = pre
            inner = pre * sigmoid(pre)
            alpha = sigmoid(jnp.sum(score * inner, axis=0, keepdims=True) + score_bias)
            if valid is not None:
                alpha = jnp.where(valid > 0, alpha, 0.0)
            gated.append(mixed[row : row + C2, cols(k)].astype(F32) * alpha)
        place_windows(p_ref, (base,), 192, 0, gated, 64)

    pairs = ((lifted, lifted_out), (pre_ref, pre_out), (logit_ref, logit_out))

    def leaving(t):
        span = pl.ds(4 * t + 1, 4)
        return [
            pltpu.make_async_copy(a.at[span], b.at[span], sems.at[n, t]) for n, (a, b) in enumerate(pairs)
        ]

    def leave(t):
        for copy in leaving(t):
            copy.start()

    convolve(z, weight, p_ref, (part_one, part_two), 9 * 192, C2, y_ref, st_ref, build, leave)
    send_planes(z, meta, h_refs, lambda i: y_ref[i], 1, z.Z)
    for t in range(z.Z // 4):
        for copy in leaving(t):
            copy.wait()


def heads_body(z, meta, yf, sa, sb, ca, cb, lab, logit_ref, gains, shifts, tail, head, head_t,
               d_ref, bs_ref, small, gc_ref, *rest):
    h_refs, acts = rest[:-1], rest[-1]
    mean, inv, factor, level = norm_coefs(
        sa[...] + sb[...], layer_gain(gains, 5), layer_gain(shifts, 5), C2, z.total
    )
    counts = jnp.sum(ca[2 * C1 :] + cb[2 * C1 :], axis=1, keepdims=True)
    row = lax.broadcasted_iota(jnp.int32, (8, 1), 0)
    everything = jnp.sum(jnp.where(row < CLS, counts, 0.0), axis=0, keepdims=True)
    class_weight = jnp.where(row < CLS, 2.0 * everything / (3.0 * counts + everything), 0.0)
    weight_total = jnp.sum(counts * class_weight, axis=0, keepdims=True)
    scaled = class_weight / weight_total
    scaled = jnp.concatenate([scaled, jnp.zeros((8, 1), F32)], axis=0)
    rows16 = lax.broadcasted_iota(jnp.int32, (16, 128), 0)
    pad13 = jnp.zeros((13, 128), F32)
    bias_fine = jnp.concatenate([tail[T_BIAS_FINE : T_BIAS_FINE + 3, :], pad13], axis=0)
    bias_coarse = jnp.concatenate([tail[T_BIAS_COARSE : T_BIAS_COARSE + 3, :], pad13], axis=0)
    bs_ref[...] = jnp.zeros(bs_ref.shape, F32)
    small[...] = jnp.zeros(small.shape, F32)

    def logit_grad(logits, label, times):
        logits = jnp.where(rows16 < CLS, logits, -1e30)
        top = jnp.max(logits, axis=0, keepdims=True)
        terms = jnp.where(rows16 < CLS, jnp.exp(logits - top), 0.0)
        soft = terms / jnp.sum(terms, axis=0, keepdims=True)
        onehot = jnp.where(rows16.astype(F32) == label, 1.0, 0.0)
        weight = jnp.sum(scaled * onehot, axis=0, keepdims=True)
        return ((soft - onehot) * (weight * times)).astype(BF)

    def step(i, slot):
        act = acts.at[slot * C2 : (slot + 1) * C2, :]
        for k in range(z.nb):
            value = yf[i, :, cols(k)] * factor + level
            act[:, cols(k)] = (value * sigmoid(value)).astype(BF)
        logits = dot(head[...], act[...])
        fine, bias_sum, coarse_sum = [], [], []
        for k in range(z.nb):
            label = lab[i, 0:1, cols(k)]
            grad = logit_grad(logits[:, cols(k)] + bias_fine, label, 1.0)
            fine.append(grad)
            bias_sum.append(grad.astype(F32))
            grad = logit_grad(logit_ref[i + 1, :, cols(k)] + bias_coarse, label, 0.5)
            gc_ref[i, :, cols(k)] = grad
            coarse_sum.append(grad.astype(F32))
        fine = jnp.concatenate(fine, axis=1)
        small[:C2, :16] += dot_nt(act[...], fine)
        small[C2 : C2 + 16, :] += fold_sums(bias_sum)
        small[C2 + 16 : C2 + 32, :] += fold_sums(coarse_sum)
        back = dot(head_t[...], fine)
        parts, cross = [], []
        for k in range(z.nb):
            y = yf[i, :, cols(k)]
            pre = y * factor + level
            sig = sigmoid(pre)
            grad = back[:, cols(k)] * (sig * (1.0 + pre * (1.0 - sig)))
            d_ref[i, :, cols(k)] = grad
            parts.append(grad)
            cross.append(grad * ((y - mean) * inv))
        bs_ref[:C2, :] += fold_sums(parts)
        bs_ref[C2:, :] += fold_sums(cross)

    def four(t, carry):
        for r in range(4):
            step(4 * t + r, r)
        return carry

    lax.fori_loop(0, z.Z // 4, four, 0)
    send_planes(z, meta, h_refs, lambda i: d_ref[i], 1, z.Z)


def dy_builder(z, meta, layer, count, refs, p_ref):
    d, d_lo, d_hi, y, y_lo, y_hi, sums, back, gains, shifts = refs
    channels = WIDTHS[layer]
    mean, inv, factor, unused = norm_coefs(
        sums, layer_gain(gains, layer), layer_gain(shifts, layer), channels, count
    )
    slope, level = grad_coefs(back, mean, inv, factor, channels, count)

    def build(zp, bases, edge):
        get_d, get_y = (lambda k: d[zp - 1, :, cols(k)]), (lambda k: y[zp - 1, :, cols(k)])
        if edge is not None:
            get_d = lambda k: (d_lo, d_hi)[edge][0, :, cols(k)].astype(F32)
            get_y = lambda k: (y_lo[y_lo.shape[0] - 1, :, cols(k)], y_hi[0, :, cols(k)])[edge].astype(F32)
        out = []
        for k in range(z.nb):
            value = factor * get_d(k) - slope * get_y(k) + level
            out.append(value if edge is None else jnp.where(meta[1 + edge] > 0, value, 0.0))
        place_windows(p_ref, bases, channels, 0, out, 64)

    def build_or_edge(zp, bases, last):
        out = []
        own = jnp.minimum(zp - 1, z.Z - 1)
        for k in range(z.nb):
            near_d = jnp.where(last, d_hi[0, :, cols(k)].astype(F32), d[own, :, cols(k)])
            near_y = jnp.where(last, y_hi[0, :, cols(k)].astype(F32), y[own, :, cols(k)])
            value = factor * near_d - slope * near_y + level
            out.append(jnp.where(jnp.logical_and(last, meta[2] == 0), 0.0, value))
        place_windows(p_ref, bases, channels, 0, out, 64)

    build.or_edge = build_or_edge
    return build


def back_body(z, layer, below, y_base, share, meta, d, d_lo, d_hi, y, y_lo, y_hi, sa, sb, ba, bb,
              yb, ua, ub, gains, shifts, weight, *rest):
    d_ref, bs_ref, dk_out = rest[:3]
    h_refs, (p_ref, x_ref, dk_ref), parts = rest[3:-5], rest[-5:-2], rest[-2:]
    make = dy_builder(z, meta, layer, z.total,
                       (d, d_lo, d_hi, y, y_lo, y_hi, sa[...] + sb[...], ba[...] + bb[...], gains, shifts), p_ref)
    width = WIDTHS[below]
    mean, inv, factor, level = norm_coefs(
        ua[...] + ub[...], layer_gain(gains, below), layer_gain(shifts, below), width, z.total
    )
    edge = jnp.zeros((2 * width, z.V), BF)
    x_ref[: 2 * width, :] = edge
    x_ref[(z.Z + 2) * width :, :] = edge
    bs_ref[...] = jnp.zeros(bs_ref.shape, F32)
    rows = 9 * WIDTHS[layer]
    part = rows // share
    dk_ref[...] = jnp.zeros(dk_ref.shape, F32)

    for part_ref in parts:
        part_ref[...] = jnp.zeros(part_ref.shape, F32)

    def build(zp, slot, edge):
        make(zp, (slot * rows,), edge)

    def consume(zp, slot):
        result = dot(weight[...], p_ref[slot * rows : (slot + 1) * rows, :])
        if not isinstance(zp, int):
            for k in range(z.nb):
                pre = yb[zp + y_base, :, cols(k)] * factor + level
                x_ref[ds((zp + 2) * width, width), cols(k)] = (pre * sigmoid(pre)).astype(BF)
        sums, cross = [], []

        def finish(at, k, value):
            y_value = yb[at + y_base, :, cols(k)]
            pre = y_value * factor + level
            sig = sigmoid(pre)
            grad = value * (sig * (1.0 + pre * (1.0 - sig)))
            d_ref[at, :, cols(k)] = grad
            sums.append(grad)
            cross.append(grad * ((y_value - mean) * inv))

        scatter(zp, result, width, parts, z.nb, finish)
        add_sums(zp, bs_ref, width, sums, cross)
        if share == 1:
            window = p_ref[slot * rows : (slot + 1) * rows, :]
        else:
            window = p_ref[ds(slot * rows + meta[3] * part, part), :]
        dk_ref[...] += dot_nt(window, x_ref[ds(zp * width, 3 * width), :])

    flow(z, build, consume, (d, y, yb))
    if width == C2:
        pack_wide(dk_out, dk_ref, part)
    else:
        dk_out[:, : 3 * width] = dk_ref[...]
    if h_refs:
        send_planes(z, meta, h_refs, lambda i: d_ref[i], 1, z.Z)


def merge_back_body(z, share, meta, d, d_lo, d_hi, y, y_lo, y_hi, sa, sb, ba, bb, skip, lifted, pre_ref, gc_ref,
                    yc, yc_lo, yc_hi, ua, ub, gains, shifts, tail, weight, gate_t,
                    gskip_out, gcoarse, bs_ref, dk_out, small, *rest):
    h_refs, (p_ref, mixed, eg, x_ref, acc, dk_ref, gskip, sems) = rest[:-8], rest[-8:]
    build = dy_builder(z, meta, 4, z.total,
                       (d, d_lo, d_hi, y, y_lo, y_hi, sa[...] + sb[...], ba[...] + bb[...], gains, shifts), p_ref)
    score = tail[T_SCORE : T_SCORE + CG, :]
    score_bias = tail[T_SCORE_BIAS : T_SCORE_BIAS + 1, :]
    small[...] = jnp.zeros(small.shape, F32)
    dk_ref[...] = jnp.zeros(dk_ref.shape, F32)
    acc[...] = jnp.zeros(acc.shape, F32)
    n = z.half
    lane = lanes(C3)
    rows = 9 * C2
    part = 27 * C2 // share

    def plane(i, r4):
        start = r4 * rows
        turn = (r4 % 2) * 192
        result = dot(weight[...], p_ref[start : start + 3 * rows, :])
        mixed[turn : turn + C2, :] = skip[i + 1]
        mixed[turn + C2 : turn + 192, :] = lifted[i + 1]
        x_ref[turn + C2 : turn + 192, :] = lifted[i + 1]
        side = (r4 % 2) * 48
        alphas, e_sum, s_sum, r_sum = [], [], [], []
        for k in range(z.nb):
            pre = pre_ref[i + 1, :, cols(k)]
            sig = sigmoid(pre)
            inner = pre * sig
            alpha = sigmoid(jnp.sum(score * inner, axis=0, keepdims=True) + score_bias)
            wide = skip[i + 1, :, cols(k)].astype(F32)
            grad = jnp.sum(result[:C2, cols(k)] * wide, axis=0, keepdims=True)
            grad = grad * alpha * (1.0 - alpha)
            e = (score * grad * (sig * (1.0 + pre * (1.0 - sig)))).astype(BF)
            eg[side : side + CG, cols(k)] = e
            x_ref[turn : turn + C2, cols(k)] = (wide * alpha).astype(BF)
            alphas.append(alpha)
            e_sum.append(e.astype(F32))
            s_sum.append(grad * inner)
            r_sum.append(grad)
        eg[side + CG : side + 48, :] = gc_ref[i]
        small[:192, :48] += dot_nt(mixed[turn : turn + 192, :], eg[side : side + 48, :])
        small[192:224, :] += fold_sums(e_sum)
        small[224:256, :] += fold_sums(s_sum)
        small[256:257, :] += fold_sums(r_sum)
        extra = dot(gate_t[...], eg[side : side + 48, :])
        for k in range(z.nb):
            gskip[i, :, cols(k)] = result[:C2, cols(k)] * alphas[k] + extra[:C2, cols(k)]
        wide = [result[C2:, cols(k)] + extra[C2:, cols(k)] for k in range(z.nb)]
        low = [
            0.75 * (wide[2 * m] + wide[2 * m + 1])
            + (0.25 * wide[2 * m + 2] if m < n - 1 else 0.0)
            + (0.25 * wide[2 * m - 1] if m > 0 else 0.0)
            for m in range(n)
        ]
        before, after = 0.25 * wide[0], 0.25 * wide[-1]
        low[0] = low[0] + jnp.where(lane < 64, before, roll(after, 64))
        low[n - 1] = low[n - 1] + jnp.where(lane < 64, roll(before, 64), after)
        j, r = i // 2, r4 % 2
        for m in range(n):
            acc[j + 1, :, cols(m)] += 0.75 * low[m]
            acc[j + 2 * r, :, cols(m)] += 0.25 * low[m]
        if share == 1:
            window = p_ref[start : start + 3 * rows, :]
        else:
            window = p_ref[ds(start + meta[3] * part, part), :]
        dk_ref[...] += dot_nt(window, x_ref[turn : turn + 192, :])

    need(0, d, y)
    for zp in range(3):
        build(zp, (zp * rows,), 0 if zp == 0 else None)

    def four(t, carry):
        need(t, skip, lifted, pre_ref, gc_ref)
        for r in range(4):
            if r == 2:

                @pl.when(t + 1 < z.Z // 4)
                def fetch():
                    need(t + 1, d, y)

            at = (r + 3) % 4
            bases = (at * rows, (at + 4) * rows) if at < 2 else (at * rows,)
            zp = 4 * t + r + 3
            if r < 2:
                build(zp, bases, None)
            else:
                build.or_edge(zp, bases, zp == z.Z + 1)
            plane(4 * t + r, r)
        leaving(t).start()
        return carry

    def leaving(t):
        span = pl.ds(4 * t, 4)
        return pltpu.make_async_copy(gskip.at[span], gskip_out.at[span], sems.at[t])

    lax.fori_loop(0, z.Z // 4, four, 0)
    pack_wide(dk_out, dk_ref, part)

    matrix = pool_matrix(lift_entries)

    def shrink(jp, carry):
        for k in range(z.nbc):
            pair = jnp.concatenate([acc[jp, :, cols(k)], acc[jp, :, cols(k + z.nbc)]], axis=1)
            gcoarse[jp, :, cols(k)] = split_dot(pair, matrix)
        return carry

    lax.fori_loop(0, z.Zc + 2, shrink, 0)

    @pl.when(meta[1] == 0)
    def low_edge():
        gcoarse[1] += gcoarse[0]
        gcoarse[0] = jnp.zeros((C3, z.Vc), F32)

    @pl.when(meta[2] == 0)
    def high_edge():
        gcoarse[z.Zc] += gcoarse[z.Zc + 1]
        gcoarse[z.Zc + 1] = jnp.zeros((C3, z.Vc), F32)

    mean, inv, factor, level = norm_coefs(
        ua[...] + ub[...], layer_gain(gains, 3), layer_gain(shifts, 3), C3, z.total // 8
    )
    bs_ref[...] = jnp.zeros(bs_ref.shape, F32)

    def sums(jp, get):
        for k in range(z.nbc):
            value = get(k)
            pre = value * factor + level
            sig = sigmoid(pre)
            grad = gcoarse[jp, :, cols(k)] * (sig * (1.0 + pre * (1.0 - sig)))
            bs_ref[:C3, :] += grad
            bs_ref[C3:, :] += grad * ((value - mean) * inv)

    sums(0, lambda k: yc_lo[0, :, cols(k)].astype(F32))
    sums(z.Zc + 1, lambda k: yc_hi[0, :, cols(k)].astype(F32))

    def own(j, carry):
        sums(j + 1, lambda k: yc[j, :, cols(k)])
        return carry

    lax.fori_loop(0, z.Zc, own, 0)
    if z.two:
        start = jnp.where(meta[0] == 0, z.Zc, 0)
        for m in range(2):
            h_refs[0][m] = gcoarse[start + m].astype(BF)
    else:
        for m in range(2):
            h_refs[0][m] = gcoarse[m].astype(BF)
            h_refs[1][m] = gcoarse[z.Zc + m].astype(BF)
    for t in range(z.Z // 4):
        leaving(t).wait()


def coarse_back_body(z, share, meta, gcoarse, g_lo, g_hi, yc, yc_lo, yc_hi, sa, sb, ba, bb, pooled, gskip, y3,
                     ua, ub, gains, shifts, weight, d_ref, bs_ref, dk_out, *rest):
    h_refs, (p_ref, x_ref, dk_ref) = rest[:-3], rest[-3:]
    mean, inv, factor, level = norm_coefs(
        sa[...] + sb[...], layer_gain(gains, 3), layer_gain(shifts, 3), C3, z.total // 8
    )
    slope, offset = grad_coefs(ba[...] + bb[...], mean, inv, factor, C3, z.total // 8)

    def plane(jp, get_y, extra, valid):
        out = []
        for k in range(z.nbc):
            value = get_y(k)
            pre = value * factor + level
            sig = sigmoid(pre)
            grad = gcoarse[jp, :, cols(k)] + extra(k)
            grad = grad * (sig * (1.0 + pre * (1.0 - sig)))
            grad = factor * grad - slope * value + offset
            out.append(grad if valid is None else jnp.where(valid > 0, grad, 0.0))
        place_windows(p_ref, (jp * (9 * C3),), C3, 0, out, 32)

    def from_lo(m):
        return lambda k: jnp.where(meta[1] > 0, g_lo[m, :, cols(k)].astype(F32), 0.0)

    def from_hi(m):
        return lambda k: jnp.where(meta[2] > 0, g_hi[m, :, cols(k)].astype(F32), 0.0)

    plane(0, lambda k: yc_lo[0, :, cols(k)].astype(F32), from_lo(0), meta[1])
    plane(1, lambda k: yc[0, :, cols(k)], from_lo(1), None)

    def inner(j):
        plane(j + 2, lambda k: yc[j + 1, :, cols(k)], lambda k: 0.0, None)

    if z.Zc > 2:
        unrolled(z.Zc - 2, 3, inner)
    plane(z.Zc, lambda k: yc[z.Zc - 1, :, cols(k)], from_hi(0), None)
    plane(z.Zc + 1, lambda k: yc_hi[0, :, cols(k)].astype(F32), from_hi(1), meta[2])

    edge = jnp.zeros((2 * C2, z.Vc), BF)
    x_ref[: 2 * C2, :] = edge
    x_ref[(z.Zc + 2) * C2 :, :] = edge

    for j in range(z.Zc):
        x_ref[(j + 2) * C2 : (j + 3) * C2, :] = pooled[j + 1]
    mean, inv, factor, level = norm_coefs(
        ua[...] + ub[...], layer_gain(gains, 2), layer_gain(shifts, 2), C2, z.total
    )
    matrix = pool_matrix(mean_entries).astype(F32).T.astype(BF)
    bs_ref[...] = jnp.zeros(bs_ref.shape, F32)
    rows = 9 * C3

    def step(s, carry):
        need(s, y3, gskip)
        result = dot(weight[...], p_ref[ds(s * (2 * rows), 4 * rows), :])
        parts, cross = [], []
        for r in range(2):
            low = result[r * C2 : (r + 1) * C2]
            spread = [None] * z.half
            for k in range(z.nbc):
                both = split_dot(low[:, cols(k)], matrix)
                spread[k], spread[k + z.nbc] = both[:, :128], both[:, 128:]
            for q in range(2):
                at = 4 * s + 2 * r + q
                for k in range(z.nb):
                    value = y3[at, :, cols(k)]
                    pre = value * factor + level
                    sig = sigmoid(pre)
                    grad = spread[k // 2] + gskip[at, :, cols(k)]
                    grad = grad * (sig * (1.0 + pre * (1.0 - sig)))
                    d_ref[at, :, cols(k)] = grad
                    parts.append(grad)
                    cross.append(grad * ((value - mean) * inv))
        bs_ref[:C2, :] += fold_sums(parts)
        bs_ref[C2:, :] += fold_sums(cross)
        return carry

    lax.fori_loop(0, z.Zc // 2, step, 0)
    part = rows // share

    def kernel_grad(zp):
        window = p_ref[ds(zp * rows + meta[3] * part, part), :]
        return dot_nt(window, x_ref[zp * C2 : (zp + 3) * C2, :])

    dk_ref[...] = fold_sums([kernel_grad(zp) for zp in range(z.Zc + 2)])
    pack_wide(dk_out, dk_ref, part)
    send_planes(z, meta, h_refs, lambda i: d_ref[i], 1, z.Z)


def first_back_body(z, meta, d, y1, p_img, sa, sb, ba, bb, gains, shifts, dk_ref, low):
    mean, inv, factor, unused = norm_coefs(
        sa[...] + sb[...], layer_gain(gains, 0), layer_gain(shifts, 0), C1, z.total
    )
    slope, level = grad_coefs(ba[...] + bb[...], mean, inv, factor, C1, z.total)

    def step(i):
        for k in range(z.nb):
            value = factor * d[i, :, cols(k)] - slope * y1[i + 1, :, cols(k)] + level
            low[ds(i * C1, C1), cols(k)] = value.astype(BF)

    unrolled(z.Z, 4, step)
    table = dot_nt(p_img[...], low[...])
    shape = (9 * z.ZP, z.Z * C1)
    gap = lax.rem(lax.broadcasted_iota(jnp.int32, shape, 0), z.ZP) - (
        lax.broadcasted_iota(jnp.int32, shape, 1) // C1
    )
    dk_ref[...] = jnp.zeros(dk_ref.shape, F32)
    for a in range(3):
        kept = jnp.where(gap == a + 1, table, 0.0)
        folded = fold_sums([kept[:, cols(k)] for k in range(z.Z * C1 // 128)])
        folded = folded + roll(folded, 64)
        folded = folded + roll(folded, 32)
        for t in range(9):
            dk_ref[9 * a + t : 9 * a + t + 1, :] = jnp.sum(
                folded[t * z.ZP : (t + 1) * z.ZP], axis=0, keepdims=True
            )


def gather_body(z, meta, *refs):
    ins, (out, norm), (stage, stage_b, flat, column, quarters, full, full_b) = refs[:-9], refs[-9:-7], refs[-7:]
    shared, ins = ins[: z.share], ins[z.share :]
    pairs = [(ins[2 * j], ins[2 * j + 1]) for j in range(len(ins) // 2)]
    (first, second, small_head, small_gate, b_first, b_second, b_third, b_coarse, b_merge, b_final) = pairs
    for k in range(z.share):
        quarters[jnp.bitwise_xor(meta[3], k)] = shared[k][...].astype(F32)

    def unpack(start, count):
        part = count // z.share
        for k in range(z.share):
            unpack_wide(full, full_b, k * part, quarters.at[k], start, part)

    def total(pair):
        return pair[0][...] + pair[1][...]

    def pack(row, taps_out, width):
        count = taps_out * width // 128
        fold = 128 // width
        lane = lanes(count)
        value = stage[pl.ds(0, count, stride=fold), :]
        for j in range(1, fold):
            part = roll(stage[pl.ds(j, count, stride=fold), :], j * width)
            value = jnp.where(lane < j * width, value, part)
        flat[row : row + count, :] = value

    flat[ROWS : ROWS + 8, :] = jnp.zeros((8, 128), F32)
    stage[0:5, :32] = jnp.zeros((5, 32), F32)
    stage[5:32, :32] = (first[0][...] + first[1][...])[:27, :32]
    pack(ROW_FIRST, 32, 32)
    wide_at = 27 * C2 // z.share * 3 // 2
    for row, out_c, in_c, source in (
        (ROW_SECOND, C2, C1, second),
        (ROW_THIRD, C2, C2, 2 * wide_at),
        (ROW_COARSE, C3, C2, wide_at + wide_at // 3),
        (ROW_FINAL, C2, C2, wide_at),
    ):
        count = 9 * out_c
        if source is second:
            full[:count, :] = total(second)
        else:
            unpack(source, count)
        for t in range(9):
            span = slice(t * out_c, (t + 1) * out_c)
            for a in range(3):
                at = (9 * a + 8 - t) * out_c
                if a * in_c < 128:
                    stage[at : at + out_c, :in_c] = full[span, a * in_c : (a + 1) * in_c]
                else:
                    stage[at : at + out_c, :in_c] = full_b[span, :in_c]
        pack(row, 27 * out_c, in_c)
    unpack(0, 27 * C2)
    for t in range(27):
        at = (26 - t) * C2
        stage[at : at + C2, :] = full[t * C2 : (t + 1) * C2, :]
        stage_b[at : at + C2, :64] = full_b[t * C2 : (t + 1) * C2, :64]
    half = 27 * C2 // 2
    even, even_b = stage[pl.ds(0, half, stride=2), :], stage_b[pl.ds(0, half, stride=2), :]
    odd, odd_b = stage[pl.ds(1, half, stride=2), :], stage_b[pl.ds(1, half, stride=2), :]
    left = lanes(half) < 64
    odd = roll(odd, 64)
    flat[pl.ds(ROW_MERGE, half, stride=3), :] = even
    flat[pl.ds(ROW_MERGE + 1, half, stride=3), :] = jnp.where(left, even_b, odd)
    flat[pl.ds(ROW_MERGE + 2, half, stride=3), :] = jnp.where(left, odd, roll(odd_b, 64))

    gate = total(small_gate)
    turned = gate[:192].T
    stage[:CG, :C2] = turned[:CG, :C2]
    pack(ROW_GATE_SKIP, CG, C2)
    flat[ROW_GATE_COARSE : ROW_GATE_COARSE + CG, :] = turned[:CG, C2:]
    heads = total(small_head)
    lane = lanes(C3)
    column[TAIL_LEN - 7 :, :] = jnp.zeros((2048 - TAIL_LEN + 7, 128), F32)
    column[T_GATE_BIAS : T_GATE_BIAS + CG, :] = gate[192:224]
    column[T_SCORE : T_SCORE + CG, :] = gate[224:256]
    column[T_SCORE_BIAS : T_SCORE_BIAS + 1, :] = gate[256:257]
    for k in range(CLS):
        at = T_HEAD_FINE + k * C2
        column[at : at + C2, :] = jnp.where(lane[:C2] == k, heads[:C2], 0.0)
        at = T_HEAD_COARSE + k * C3
        column[at : at + C3, :] = jnp.where(lane == CG + k, gate[C2:192], 0.0)
    column[T_BIAS_FINE : T_BIAS_FINE + 3, :] = heads[C2 : C2 + 3]
    column[T_BIAS_COARSE : T_BIAS_COARSE + 3, :] = heads[C2 + 16 : C2 + 19]
    for layer, pair in enumerate((b_first, b_second, b_third, b_coarse, b_merge, b_final)):
        sums = total(pair)
        width = WIDTHS[layer]
        at = T_GAINS + NORM_AT[layer]
        column[at : at + width, :] = sums[width : 2 * width]
        at = T_SHIFTS + NORM_AT[layer]
        column[at : at + width, :] = sums[:width]
    for k in range(16):
        flat[ROW_TAIL + k : ROW_TAIL + k + 1, :] = jnp.sum(
            column[k * 128 : (k + 1) * 128, :].T, axis=0, keepdims=True
        )
    chunk = ROWS // 21
    mask = lanes(chunk) < 96

    def finish(i, acc):
        base = pl.multiple_of(i * chunk, 8)
        block = roll(flat[pl.ds(base, chunk + 8), :], 96)
        out[pl.ds(base, chunk), :] = jnp.where(mask, block[1 : chunk + 1], block[2 : chunk + 2])
        return acc + fold_sums([block[8 * m : 8 * m + 8] * block[8 * m : 8 * m + 8] for m in range(chunk // 8)])

    acc = lax.fori_loop(0, 21, finish, jnp.zeros((8, 128), F32))
    sq = jnp.sum(jnp.sum(acc, axis=1, keepdims=True), axis=0, keepdims=True)
    norm[...] = jnp.broadcast_to(jnp.sqrt(sq), (8, 128))


def local(z, images, labels, weights, first_moment, second_moment):
    devices = z.D * z.H
    linear = lax.axis_index("depth") * z.H + lax.axis_index("height")
    position = lax.rem(linear, z.G)
    meta = jnp.stack(
        [position, (position > 0).astype(jnp.int32), (position < z.G - 1).astype(jnp.int32),
         lax.rem(linear // z.G, z.share)]
    ).astype(jnp.int32)

    call = functools.partial(kernel_call, room=12 if z.V <= 1024 else 18)

    def partner(value, step):
        return lax.ppermute(value, AXES, [(i, i ^ step) for i in range(devices)])

    def both(value):
        step = 1
        while step * 2 < z.G:
            value = value + partner(value, step)
            step *= 2
        return value, partner(value, step)

    def neighbours(sent):
        if z.two:
            got = partner(sent[0], 1)
            return got, got
        up = [(i, i + 1) for i in range(devices) if i % z.G != z.G - 1]
        return (
            lax.ppermute(sent[1], AXES, up),
            lax.ppermute(sent[0], AXES, [(j, i) for i, j in up]),
        )

    def shares(values):
        value = jnp.concatenate([one + two for one, two in values], axis=0).astype(BF)
        return [value] + [
            lax.ppermute(value, AXES, [(i, (i // z.G ^ k) * z.G + i % z.G) for i in range(devices)])
            for k in range(1, z.share)
        ]

    def sent(count, channels, lanes_):
        return [((count, channels, lanes_), BF)] * (1 if z.two else 2)

    V, Vc, Z, Zc = z.V, z.Vc, z.Z, z.Zc
    local_rows = z.lz * z.ly
    mine = jnp.concatenate(
        [images.reshape(local_rows, 64).astype(BF), labels.reshape(local_rows, 64).astype(BF)], axis=1
    )
    everyone = lax.all_to_all(
        jnp.broadcast_to(mine[None], (devices, local_rows, 128)), AXES, 0, 0
    ).reshape(devices * local_rows, 128)
    flat = jnp.pad(weights, (PAD, ROWS * 128 - PAD - weights.shape[0])).reshape(ROWS, 128)
    tail = jnp.broadcast_to(
        jnp.pad(weights[TAIL_AT:], (0, 1))[:, None], (TAIL_LEN + 1, 128)
    )
    w = prepare(z, meta, flat, tail)
    gains, shifts = w["gains"], w["shifts"]

    def fars(values, base=None):
        return [Far(value, base) for value in values]

    y1, st1, p_img, lab = call(
        lambda *r: first_body(z, *r), meta, [Far(everyone), Far(w["big"])],
        [(((Z + 2) * C1, V), F32), ((72, 128), F32), ((9 * z.ZP, V), BF), ((Z, 8, V), F32)],
        [pltpu.VMEM((devices * local_rows, 128), F32), pltpu.VMEM((z.PY * z.DP, 128), F32)],
    )
    st1 = both(st1)
    parts = [pltpu.VMEM((C2, V), F32), pltpu.VMEM((C2, V), F32)]
    y2, st2, *h2 = call(
        lambda *r: second_body(z, *r), meta, [y1, *st1, gains, shifts, w["second"]],
        [((Z, C2, V), F32), ((2 * C2, 128), F32)] + sent(1, C2, V),
        [pltpu.VMEM((2 * 9 * C1, V), BF), *parts],
    )
    st2, h2 = both(st2), neighbours(h2)
    wide_p = pltpu.VMEM((2 * 9 * C2, V), BF)
    y3, st3, *h3 = call(
        lambda *r: middle_body(z, 1, 2, *r), meta, [y2, *h2, *st2, gains, shifts, w["third"]],
        [((Z, C2, V), F32), ((2 * C2, 128), F32)] + sent(2, C2, V), [wide_p, *parts],
    )
    st3, h3 = both(st3), neighbours(h3)
    skip, pooled, yc, stc, *hc = call(
        lambda *r: coarse_body(z, *r), meta, [y3, *h3, *st3, gains, shifts, w["coarse"]],
        [((Z + 2, C2, V), BF), ((Zc + 2, C2, Vc), BF), ((Zc, C3, Vc), F32), ((2 * C3, 128), F32)]
        + sent(1, C3, Vc),
        [pltpu.VMEM(((Zc + 2) * 9 * C2, Vc), BF)],
    )
    stc, hc = both(stc), neighbours(hc)
    lifted, pre, logits, ym, stm, *hm = call(
        lambda *r: merge_body(z, *r), meta,
        [yc, *hc, *stc, gains, shifts, tail, skip, w["gate"], w["merge"]],
        [((Z + 2, C3, V), BF), ((Z + 2, CG, V), F32), ((Z + 2, 16, V), F32), ((Z, C2, V), F32),
         ((2 * C2, 128), F32)] + sent(1, C2, V),
        [pltpu.VMEM((2 * 9 * 192, V), BF), pltpu.VMEM((2, C3, V), F32), pltpu.VMEM((Zc + 2, C3, Vc), BF),
         pltpu.VMEM((384, V), BF), *parts, pltpu.VMEM((Z + 2, C3, V), BF), pltpu.VMEM((Z + 2, CG, V), F32),
         pltpu.VMEM((Z + 2, 16, V), F32), pltpu.SemaphoreType.DMA((3, Z // 4))],
        hbm_outs=(0, 1, 2),
    )
    stm, hm = both(stm), neighbours(hm)
    yf, stf, *hf = call(
        lambda *r: middle_body(z, 4, 1, *r), meta, [ym, *hm, *stm, gains, shifts, w["final"]],
        [((Z, C2, V), F32), ((2 * C2, 128), F32)] + sent(1, C2, V), [wide_p, *parts],
    )
    stf, hf = both(stf), neighbours(hf)
    counts = fars(st1)
    df, bf, small_head, gc, *hdf = call(
        lambda *r: heads_body(z, *r), meta,
        [yf, *stf, *counts, Far(lab), Far(logits), gains, shifts, tail, w["head"], w["head_t"]],
        [((Z, C2, V), F32), ((2 * C2, 128), F32), ((C2 + 32, 128), F32), ((Z, 16, V), BF)] + sent(1, C2, V),
        [pltpu.VMEM((4 * C2, V), BF)],
    )
    bf, hdf, small_head = both(bf), neighbours(hdf), both(small_head)
    x_wide = pltpu.VMEM(((Z + 4) * C2, V), BF)
    part_rows = 9 * C2 // z.share
    packed = 3 * part_rows // 2
    dk_wide = pltpu.VMEM((part_rows, 192), F32)
    dm, bm, kf, *hdm = call(
        lambda *r: back_body(z, 5, 4, 0, z.share, *r), meta,
        [df, *hdf, yf, *fars(hf), *fars(stf), *bf, ym, *fars(stm), gains, shifts, w["b_final"]],
        [((Z, C2, V), F32), ((2 * C2, 128), F32), ((packed, 128), F32)] + sent(1, C2, V),
        [wide_p, x_wide, dk_wide, *parts],
    )
    bm, hdm, kf = both(bm), neighbours(hdm), both(kf)
    gskip, gcoarse, bc, km, small_gate, *hg = call(
        lambda *r: merge_back_body(z, z.share, *r), meta,
        [dm, *hdm, ym, *fars(hm), *fars(stm), *bm, Far(skip, 1), Far(lifted, 1), Far(pre, 1), Far(gc, 0),
         Far(yc), *fars(hc), *fars(stc), gains, shifts, tail, w["b_merge"], w["gate_t"]],
        [((Z, C2, V), F32), ((Zc + 2, C3, Vc), F32), ((2 * C3, 128), F32), ((3 * packed, 128), F32),
         ((264, 128), F32)] + sent(2, C3, Vc),
        [pltpu.VMEM((6 * 9 * C2, V), BF), pltpu.VMEM((384, V), BF), pltpu.VMEM((96, V), BF), pltpu.VMEM((384, V), BF),
         pltpu.VMEM((Zc + 2, C3, V // 2), F32), pltpu.VMEM((3 * part_rows, 192), F32),
         pltpu.VMEM((Z, C2, V), F32), pltpu.SemaphoreType.DMA((Z // 4,))],
        hbm_outs=(0,),
    )
    bc, hg, km, small_gate = both(bc), neighbours(hg), both(km), both(small_gate)
    d3, b3, kc, *hd3 = call(
        lambda *r: coarse_back_body(z, z.share, *r), meta,
        [gcoarse, *hg, Far(yc), *fars(hc), *fars(stc), *bc, Far(pooled), Far(gskip, 0), Far(y3, 0), *fars(st3),
         gains, shifts, w["b_coarse"]],
        [((Z, C2, V), F32), ((2 * C2, 128), F32), ((2 * packed, 128), F32)] + sent(1, C2, V),
        [pltpu.VMEM(((Zc + 2) * 9 * C3, Vc), BF), pltpu.VMEM(((Zc + 4) * C2, Vc), BF),
         pltpu.VMEM((2 * part_rows, 192), F32)],
    )
    b3, hd3, kc = both(b3), neighbours(hd3), both(kc)
    d2, b2, k3, *hd2 = call(
        lambda *r: back_body(z, 2, 1, 0, z.share, *r), meta,
        [d3, *hd3, Far(y3, 0), *fars(h3), *fars(st3), *b3, Far(y2, 0), *fars(st2), gains, shifts, w["b_third"]],
        [((Z, C2, V), F32), ((2 * C2, 128), F32), ((packed, 128), F32)] + sent(1, C2, V),
        [wide_p, x_wide, dk_wide, *parts],
    )
    b2, hd2, shared = both(b2), neighbours(hd2), shares([km, kf, kc, both(k3)])
    y1_planes = y1.reshape(Z + 2, C1, V)
    d1, b1, k2 = call(
        lambda *r: back_body(z, 1, 0, 1, 1, *r), meta,
        [d2, *hd2, Far(y2, 0), *fars(h2), *fars(st2), *b2, Far(y1_planes, 1), *fars(st1), gains, shifts,
         w["b_second"], ],
        [((Z, C1, V), F32), ((2 * C1, 128), F32), ((9 * C2, 128), F32)],
        [wide_p, pltpu.VMEM(((Z + 4) * C1, V), BF), pltpu.VMEM((9 * C2, 3 * C1), F32), pltpu.VMEM((C1, V), F32), pltpu.VMEM((C1, V), F32)],
    )
    b1, k2 = both(b1), both(k2)
    (k1,) = call(
        lambda *r: first_back_body(z, *r), meta,
        [d1, Far(y1_planes), Far(p_img), *fars(st1), *b1, gains, shifts, *[Held(part) for part in shared]],
        [((32, 128), F32)], [pltpu.VMEM((Z * C1, V), BF)],
    )
    k1 = both(k1)
    pieces = (k1, k2, small_head, small_gate, b1, b2, b3, bc, bm, bf)
    grad, norm = call(
        lambda *r: gather_body(z, *r), meta,
        fars(shared) + [Far(part) for pair in pieces for part in pair],
        [((ROWS, 128), F32), ((8, 128), F32)],
        [pltpu.VMEM((27 * C3, 128), F32), pltpu.VMEM((27 * C2, 128), F32),
         pltpu.VMEM((ROWS + 8, 128), F32), pltpu.VMEM((2048, 128), F32)]
        + [pltpu.VMEM((z.share, 7 * packed, 128), F32)] + [pltpu.VMEM((27 * C2, 128), F32)] * 2,
    )
    gradient = grad.reshape(ROWS * 128)[: weights.shape[0]]
    grad_norm = norm[0, 0]
    clipped = gradient * jnp.minimum(1.0, CLIP_NORM / (grad_norm + 1e-06))
    moment_one = BETA_ONE * first_moment + (1.0 - BETA_ONE) * clipped
    moment_two = BETA_TWO * second_moment + (1.0 - BETA_TWO) * clipped * clipped
    corrected_one = moment_one / (1.0 - BETA_ONE**STEP)
    corrected_two = moment_two / (1.0 - BETA_TWO**STEP)
    updated = weights - LEARN_RATE * (
        corrected_one / (jnp.sqrt(corrected_two) + ADAM_EPS) + DECAY_RATE * weights
    )
    return (grad_norm, moment_one, moment_two, updated, updated.astype(BF))


def solution(mesh):
    depth, height = mesh.shape["depth"], mesh.shape["height"]

    def step(images, labels, weights, first_moment, second_moment):
        z = Sizes(depth, height, images.shape[1] // depth, images.shape[2] // height, images.shape[3])
        placed = (P(None, "depth", "height", None), P(None, "depth", "height", None), P(), P(), P())
        return jax.shard_map(
            lambda *arrays: local(z, *arrays), mesh=mesh, in_specs=placed,
            out_specs=(P(), P(), P(), P(), P()), check_vma=False,
        )(images, labels, weights, first_moment, second_moment)

    return step
```

```python
import functools
import math

import jax
import jax.numpy as jnp
from jax import lax
from jax.experimental import pallas as pl
from jax.experimental.pallas import tpu as pltpu
from jax.sharding import PartitionSpec as P

C1 = 32
C2 = 64
C3 = 128
CG = 32
CLS = 3
STEP = 10

EPS_NORM = 1e-05
CLIP_NORM = 0.005
LEARN_RATE = 0.02
BETA_ONE = 0.9
BETA_TWO = 0.999
ADAM_EPS = 1e-08
DECAY_RATE = 0.01

BF = jnp.bfloat16
F32 = jnp.float32
AXES = ("depth", "height")
WIDTHS = (C1, C2, C2, C3, C2, C2)
NORM_AT = (0, 32, 96, 160, 288, 352)
VOXELS = 18432
PAD = 160
ROWS = 6552
ROW_FIRST, ROW_SECOND, ROW_THIRD, ROW_COARSE = 0, 8, 440, 1304
ROW_MERGE, ROW_FINAL, ROW_GATE_SKIP, ROW_GATE_COARSE, ROW_TAIL = 3032, 5624, 6488, 6504, 6536
TAIL_AT = 836448
TAIL_LEN = 1479
T_GATE_BIAS, T_SCORE, T_SCORE_BIAS, T_HEAD_FINE, T_BIAS_FINE = 0, 32, 64, 65, 257
T_HEAD_COARSE, T_BIAS_COARSE, T_GAINS, T_SHIFTS = 260, 644, 647, 1063


class Sizes:
    def __init__(self, mesh_depth, mesh_height, local_z, local_y, width):
        self.D, self.H, self.lz, self.ly = mesh_depth, mesh_height, local_z, local_y
        self.planes = mesh_depth * local_z
        self.PY = mesh_height * local_y
        self.V = self.PY * width
        self.nb = self.V // 128
        self.half = self.nb // 2
        self.nbc = self.nb // 4
        self.Vc = self.V // 4
        self.total = self.planes * self.V
        self.G = 2
        while (self.planes // self.G + 2) * self.V > VOXELS:
            self.G *= 2
        self.Z = self.planes // self.G
        self.Zc = self.Z // 2
        self.ZP = -(-(self.Z + 4) // 16) * 16
        self.DP = self.planes - self.Z + self.ZP + 8
        self.two = self.G == 2
        self.share = 4 if mesh_depth * mesh_height // self.G % 4 == 0 else 1


def dot(left, right):
    return lax.dot_general(left, right, (((1,), (0,)), ((), ())), preferred_element_type=F32)


def dot_nt(left, right):
    return lax.dot_general(left, right, (((1,), (1,)), ((), ())), preferred_element_type=F32)


def ds(start, size, multiple=16):
    return pl.ds(start if isinstance(start, int) else pl.multiple_of(start, multiple), size)


def cols(k):
    return slice(k * 128, (k + 1) * 128)


def lanes(channels):
    return lax.broadcasted_iota(jnp.int32, (channels, 128), 1)


def sigmoid(value):
    return 0.5 * jnp.tanh(0.5 * value) + 0.5


def roll(value, steps):
    return pltpu.roll(value, steps % 128, axis=1)


def split_dot(value, matrix):
    high = value.astype(BF)
    low = (value - high.astype(F32)).astype(BF)
    return dot(high, matrix) + dot(low, matrix)


def norm_coefs(sums, gain, shift, channels, count):
    mean = jnp.sum(sums[:channels], axis=1, keepdims=True) / count
    square = jnp.sum(sums[channels : 2 * channels], axis=1, keepdims=True) / count
    inv = lax.rsqrt(square - mean * mean + EPS_NORM)
    full = (channels, 128)
    mean, inv = jnp.broadcast_to(mean, full), jnp.broadcast_to(inv, full)
    factor = inv * gain
    return mean, inv, factor, shift - mean * factor


def grad_coefs(sums, mean, inv, factor, channels, count):
    total = jnp.sum(sums[:channels], axis=1, keepdims=True) / count
    cross = jnp.sum(sums[channels : 2 * channels], axis=1, keepdims=True) / count
    slope = factor * cross * inv
    return slope, slope * mean - factor * total


def run(steps):
    for unused in steps:
        pass


def interleave(first, second, ratio):
    first, second = iter(first), iter(second)
    done = object()
    one = two = None
    while one is not done or two is not done:
        one = next(first, done)
        for unused in range(ratio):
            two = next(second, done)


def place_windows(p_ref, bases, rows, offset, blocks, seg):
    run(window_steps(p_ref, bases, rows, offset, blocks, seg))


def window_steps(p_ref, bases, rows, offset, blocks, seg):
    channels, count = blocks[0].shape[0], len(blocks)
    lane = lanes(channels)
    inner = lane & (seg - 1)
    zero = jnp.zeros((channels, 128), BF)
    blocks = [v.astype(BF) for v in blocks]
    for c in range(3):
        if c == 0:
            low = [jnp.where(inner == 0, zero, roll(v, 1)) for v in blocks]
        elif c == 1:
            low = blocks
        else:
            low = [jnp.where(inner == seg - 1, zero, roll(v, 127)) for v in blocks]
        before = jnp.where(lane < seg, zero, roll(low[-1], seg))
        after = jnp.where(lane >= 128 - seg, zero, roll(low[0], 128 - seg))
        extended = [before] + low + [after]
        for b in range(3):
            for k in range(count):
                for base in bases:
                    p_ref[ds(base + (3 * b + c) * rows + offset, channels), cols(k)] = extended[k + b]
            yield


def pack_wide(out, wide, rows):
    half = rows // 2
    out[:rows, :] = wide[:, :128]
    low = jnp.concatenate([wide[:half, 128:], wide[half:, 128:]], axis=1)
    out[rows : rows + half, :] = low


def unpack_wide(full, full_b, at, packed, start, rows):
    half = rows // 2
    full[at : at + rows, :] = packed[start : start + rows, :].astype(F32)
    low = packed[start + rows : start + rows + half, :].astype(F32)
    full_b[at : at + half, :] = low
    full_b[at + half : at + rows, :] = roll(low, 64)


def unrolled(count, times, body):
    while count % times:
        times -= 1

    def step(t, carry):
        for r in range(times):
            body(times * t + r)
        return carry

    if count == times:
        for i in range(count):
            body(i)
    else:
        lax.fori_loop(0, count // times, step, 0)


def fold_sums(values):
    total = values[0]
    for value in values[1:]:
        total = total + value
    return total


CHUNK = 4


class Far:
    def __init__(self, array, base=None):
        self.array, self.base = array, base


class Held:
    def __init__(self, array):
        self.array = array


class Copied:
    def __init__(self, source, target, sems, base):
        self.target, self.copies = target, []
        self.source, self.sems, self.base = source, sems, base

    def copy(self, c):
        if self.base is None:
            return pltpu.make_async_copy(self.source, self.target, self.sems.at[0])
        span = pl.ds(self.base + c * CHUNK, CHUNK)
        return pltpu.make_async_copy(self.source.at[span], self.target.at[span], self.sems.at[c])

    def __getitem__(self, at):
        return self.target[at]

    @property
    def shape(self):
        return self.target.shape


def need(c, *refs):
    for ref in refs:
        if isinstance(ref, Copied):
            ref.copy(c).wait()


def kernel_call(body, meta, ins, outs, scratch=(), far_outs=False, hbm_outs=(), room=12, us=10):
    def size(shape, dtype):
        return math.prod(shape[:-1]) * (-(-shape[-1] // 128) * 128) * jnp.dtype(dtype).itemsize

    scratch = list(scratch)
    own = len(scratch)
    hbm = range(len(outs)) if far_outs else hbm_outs
    held = [isinstance(a, Held) for a in ins]
    far = [a if isinstance(a, (Far, Held)) else None for a in ins]
    arrays = [
        a if f is None else pltpu.with_memory_space_constraint(a.array, pltpu.HBM) for a, f in zip(ins, far)
    ]
    far = [None if h else f for f, h in zip(far, held)]
    chunks = []
    for a in far:
        if a is not None:
            count = 1 if a.base is None else (a.array.shape[0] - 2 * a.base) // CHUNK
            chunks.append(count)
            scratch += [pltpu.VMEM(a.array.shape, a.array.dtype), pltpu.SemaphoreType.DMA((count,))]
    if far_outs:
        scratch += [pltpu.VMEM(*o) for o in outs] + [pltpu.SemaphoreType.DMA((len(outs),))]

    def wrapped(meta_ref, *refs):
        in_refs, out_refs = refs[: len(ins)], refs[len(ins) : len(ins) + len(outs)]
        own_refs, extra = refs[len(ins) + len(outs) :][:own], list(refs[len(ins) + len(outs) + own :])
        given, whole = [], []
        for a, h, ref in zip(far, held, in_refs):
            if h:
                continue
            if a is None:
                given.append(ref)
                continue
            target, sems = extra.pop(0), extra.pop(0)
            copied = Copied(ref, target, sems, a.base)
            if a.base is None:
                copied.copy(0).start()
                whole.append(copied)
                given.append(target)
            else:
                given.append(copied)
        for copied in given:
            if isinstance(copied, Copied):
                for c in range(copied.sems.shape[0]):
                    copied.copy(c).start()
        for copied in whole:
            copied.copy(0).wait()
        if not far_outs:
            body(meta_ref, *given, *out_refs, *own_refs)
            return
        buffers, sems = extra[:-1], extra[-1]
        copies = [
            pltpu.make_async_copy(source, target, sems.at[index])
            for index, (source, target) in enumerate(zip(buffers, out_refs))
        ]
        body(lambda index: copies[index].start(), meta_ref, *given, *buffers, *own_refs)
        for copy in copies:
            copy.wait()

    vmem = sum(size(x.shape, x.dtype) for x in scratch if getattr(x, "memory_space", None) == pltpu.VMEM) + (room << 20)
    return pl.pallas_call(
        wrapped,
        out_shape=[pltpu.HBM(*o) if k in hbm else jax.ShapeDtypeStruct(*o) for k, o in enumerate(outs)],
        in_specs=[pl.BlockSpec(memory_space=pltpu.SMEM)]
        + [pl.BlockSpec(memory_space=pltpu.HBM if a or h else pltpu.VMEM) for a, h in zip(far, held)],
        out_specs=[pl.BlockSpec(memory_space=pltpu.HBM if k in hbm else pltpu.VMEM) for k in range(len(outs))],
        scratch_shapes=scratch,
        compiler_params=pltpu.CompilerParams(vmem_limit_bytes=min(vmem, 63 << 20)),
        cost_estimate=pl.CostEstimate(flops=us * 1000000000, bytes_accessed=1000, transcendentals=0),
    )(meta, *arrays)


def prep_body(z, leave, meta, flat, tail, big, second, third, coarse, merge, final, b_second, b_third,
              b_coarse, b_merge, b_final, gate, gate_t, head, head_t, gains, shifts, stage, stage_b):
    def unroll(row, taps_out, width):
        count = taps_out * width // 128
        if width == 192:
            rows = count // 3
            one, two, three = (flat[pl.ds(row + j, rows, stride=3), :] for j in range(3))
            left = lanes(rows) < 64
            turned = roll(three, 64)
            stage[pl.ds(0, rows, stride=2), :] = one
            stage_b[pl.ds(0, rows, stride=2), :] = two
            stage[pl.ds(1, rows, stride=2), :] = jnp.where(left, roll(two, 64), turned)
            stage_b[pl.ds(1, rows, stride=2), :] = turned
        else:
            pack = 128 // width
            block = flat[row : row + count, :]
            for j in range(pack):
                stage[pl.ds(j, count, stride=pack), :] = roll(block, -j * width) if j else block

    def staged(at, count, width):
        if width <= 128:
            return stage[at : at + count, :width]
        return jnp.concatenate([stage[at : at + count, :], stage_b[at : at + count, : width - 128]], axis=1)

    def forward(out_c, in_c):
        return [
            jnp.concatenate(
                [staged((9 * a + t) * out_c, out_c, in_c) for t in range(9)],
                axis=1,
            )
            for a in range(3)
        ]

    def backward_plane(out_c, in_c, a):
        at = 26 - 9 * a
        return jnp.concatenate(
            [staged((at - t) * out_c, out_c, in_c) for t in range(9)], axis=0
        ).T

    def backward(out_c, in_c):
        return jnp.concatenate(
            [staged((26 - t) * out_c, out_c, in_c) for t in range(27)], axis=0
        ).T

    def double(ref, full, copies, step):
        rows, width = full.shape
        for r in range(copies):
            parts = []
            if r:
                parts.append(jnp.zeros((rows, r * step), F32))
            parts.append(full)
            if r < copies - 1:
                parts.append(jnp.zeros((rows, (copies - 1 - r) * step), F32))
            ref[r * rows : (r + 1) * rows, :] = jnp.concatenate(parts, axis=1).astype(BF)

    block = flat[0:8, :]
    for j in range(4):
        stage[pl.ds(j, 8, stride=4), :] = roll(block, -j * 32) if j else block
    taps = stage[0:32, :32].T.astype(BF)
    tall = jnp.concatenate([taps] * (z.Z + 2), axis=0)
    shape = ((z.Z + 2) * C1, 9 * z.ZP)
    source = lax.broadcasted_iota(jnp.int32, (32, 9 * z.ZP), 0)
    target = lax.broadcasted_iota(jnp.int32, (32, 9 * z.ZP), 1) // z.ZP
    gap = lax.rem(lax.broadcasted_iota(jnp.int32, shape, 1), z.ZP) - (
        lax.broadcasted_iota(jnp.int32, shape, 0) // C1
    )
    total = jnp.zeros(shape, F32)
    for a in range(3):
        spread = dot(tall, jnp.where(source == target + 5 + 9 * a, 1.0, 0.0).astype(BF))
        total = total + jnp.where(gap == a, spread, 0.0)
    big[...] = total.astype(BF)
    leave(0)

    for index, row, ref, b_ref, width in (
        (1, ROW_SECOND, second, b_second, C1),
        (2, ROW_THIRD, third, b_third, C2),
        (5, ROW_FINAL, final, b_final, C2),
    ):
        unroll(row, 27 * C2, width)
        ref[...] = jnp.concatenate(forward(C2, width), axis=0).astype(BF)
        for a in range(3):
            b_ref[a * width : (a + 1) * width, :] = backward_plane(C2, width, a).astype(BF)
        leave(index)
        leave(10 if index == 5 else index + 5)
    unroll(ROW_COARSE, 27 * C3, C2)
    coarse[...] = jnp.concatenate(forward(C3, C2), axis=1).astype(BF)
    double(b_coarse, backward(C3, C2), 2, 9 * C3)
    leave(3)
    leave(8)
    unroll(ROW_MERGE, 27 * C2, C2 + C3)
    merge[...] = jnp.concatenate(forward(C2, C2 + C3), axis=0).astype(BF)
    b_merge[...] = backward(C2, C2 + C3).astype(BF)
    leave(4)
    leave(9)

    unroll(ROW_GATE_SKIP, CG, C2)
    gate_skip = stage[:CG, :C2]
    gate_coarse = flat[ROW_GATE_COARSE : ROW_GATE_COARSE + CG, :]
    lane = lanes(C3)

    def columns(at, channels):
        value = jnp.zeros((channels, 128), F32)
        for k in range(CLS):
            piece = tail[at + k * channels : at + (k + 1) * channels, :]
            value = jnp.where(lane[:channels] == k, piece, value)
        return value

    fine_cols = columns(T_HEAD_FINE, C2)
    coarse_cols = columns(T_HEAD_COARSE, C3)
    head_t[...] = fine_cols[:, :16].astype(BF)
    head[...] = fine_cols.T[:16, :].astype(BF)
    rows = jnp.concatenate(
        [
            jnp.concatenate([gate_skip, gate_coarse], axis=1),
            jnp.concatenate([jnp.zeros((16, C2), F32), coarse_cols.T[:16, :]], axis=1),
        ],
        axis=0,
    )
    gate[...] = rows.astype(BF)
    gate_t[...] = rows.T.astype(BF)
    gains[...] = tail[T_GAINS : T_GAINS + 416, :]
    shifts[...] = tail[T_SHIFTS : T_SHIFTS + 416, :]
    for index in range(11, 17):
        leave(index)


def prepare(z, meta, flat, tail):
    outs = [
        (((z.Z + 2) * C1, 9 * z.ZP), BF),
        ((192, 9 * C1), BF),
        ((192, 9 * C2), BF),
        ((128, 27 * C2), BF),
        ((192, 9 * 192), BF),
        ((192, 9 * C2), BF),
        ((96, 9 * C2), BF),
        ((192, 9 * C2), BF),
        ((128, 36 * C3), BF),
        ((192, 27 * C2), BF),
        ((192, 9 * C2), BF),
        ((48, 192), BF),
        ((192, 48), BF),
        ((16, C2), BF),
        ((C2, 16), BF),
        ((416, 128), F32),
        ((416, 128), F32),
    ]
    names = (
        "big", "second", "third", "coarse", "merge", "final", "b_second", "b_third", "b_coarse",
        "b_merge", "b_final", "gate", "gate_t", "head", "head_t", "gains", "shifts",
    )
    out = kernel_call(
        lambda *refs: prep_body(z, *refs), meta, [flat, tail], outs,
        [pltpu.VMEM((27 * C3, 128), F32), pltpu.VMEM((27 * C2, 128), F32)], far_outs=True,
    )
    return dict(zip(names, out))


def layer_gain(gains, layer):
    return gains[NORM_AT[layer] : NORM_AT[layer] + WIDTHS[layer], :]


def send_planes(z, meta, h_refs, source, count, planes):
    if z.two:
        start = jnp.where(meta[0] == 0, planes - count, 0)
        for j in range(count):
            h_refs[0][j] = source(start + j).astype(BF)
    else:
        for j in range(count):
            h_refs[0][j] = source(j).astype(BF)
            h_refs[1][j] = source(planes - count + j).astype(BF)


UNROLL = CHUNK


def flow(z, build, consume, ratio, fetch=(), leave=None):
    run(build(0, 0, 0))

    def body(t, carry):
        need(t, *fetch)
        for r in range(UNROLL):
            zp = UNROLL * t + r
            interleave(consume(zp, r % 2), build(zp + 1, (r + 1) % 2, None), ratio)
        if leave:
            leave(t)
        return carry

    lax.fori_loop(0, z.Z // UNROLL, body, 0)
    interleave(consume(z.Z, 0), build(z.Z + 1, 1, 1), ratio)
    run(consume(z.Z + 1, 1))


def scatter(zp, weight, window, width, parts, nb, finish):
    part_one, part_two = parts
    at = zp - 2 if isinstance(zp, int) else jnp.maximum(zp - 2, 0)
    for n in range(nb // 2):
        result = dot(weight[...], window[:, 256 * n : 256 * (n + 1)])
        for k in (2 * n, 2 * n + 1):
            piece = result[:, cols(k - 2 * n)]
            finish(at, k, part_one[:, cols(k)] + piece[2 * width :])
            part_one[:, cols(k)] = part_two[:, cols(k)] + piece[width : 2 * width]
            part_two[:, cols(k)] = piece[:width]
        yield


def add_sums(zp, st_ref, channels, first, second):
    first, second = fold_sums(first), fold_sums(second)
    if not isinstance(zp, int):
        first, second = jnp.where(zp >= 2, first, 0.0), jnp.where(zp >= 2, second, 0.0)
    st_ref[:channels, :] += first
    st_ref[channels : 2 * channels, :] += second


def convolve(z, weight, p_ref, parts, rows, channels, y_ref, st_ref, build, leave=None, ratio=3):
    st_ref[...] = jnp.zeros(st_ref.shape, F32)
    for part in parts:
        part[...] = jnp.zeros(part.shape, F32)

    def consume(zp, slot):
        values = []

        def finish(at, k, value):
            y_ref[at, :, cols(k)] = value
            values.append(value)

        window = p_ref.at[slot * rows : (slot + 1) * rows, :]
        yield from scatter(zp, weight, window, channels, parts, z.nb, finish)
        add_sums(zp, st_ref, channels, values, [v * v for v in values])

    flow(z, build, consume, ratio, leave=leave)


def mine_body(z, meta, images, labels, out, rows):
    for i in range(z.lz):
        rows[i * z.ly : (i + 1) * z.ly, :] = jnp.concatenate(
            [images[0, i], labels[0, i].astype(F32)], axis=1
        )
    value = rows[...].astype(BF)
    for i in range(out.shape[0]):
        out[i] = value


def first_body(z, meta, recv, big, y_ref, st_ref, p_ref, lab_ref, wide, rows):
    wide[...] = recv[...].astype(F32)
    rows[...] = jnp.zeros(rows.shape, F32)
    per = z.lz * z.ly
    for hh in range(z.H):
        for yy in range(z.ly):
            for zz in range(z.lz):
                rows[pl.ds((hh * z.ly + yy) * z.DP + 2 + zz, z.D, stride=z.lz), :] = wide[
                    pl.ds(hh * per + zz * z.ly + yy, z.D, stride=z.H * per), :
                ]
    lane = lanes(z.ZP)
    start = pl.multiple_of(meta[0] * z.Z // 8 * 8, 8)

    def source(y):
        if z.Z % 8 == 0:
            return rows[pl.ds(pl.multiple_of(y * z.DP + start, 8), z.ZP), :]
        block = rows[pl.ds(pl.multiple_of(y * z.DP + start, 8), z.ZP + 8), :]
        return jnp.where(lax.rem(meta[0], 2) == 0, block[: z.ZP], block[4 : z.ZP + 4])

    blocks = []
    hits = [jnp.zeros((1, 128), F32) for unused in range(CLS)]
    for k in range(z.nb):
        one, two = source(k), source(k + z.nb)
        blocks.append(jnp.where(lane < 64, one, roll(two, 64)))
        label = jnp.where(lane < 64, roll(one, 64), two)[2 : 2 + z.Z]
        for i in range(z.Z):
            lab_ref[i, :, cols(k)] = jnp.broadcast_to(label[i : i + 1], (8, 128))
        for c in range(CLS):
            hits[c] = hits[c] + jnp.sum(
                jnp.where(label == float(c), 1.0, 0.0), axis=0, keepdims=True
            )
    place_windows(p_ref, (0,), z.ZP, 0, blocks, 64)
    y_ref[...] = dot(big[...], p_ref[...])
    st_ref[...] = jnp.zeros(st_ref.shape, F32)

    def step(i):
        values = [y_ref[ds(C1 + i * C1, C1), cols(k)] for k in range(z.nb)]
        st_ref[:C1, :] += fold_sums(values)
        st_ref[C1 : 2 * C1, :] += fold_sums([v * v for v in values])

    unrolled(z.Z, 4, step)
    row = lax.broadcasted_iota(jnp.int32, (8, 128), 0)
    counts = jnp.zeros((8, 128), F32)
    for c in range(CLS):
        counts = jnp.where(row == c, hits[c], counts)
    st_ref[2 * C1 : 2 * C1 + 8, :] = counts


def second_body(z, meta, y1, sa, sb, gains, shifts, weight, y_ref, st_ref, *rest):
    h_refs, p_ref, parts = rest[:-3], rest[-3], rest[-2:]
    unused, unused, factor, level = norm_coefs(
        sa[...] + sb[...], layer_gain(gains, 0), layer_gain(shifts, 0), C1, z.total
    )

    def build(zp, slot, edge):
        blocks = []
        for k in range(z.nb):
            value = y1[ds(zp * C1, C1), cols(k)] * factor + level
            value = value * sigmoid(value)
            blocks.append(value if edge is None else jnp.where(meta[1 + edge] > 0, value, 0.0))
            if k % 2:
                yield
        yield from window_steps(p_ref, (slot * 9 * C1,), C1, 0, blocks, 64)

    convolve(z, weight, p_ref, parts, 9 * C1, C2, y_ref, st_ref, build)
    send_planes(z, meta, h_refs, lambda i: y_ref[i], 1, z.Z)


def middle_body(z, layer, send, meta, y_in, lo, hi, sa, sb, gains, shifts, weight, y_ref, st_ref, *rest):
    h_refs, p_ref, parts = rest[:-3], rest[-3], rest[-2:]
    unused, unused, factor, level = norm_coefs(
        sa[...] + sb[...], layer_gain(gains, layer), layer_gain(shifts, layer), C2, z.total
    )

    def build(zp, slot, edge):
        if edge is None:
            get = lambda k: y_in[zp - 1, :, cols(k)]
        else:
            get = lambda k: (lo, hi)[edge][0, :, cols(k)].astype(F32)
        blocks = []
        for k in range(z.nb):
            value = get(k) * factor + level
            value = value * sigmoid(value)
            blocks.append(value if edge is None else jnp.where(meta[1 + edge] > 0, value, 0.0))
            if k % 2:
                yield
        yield from window_steps(p_ref, (slot * 9 * C2,), C2, 0, blocks, 64)

    convolve(z, weight, p_ref, parts, 9 * C2, C2, y_ref, st_ref, build)
    send_planes(z, meta, h_refs, lambda i: y_ref[i], send, z.Z)


def pool_matrix(entries):
    row = lax.broadcasted_iota(jnp.int32, (256, 128), 0)
    col = lax.broadcasted_iota(jnp.int32, (256, 128), 1)
    same = (col // 32) == 2 * (lax.rem(row, 128) // 64) + row // 128
    return jnp.where(same, entries(lax.rem(row, 64), lax.rem(col, 32)), 0.0).astype(BF)


def mean_entries(fine, coarse):
    return jnp.where(fine // 2 == coarse, 0.125, 0.0)


def lift_entries(fine, coarse):
    near = fine // 2
    other = jnp.clip(jnp.where(lax.rem(fine, 2) == 0, near - 1, near + 1), 0, 31)
    return jnp.where(coarse == near, 0.75, 0.0) + jnp.where(coarse == other, 0.25, 0.0)


def coarse_body(z, meta, y3, lo, hi, sa, sb, gains, shifts, weight, skip, pooled, y_ref, st_ref, *rest):
    h_refs, p_ref = rest[:-1], rest[-1]
    unused, unused, factor, level = norm_coefs(
        sa[...] + sb[...], layer_gain(gains, 2), layer_gain(shifts, 2), C2, z.total
    )
    matrix = pool_matrix(mean_entries)

    def plane(jp, gets, valid, skip_at):
        sums = []
        for i in range(z.half):
            parts = []
            for index, get in enumerate(gets):
                for k in (2 * i, 2 * i + 1):
                    value = get(k) * factor + level
                    value = value * sigmoid(value)
                    if valid is not None:
                        value = jnp.where(valid > 0, value, 0.0)
                    if skip_at[index] is not None:
                        skip[skip_at[index], :, cols(k)] = value.astype(BF)
                    parts.append(value)
            sums.append(fold_sums(parts))
        blocks = []
        for kc in range(z.nbc):
            pair = jnp.concatenate([sums[kc], sums[kc + z.nbc]], axis=1)
            blocks.append(split_dot(pair, matrix))
        for kc in range(z.nbc):
            pooled[jp, :, cols(kc)] = blocks[kc].astype(BF)
        place_windows(p_ref, (jp * (9 * C2),), C2, 0, blocks, 32)

    plane(0, [lambda k: lo[0, :, cols(k)].astype(F32), lambda k: lo[1, :, cols(k)].astype(F32)],
          meta[1], (None, 0))
    plane(z.Zc + 1, [lambda k: hi[0, :, cols(k)].astype(F32), lambda k: hi[1, :, cols(k)].astype(F32)],
          meta[2], (z.Z + 1, None))

    def step(j):
        plane(j + 1, [lambda k: y3[2 * j, :, cols(k)], lambda k: y3[2 * j + 1, :, cols(k)]],
              None, (2 * j + 1, 2 * j + 2))

    unrolled(z.Zc, 4, step)
    st_ref[...] = jnp.zeros(st_ref.shape, F32)

    def conv(j):
        result = dot(weight[...], p_ref[ds(j * (9 * C2), 27 * C2), :])
        y_ref[j] = result
        values = [result[:, cols(k)] for k in range(z.nbc)]
        st_ref[:C3, :] += fold_sums(values)
        st_ref[C3 : 2 * C3, :] += fold_sums([v * v for v in values])

    unrolled(z.Zc, 8, conv)
    send_planes(z, meta, h_refs, lambda i: y_ref[i], 1, z.Zc)


def merge_body(z, meta, yc, lo, hi, sa, sb, gains, shifts, tail, skip, gate, weight,
               lifted_out, pre_out, logit_out, y_ref, st_ref, *rest):
    h_refs = rest[:-10]
    p_ref, t_ref, act, mixed, part_one, part_two, lifted, pre_ref, logit_ref, sems = rest[-10:]
    unused, unused, factor, level = norm_coefs(
        sa[...] + sb[...], layer_gain(gains, 3), layer_gain(shifts, 3), C3, z.total // 8
    )
    matrix = pool_matrix(lift_entries).astype(F32).T.astype(BF)
    n = z.half

    def coarse_act(get):
        out = []
        for k in range(z.nbc):
            value = get(k) * factor + level
            out.append((value * sigmoid(value)).astype(BF))
        return out

    for k, value in enumerate(coarse_act(lambda k: lo[0, :, cols(k)].astype(F32))):
        act[0, :, cols(k)] = value
    for k, value in enumerate(coarse_act(lambda k: hi[0, :, cols(k)].astype(F32))):
        act[z.Zc + 1, :, cols(k)] = value

    def own(j, carry):
        for k, value in enumerate(coarse_act(lambda k: yc[j, :, cols(k)])):
            act[j + 1, :, cols(k)] = value
        return carry

    lax.fori_loop(0, z.Zc, own, 0)

    @pl.when(meta[1] == 0)
    def low_edge():
        act[0] = act[1]

    @pl.when(meta[2] == 0)
    def high_edge():
        act[z.Zc + 1] = act[z.Zc]

    def spread(jp, slot):
        rows = [None] * n
        for k in range(z.nbc):
            both = dot(act[jp, :, cols(k)], matrix)
            rows[k], rows[k + z.nbc] = both[:, :128], both[:, 128:]
        lane = lanes(C3)
        first, last = rows[0], rows[n - 1]
        before = jnp.where(lane < 64, first, roll(last, 64))
        after = jnp.where(lane < 64, roll(first, 64), last)
        extended = [before] + rows + [after]
        for i in range(n):
            t_ref[slot, :, cols(2 * i)] = 0.25 * extended[i] + 0.75 * extended[i + 1]
            t_ref[slot, :, cols(2 * i + 1)] = 0.75 * extended[i + 1] + 0.25 * extended[i + 2]
            if i % 2:
                yield

    run(spread(0, 0))
    bias = tail[T_GATE_BIAS : T_GATE_BIAS + CG, :]
    score = tail[T_SCORE : T_SCORE + CG, :]
    score_bias = tail[T_SCORE_BIAS : T_SCORE_BIAS + 1, :]

    def build(zp, slot, edge):
        turn = zp % 2 if isinstance(zp, int) else 1 - (slot + 1) % 2
        wa, wb = (0.75, 0.25) if turn == 0 else (0.25, 0.75)
        old = (zp // 2) % 2 if isinstance(zp, int) else lax.rem(zp // 2, 2)
        new = 1 - old
        if turn == 0:
            yield from spread(zp // 2 + 1, new)
        valid = None if edge is None else meta[1 + edge]
        base, row = slot * 9 * 192, slot * 192
        mixed[row : row + C2, :] = skip[zp]
        wide = []
        for k in range(z.nb):
            value = (wa * t_ref[old, :, cols(k)] + wb * t_ref[new, :, cols(k)]).astype(BF)
            mixed[row + C2 : row + 192, cols(k)] = value
            lifted[zp, :, cols(k)] = value
            value = value.astype(F32)
            wide.append(value if valid is None else jnp.where(valid > 0, value, 0.0))
            if k % 2:
                yield
        gated = []
        for n in range(z.half):
            rows = dot(gate[...], mixed[row : row + 192, 256 * n : 256 * (n + 1)])
            logit_ref[zp, :, 256 * n : 256 * (n + 1)] = rows[CG:]
            for k in (2 * n, 2 * n + 1):
                pre = rows[:CG, cols(k - 2 * n)] + bias
                pre_ref[zp, :, cols(k)] = pre
                inner = pre * sigmoid(pre)
                alpha = sigmoid(jnp.sum(score * inner, axis=0, keepdims=True) + score_bias)
                if valid is not None:
                    alpha = jnp.where(valid > 0, alpha, 0.0)
                gated.append(mixed[row : row + C2, cols(k)].astype(F32) * alpha)
            yield
        yield from window_steps(p_ref, (base,), 192, C2, wide, 64)
        yield from window_steps(p_ref, (base,), 192, 0, gated, 64)

    pairs = ((lifted, lifted_out), (pre_ref, pre_out), (logit_ref, logit_out))

    def leaving(t):
        span = pl.ds(4 * t + 1, 4)
        return [
            pltpu.make_async_copy(a.at[span], b.at[span], sems.at[n, t]) for n, (a, b) in enumerate(pairs)
        ]

    def leave(t):
        for copy in leaving(t):
            copy.start()

    convolve(z, weight, p_ref, (part_one, part_two), 9 * 192, C2, y_ref, st_ref, build, leave, ratio=5)
    send_planes(z, meta, h_refs, lambda i: y_ref[i], 1, z.Z)
    for t in range(z.Z // 4):
        for copy in leaving(t):
            copy.wait()


def heads_body(z, meta, yf, sa, sb, ca, cb, lab, logit_ref, gains, shifts, tail, head, head_t,
               d_ref, bs_ref, small, gc_ref, *rest):
    h_refs, acts = rest[:-1], rest[-1]
    mean, inv, factor, level = norm_coefs(
        sa[...] + sb[...], layer_gain(gains, 5), layer_gain(shifts, 5), C2, z.total
    )
    counts = jnp.sum(ca[2 * C1 :] + cb[2 * C1 :], axis=1, keepdims=True)
    row = lax.broadcasted_iota(jnp.int32, (8, 1), 0)
    everything = jnp.sum(jnp.where(row < CLS, counts, 0.0), axis=0, keepdims=True)
    class_weight = jnp.where(row < CLS, 2.0 * everything / (3.0 * counts + everything), 0.0)
    weight_total = jnp.sum(counts * class_weight, axis=0, keepdims=True)
    scaled = class_weight / weight_total
    scaled = jnp.concatenate([scaled, jnp.zeros((8, 1), F32)], axis=0)
    rows16 = lax.broadcasted_iota(jnp.int32, (16, 128), 0)
    pad13 = jnp.zeros((13, 128), F32)
    bias_fine = jnp.concatenate([tail[T_BIAS_FINE : T_BIAS_FINE + 3, :], pad13], axis=0)
    bias_coarse = jnp.concatenate([tail[T_BIAS_COARSE : T_BIAS_COARSE + 3, :], pad13], axis=0)
    bs_ref[...] = jnp.zeros(bs_ref.shape, F32)
    small[...] = jnp.zeros(small.shape, F32)

    def logit_grad(logits, label, times):
        logits = jnp.where(rows16 < CLS, logits, -1e30)
        top = jnp.max(logits, axis=0, keepdims=True)
        terms = jnp.where(rows16 < CLS, jnp.exp(logits - top), 0.0)
        soft = terms / jnp.sum(terms, axis=0, keepdims=True)
        onehot = jnp.where(rows16.astype(F32) == label, 1.0, 0.0)
        weight = jnp.sum(scaled * onehot, axis=0, keepdims=True)
        return ((soft - onehot) * (weight * times)).astype(BF)

    def step(i, slot):
        act = acts.at[slot * C2 : (slot + 1) * C2, :]
        for k in range(z.nb):
            value = yf[i, :, cols(k)] * factor + level
            act[:, cols(k)] = (value * sigmoid(value)).astype(BF)
        logits = dot(head[...], act[...])
        fine, bias_sum, coarse_sum = [], [], []
        for k in range(z.nb):
            label = lab[i, 0:1, cols(k)]
            grad = logit_grad(logits[:, cols(k)] + bias_fine, label, 1.0)
            fine.append(grad)
            bias_sum.append(grad.astype(F32))
            grad = logit_grad(logit_ref[i + 1, :, cols(k)] + bias_coarse, label, 0.5)
            gc_ref[i, :, cols(k)] = grad
            coarse_sum.append(grad.astype(F32))
        fine = jnp.concatenate(fine, axis=1)
        small[:C2, :16] += dot_nt(act[...], fine)
        small[C2 : C2 + 16, :] += fold_sums(bias_sum)
        small[C2 + 16 : C2 + 32, :] += fold_sums(coarse_sum)
        back = dot(head_t[...], fine)
        parts, cross = [], []
        for k in range(z.nb):
            y = yf[i, :, cols(k)]
            pre = y * factor + level
            sig = sigmoid(pre)
            grad = back[:, cols(k)] * (sig * (1.0 + pre * (1.0 - sig)))
            d_ref[i, :, cols(k)] = grad
            parts.append(grad)
            cross.append(grad * ((y - mean) * inv))
        bs_ref[:C2, :] += fold_sums(parts)
        bs_ref[C2:, :] += fold_sums(cross)

    def four(t, carry):
        for r in range(4):
            step(4 * t + r, r)
        return carry

    lax.fori_loop(0, z.Z // 4, four, 0)
    send_planes(z, meta, h_refs, lambda i: d_ref[i], 1, z.Z)


def dy_builder(z, meta, layer, count, refs, p_ref):
    d, d_lo, d_hi, y, y_lo, y_hi, sums, back, gains, shifts = refs
    channels = WIDTHS[layer]
    mean, inv, factor, unused = norm_coefs(
        sums, layer_gain(gains, layer), layer_gain(shifts, layer), channels, count
    )
    slope, level = grad_coefs(back, mean, inv, factor, channels, count)

    def build(zp, bases, edge):
        get_d, get_y = (lambda k: d[zp - 1, :, cols(k)]), (lambda k: y[zp - 1, :, cols(k)])
        if edge is not None:
            get_d = lambda k: (d_lo, d_hi)[edge][0, :, cols(k)].astype(F32)
            get_y = lambda k: (y_lo[y_lo.shape[0] - 1, :, cols(k)], y_hi[0, :, cols(k)])[edge].astype(F32)
        out = []
        for k in range(z.nb):
            value = factor * get_d(k) - slope * get_y(k) + level
            out.append(value if edge is None else jnp.where(meta[1 + edge] > 0, value, 0.0))
            if k % 2:
                yield
        yield from window_steps(p_ref, bases, channels, 0, out, 64)

    def build_or_edge(zp, bases, last):
        out = []
        own = jnp.minimum(zp - 1, z.Z - 1)
        for k in range(z.nb):
            near_d = jnp.where(last, d_hi[0, :, cols(k)].astype(F32), d[own, :, cols(k)])
            near_y = jnp.where(last, y_hi[0, :, cols(k)].astype(F32), y[own, :, cols(k)])
            value = factor * near_d - slope * near_y + level
            out.append(jnp.where(jnp.logical_and(last, meta[2] == 0), 0.0, value))
            if k % 2:
                yield
        yield from window_steps(p_ref, bases, channels, 0, out, 64)

    build.or_edge = build_or_edge
    return build


def back_body(z, layer, below, y_base, share, meta, d, d_lo, d_hi, y, y_lo, y_hi, sa, sb, ba, bb,
              yb, ua, ub, gains, shifts, weight, *rest):
    d_ref, bs_ref, dk_out = rest[:3]
    h_refs, (p_ref, x_ref, dk_ref), parts = rest[3:-5], rest[-5:-2], rest[-2:]
    make = dy_builder(z, meta, layer, z.total,
                       (d, d_lo, d_hi, y, y_lo, y_hi, sa[...] + sb[...], ba[...] + bb[...], gains, shifts), p_ref)
    width = WIDTHS[below]
    mean, inv, factor, level = norm_coefs(
        ua[...] + ub[...], layer_gain(gains, below), layer_gain(shifts, below), width, z.total
    )
    edge = jnp.zeros((2 * width, z.V), BF)
    x_ref[: 2 * width, :] = edge
    x_ref[(z.Z + 2) * width :, :] = edge
    bs_ref[...] = jnp.zeros(bs_ref.shape, F32)
    rows = 9 * WIDTHS[layer]
    part = rows // share
    dk_ref[...] = jnp.zeros(dk_ref.shape, F32)

    for part_ref in parts:
        part_ref[...] = jnp.zeros(part_ref.shape, F32)

    def build(zp, slot, edge):
        return make(zp, (slot * rows,), edge)

    def consume(zp, slot):
        if not isinstance(zp, int):
            for k in range(z.nb):
                pre = yb[zp + y_base, :, cols(k)] * factor + level
                x_ref[ds((zp + 2) * width, width), cols(k)] = (pre * sigmoid(pre)).astype(BF)
        sums, cross = [], []

        def finish(at, k, value):
            y_value = yb[at + y_base, :, cols(k)]
            pre = y_value * factor + level
            sig = sigmoid(pre)
            grad = value * (sig * (1.0 + pre * (1.0 - sig)))
            d_ref[at, :, cols(k)] = grad
            sums.append(grad)
            cross.append(grad * ((y_value - mean) * inv))

        yield from scatter(zp, weight, p_ref.at[slot * rows : (slot + 1) * rows, :], width, parts, z.nb, finish)
        add_sums(zp, bs_ref, width, sums, cross)
        if share == 1:
            window = p_ref[slot * rows : (slot + 1) * rows, :]
        else:
            window = p_ref[ds(slot * rows + meta[3] * part, part), :]
        dk_ref[...] += dot_nt(window, x_ref[ds(zp * width, 3 * width), :])

    flow(z, build, consume, 3, (d, y, yb))
    if width == C2:
        pack_wide(dk_out, dk_ref, part)
    else:
        dk_out[:, : 3 * width] = dk_ref[...]
    if h_refs:
        send_planes(z, meta, h_refs, lambda i: d_ref[i], 1, z.Z)


def merge_back_body(z, share, meta, d, d_lo, d_hi, y, y_lo, y_hi, sa, sb, ba, bb, skip, lifted, pre_ref, gc_ref,
                    yc, yc_lo, yc_hi, ua, ub, gains, shifts, tail, weight, gate_t,
                    gskip_out, gcoarse, bs_ref, dk_out, small, *rest):
    h_refs, (p_ref, eg, x_ref, acc, dk_ref, gskip, sems) = rest[:-7], rest[-7:]
    build = dy_builder(z, meta, 4, z.total,
                       (d, d_lo, d_hi, y, y_lo, y_hi, sa[...] + sb[...], ba[...] + bb[...], gains, shifts), p_ref)
    score = tail[T_SCORE : T_SCORE + CG, :]
    score_bias = tail[T_SCORE_BIAS : T_SCORE_BIAS + 1, :]
    small[...] = jnp.zeros(small.shape, F32)
    dk_ref[...] = jnp.zeros(dk_ref.shape, F32)
    acc[...] = jnp.zeros(acc.shape, F32)
    n = z.half
    lane = lanes(C3)
    rows = 9 * C2
    part = 27 * C2 // share

    def plane(i, r4):
        start = r4 * rows
        turn = (r4 % 2) * 256
        side = (r4 % 2) * 48
        eg[side + CG : side + 48, :] = gc_ref[i]
        x_ref[turn + C2 : turn + 192, :] = lifted[i + 1]
        x_ref[turn + 192 : turn + 256, :] = skip[i + 1]
        wide, e_sum, s_sum, r_sum = [], [], [], []
        for q in range(z.half):
            span = slice(256 * q, 256 * (q + 1))
            result = dot(weight[...], p_ref[start : start + 3 * rows, span])
            alphas = []
            for k in (2 * q, 2 * q + 1):
                piece = result[:C2, cols(k - 2 * q)]
                pre = pre_ref[i + 1, :, cols(k)]
                sig = sigmoid(pre)
                inner = pre * sig
                alpha = sigmoid(jnp.sum(score * inner, axis=0, keepdims=True) + score_bias)
                near = skip[i + 1, :, cols(k)].astype(F32)
                grad = jnp.sum(piece * near, axis=0, keepdims=True)
                grad = grad * alpha * (1.0 - alpha)
                e = (score * grad * (sig * (1.0 + pre * (1.0 - sig)))).astype(BF)
                eg[side : side + CG, cols(k)] = e
                x_ref[turn : turn + C2, cols(k)] = (near * alpha).astype(BF)
                alphas.append(alpha)
                e_sum.append(e.astype(F32))
                s_sum.append(grad * inner)
                r_sum.append(grad)
            extra = dot(gate_t[...], eg[side : side + 48, span])
            for k in (2 * q, 2 * q + 1):
                at = cols(k - 2 * q)
                gskip[i, :, cols(k)] = result[:C2, at] * alphas[k - 2 * q] + extra[:C2, at]
                wide.append(result[C2:, at] + extra[C2:, at])
            yield
        small[192:224, :] += fold_sums(e_sum)
        small[224:256, :] += fold_sums(s_sum)
        small[256:257, :] += fold_sums(r_sum)
        low = [
            0.75 * (wide[2 * m] + wide[2 * m + 1])
            + (0.25 * wide[2 * m + 2] if m < n - 1 else 0.0)
            + (0.25 * wide[2 * m - 1] if m > 0 else 0.0)
            for m in range(n)
        ]
        before, after = 0.25 * wide[0], 0.25 * wide[-1]
        low[0] = low[0] + jnp.where(lane < 64, before, roll(after, 64))
        low[n - 1] = low[n - 1] + jnp.where(lane < 64, roll(before, 64), after)
        j, r = i // 2, r4 % 2
        for m in range(n):
            acc[j + 1, :, cols(m)] += 0.75 * low[m]
            acc[j + 2 * r, :, cols(m)] += 0.25 * low[m]
        yield
        if share == 1:
            window = p_ref[start : start + 3 * rows, :]
        else:
            window = p_ref[ds(start + meta[3] * part, part), :]
        tall = jnp.concatenate([window, eg[side : side + 48, :]], axis=0)
        dk_ref[...] += dot_nt(tall, x_ref[turn : turn + 256, :])

    need(0, d, y)
    for zp in range(3):
        run(build(zp, (zp * rows,), 0 if zp == 0 else None))

    def four(t, carry):
        need(t, skip, lifted, pre_ref, gc_ref)
        for r in range(4):
            if r == 2:

                @pl.when(t + 1 < z.Z // 4)
                def fetch():
                    need(t + 1, d, y)

            at = (r + 3) % 4
            bases = (at * rows, (at + 4) * rows) if at < 2 else (at * rows,)
            zp = 4 * t + r + 3
            if r < 2:
                steps = build(zp, bases, None)
            else:
                steps = build.or_edge(zp, bases, zp == z.Z + 1)
            interleave(plane(4 * t + r, r), steps, 2)
        leaving(t).start()
        return carry

    def leaving(t):
        span = pl.ds(4 * t, 4)
        return pltpu.make_async_copy(gskip.at[span], gskip_out.at[span], sems.at[t])

    lax.fori_loop(0, z.Z // 4, four, 0)
    pack_wide(dk_out, dk_ref[:part, :192], part)
    tall = dk_ref[part:, :].T
    small[:C2, :48] = tall[192:]
    small[C2:192, :48] = tall[C2:192]

    matrix = pool_matrix(lift_entries)

    def shrink(jp, carry):
        for k in range(z.nbc):
            pair = jnp.concatenate([acc[jp, :, cols(k)], acc[jp, :, cols(k + z.nbc)]], axis=1)
            gcoarse[jp, :, cols(k)] = split_dot(pair, matrix)
        return carry

    lax.fori_loop(0, z.Zc + 2, shrink, 0)

    @pl.when(meta[1] == 0)
    def low_edge():
        gcoarse[1] += gcoarse[0]
        gcoarse[0] = jnp.zeros((C3, z.Vc), F32)

    @pl.when(meta[2] == 0)
    def high_edge():
        gcoarse[z.Zc] += gcoarse[z.Zc + 1]
        gcoarse[z.Zc + 1] = jnp.zeros((C3, z.Vc), F32)

    mean, inv, factor, level = norm_coefs(
        ua[...] + ub[...], layer_gain(gains, 3), layer_gain(shifts, 3), C3, z.total // 8
    )
    bs_ref[...] = jnp.zeros(bs_ref.shape, F32)

    def sums(jp, get):
        for k in range(z.nbc):
            value = get(k)
            pre = value * factor + level
            sig = sigmoid(pre)
            grad = gcoarse[jp, :, cols(k)] * (sig * (1.0 + pre * (1.0 - sig)))
            bs_ref[:C3, :] += grad
            bs_ref[C3:, :] += grad * ((value - mean) * inv)

    sums(0, lambda k: yc_lo[0, :, cols(k)].astype(F32))
    sums(z.Zc + 1, lambda k: yc_hi[0, :, cols(k)].astype(F32))

    def own(j, carry):
        sums(j + 1, lambda k: yc[j, :, cols(k)])
        return carry

    lax.fori_loop(0, z.Zc, own, 0)
    if z.two:
        start = jnp.where(meta[0] == 0, z.Zc, 0)
        for m in range(2):
            h_refs[0][m] = gcoarse[start + m].astype(BF)
    else:
        for m in range(2):
            h_refs[0][m] = gcoarse[m].astype(BF)
            h_refs[1][m] = gcoarse[z.Zc + m].astype(BF)
    for t in range(z.Z // 4):
        leaving(t).wait()


def coarse_back_body(z, share, meta, gcoarse, g_lo, g_hi, yc, yc_lo, yc_hi, sa, sb, ba, bb, pooled, gskip, y3,
                     ua, ub, gains, shifts, weight, d_ref, bs_ref, dk_out, *rest):
    h_refs, (p_ref, x_ref, dk_ref) = rest[:-3], rest[-3:]
    mean, inv, factor, level = norm_coefs(
        sa[...] + sb[...], layer_gain(gains, 3), layer_gain(shifts, 3), C3, z.total // 8
    )
    slope, offset = grad_coefs(ba[...] + bb[...], mean, inv, factor, C3, z.total // 8)

    def plane(jp, get_y, extra, valid):
        out = []
        for k in range(z.nbc):
            value = get_y(k)
            pre = value * factor + level
            sig = sigmoid(pre)
            grad = gcoarse[jp, :, cols(k)] + extra(k)
            grad = grad * (sig * (1.0 + pre * (1.0 - sig)))
            grad = factor * grad - slope * value + offset
            out.append(grad if valid is None else jnp.where(valid > 0, grad, 0.0))
        place_windows(p_ref, (jp * (9 * C3),), C3, 0, out, 32)

    def from_lo(m):
        return lambda k: jnp.where(meta[1] > 0, g_lo[m, :, cols(k)].astype(F32), 0.0)

    def from_hi(m):
        return lambda k: jnp.where(meta[2] > 0, g_hi[m, :, cols(k)].astype(F32), 0.0)

    plane(0, lambda k: yc_lo[0, :, cols(k)].astype(F32), from_lo(0), meta[1])
    plane(1, lambda k: yc[0, :, cols(k)], from_lo(1), None)

    def inner(j):
        plane(j + 2, lambda k: yc[j + 1, :, cols(k)], lambda k: 0.0, None)

    if z.Zc > 2:
        unrolled(z.Zc - 2, 3, inner)
    plane(z.Zc, lambda k: yc[z.Zc - 1, :, cols(k)], from_hi(0), None)
    plane(z.Zc + 1, lambda k: yc_hi[0, :, cols(k)].astype(F32), from_hi(1), meta[2])

    edge = jnp.zeros((2 * C2, z.Vc), BF)
    x_ref[: 2 * C2, :] = edge
    x_ref[(z.Zc + 2) * C2 :, :] = edge

    for j in range(z.Zc):
        x_ref[(j + 2) * C2 : (j + 3) * C2, :] = pooled[j + 1]
    mean, inv, factor, level = norm_coefs(
        ua[...] + ub[...], layer_gain(gains, 2), layer_gain(shifts, 2), C2, z.total
    )
    matrix = pool_matrix(mean_entries).astype(F32).T.astype(BF)
    bs_ref[...] = jnp.zeros(bs_ref.shape, F32)
    rows = 9 * C3

    def step(s, carry):
        need(s, y3, gskip)
        result = dot(weight[...], p_ref[ds(s * (2 * rows), 4 * rows), :])
        parts, cross = [], []
        for r in range(2):
            low = result[r * C2 : (r + 1) * C2]
            spread = [None] * z.half
            for k in range(z.nbc):
                both = split_dot(low[:, cols(k)], matrix)
                spread[k], spread[k + z.nbc] = both[:, :128], both[:, 128:]
            for q in range(2):
                at = 4 * s + 2 * r + q
                for k in range(z.nb):
                    value = y3[at, :, cols(k)]
                    pre = value * factor + level
                    sig = sigmoid(pre)
                    grad = spread[k // 2] + gskip[at, :, cols(k)]
                    grad = grad * (sig * (1.0 + pre * (1.0 - sig)))
                    d_ref[at, :, cols(k)] = grad
                    parts.append(grad)
                    cross.append(grad * ((value - mean) * inv))
        bs_ref[:C2, :] += fold_sums(parts)
        bs_ref[C2:, :] += fold_sums(cross)
        return carry

    lax.fori_loop(0, z.Zc // 2, step, 0)
    part = rows // share

    def kernel_grad(zp):
        window = p_ref[ds(zp * rows + meta[3] * part, part), :]
        return dot_nt(window, x_ref[zp * C2 : (zp + 3) * C2, :])

    dk_ref[...] = fold_sums([kernel_grad(zp) for zp in range(z.Zc + 2)])
    pack_wide(dk_out, dk_ref, part)
    send_planes(z, meta, h_refs, lambda i: d_ref[i], 1, z.Z)


def first_back_body(z, meta, d, y1, p_img, sa, sb, ba, bb, gains, shifts, dk_ref, low):
    mean, inv, factor, unused = norm_coefs(
        sa[...] + sb[...], layer_gain(gains, 0), layer_gain(shifts, 0), C1, z.total
    )
    slope, level = grad_coefs(ba[...] + bb[...], mean, inv, factor, C1, z.total)

    def step(i):
        for k in range(z.nb):
            value = factor * d[i, :, cols(k)] - slope * y1[i + 1, :, cols(k)] + level
            low[ds(i * C1, C1), cols(k)] = value.astype(BF)

    unrolled(z.Z, 4, step)
    table = dot_nt(p_img[...], low[...])
    shape = (9 * z.ZP, z.Z * C1)
    gap = lax.rem(lax.broadcasted_iota(jnp.int32, shape, 0), z.ZP) - (
        lax.broadcasted_iota(jnp.int32, shape, 1) // C1
    )
    dk_ref[...] = jnp.zeros(dk_ref.shape, F32)
    for a in range(3):
        kept = jnp.where(gap == a + 1, table, 0.0)
        folded = fold_sums([kept[:, cols(k)] for k in range(z.Z * C1 // 128)])
        folded = folded + roll(folded, 64)
        folded = folded + roll(folded, 32)
        for t in range(9):
            dk_ref[9 * a + t : 9 * a + t + 1, :] = jnp.sum(
                folded[t * z.ZP : (t + 1) * z.ZP], axis=0, keepdims=True
            )


def gather_body(z, meta, *refs):
    ins, (out, norm), (stage, stage_b, flat, column, quarters, full, full_b) = refs[:-9], refs[-9:-7], refs[-7:]
    shared, ins = ins[: z.share], ins[z.share :]
    pairs = [(ins[2 * j], ins[2 * j + 1]) for j in range(len(ins) // 2)]
    (first, second, small_head, small_gate, b_first, b_second, b_third, b_coarse, b_merge, b_final) = pairs
    for k in range(z.share):
        quarters[jnp.bitwise_xor(meta[3], k)] = shared[k][...].astype(F32)

    def unpack(start, count):
        part = count // z.share
        for k in range(z.share):
            unpack_wide(full, full_b, k * part, quarters.at[k], start, part)

    def total(pair):
        return pair[0][...] + pair[1][...]

    def pack(row, taps_out, width):
        count = taps_out * width // 128
        fold = 128 // width
        lane = lanes(count)
        value = stage[pl.ds(0, count, stride=fold), :]
        for j in range(1, fold):
            part = roll(stage[pl.ds(j, count, stride=fold), :], j * width)
            value = jnp.where(lane < j * width, value, part)
        flat[row : row + count, :] = value

    flat[ROWS : ROWS + 8, :] = jnp.zeros((8, 128), F32)
    stage[0:5, :32] = jnp.zeros((5, 32), F32)
    stage[5:32, :32] = (first[0][...] + first[1][...])[:27, :32]
    pack(ROW_FIRST, 32, 32)
    wide_at = 27 * C2 // z.share * 3 // 2
    for row, out_c, in_c, source in (
        (ROW_SECOND, C2, C1, second),
        (ROW_THIRD, C2, C2, 2 * wide_at),
        (ROW_COARSE, C3, C2, wide_at + wide_at // 3),
        (ROW_FINAL, C2, C2, wide_at),
    ):
        count = 9 * out_c
        if source is second:
            full[:count, :] = total(second)
        else:
            unpack(source, count)
        for t in range(9):
            span = slice(t * out_c, (t + 1) * out_c)
            for a in range(3):
                at = (9 * a + 8 - t) * out_c
                if a * in_c < 128:
                    stage[at : at + out_c, :in_c] = full[span, a * in_c : (a + 1) * in_c]
                else:
                    stage[at : at + out_c, :in_c] = full_b[span, :in_c]
        pack(row, 27 * out_c, in_c)
    unpack(0, 27 * C2)
    for t in range(27):
        at = (26 - t) * C2
        stage[at : at + C2, :] = full[t * C2 : (t + 1) * C2, :]
        stage_b[at : at + C2, :64] = full_b[t * C2 : (t + 1) * C2, :64]
    half = 27 * C2 // 2
    even, even_b = stage[pl.ds(0, half, stride=2), :], stage_b[pl.ds(0, half, stride=2), :]
    odd, odd_b = stage[pl.ds(1, half, stride=2), :], stage_b[pl.ds(1, half, stride=2), :]
    left = lanes(half) < 64
    odd = roll(odd, 64)
    flat[pl.ds(ROW_MERGE, half, stride=3), :] = even
    flat[pl.ds(ROW_MERGE + 1, half, stride=3), :] = jnp.where(left, even_b, odd)
    flat[pl.ds(ROW_MERGE + 2, half, stride=3), :] = jnp.where(left, odd, roll(odd_b, 64))

    gate = total(small_gate)
    turned = gate[:192].T
    stage[:CG, :C2] = turned[:CG, :C2]
    pack(ROW_GATE_SKIP, CG, C2)
    flat[ROW_GATE_COARSE : ROW_GATE_COARSE + CG, :] = turned[:CG, C2:]
    heads = total(small_head)
    lane = lanes(C3)
    column[TAIL_LEN - 7 :, :] = jnp.zeros((2048 - TAIL_LEN + 7, 128), F32)
    column[T_GATE_BIAS : T_GATE_BIAS + CG, :] = gate[192:224]
    column[T_SCORE : T_SCORE + CG, :] = gate[224:256]
    column[T_SCORE_BIAS : T_SCORE_BIAS + 1, :] = gate[256:257]
    for k in range(CLS):
        at = T_HEAD_FINE + k * C2
        column[at : at + C2, :] = jnp.where(lane[:C2] == k, heads[:C2], 0.0)
        at = T_HEAD_COARSE + k * C3
        column[at : at + C3, :] = jnp.where(lane == CG + k, gate[C2:192], 0.0)
    column[T_BIAS_FINE : T_BIAS_FINE + 3, :] = heads[C2 : C2 + 3]
    column[T_BIAS_COARSE : T_BIAS_COARSE + 3, :] = heads[C2 + 16 : C2 + 19]
    for layer, pair in enumerate((b_first, b_second, b_third, b_coarse, b_merge, b_final)):
        sums = total(pair)
        width = WIDTHS[layer]
        at = T_GAINS + NORM_AT[layer]
        column[at : at + width, :] = sums[width : 2 * width]
        at = T_SHIFTS + NORM_AT[layer]
        column[at : at + width, :] = sums[:width]
    for k in range(16):
        flat[ROW_TAIL + k : ROW_TAIL + k + 1, :] = jnp.sum(
            column[k * 128 : (k + 1) * 128, :].T, axis=0, keepdims=True
        )
    chunk = ROWS // 21
    mask = lanes(chunk) < 96

    def finish(i, acc):
        base = pl.multiple_of(i * chunk, 8)
        block = roll(flat[pl.ds(base, chunk + 8), :], 96)
        out[pl.ds(base, chunk), :] = jnp.where(mask, block[1 : chunk + 1], block[2 : chunk + 2])
        return acc + fold_sums([block[8 * m : 8 * m + 8] * block[8 * m : 8 * m + 8] for m in range(chunk // 8)])

    acc = lax.fori_loop(0, 21, finish, jnp.zeros((8, 128), F32))
    sq = jnp.sum(jnp.sum(acc, axis=1, keepdims=True), axis=0, keepdims=True)
    norm[...] = jnp.broadcast_to(jnp.sqrt(sq), (8, 128))


def local(z, images, labels, weights, first_moment, second_moment):
    devices = z.D * z.H
    linear = lax.axis_index("depth") * z.H + lax.axis_index("height")
    position = lax.rem(linear, z.G)
    meta = jnp.stack(
        [position, (position > 0).astype(jnp.int32), (position < z.G - 1).astype(jnp.int32),
         lax.rem(linear // z.G, z.share)]
    ).astype(jnp.int32)

    call = functools.partial(kernel_call, room=12 if z.V <= 1024 else 18)

    def partner(value, step):
        return lax.ppermute(value, AXES, [(i, i ^ step) for i in range(devices)])

    def both(value):
        step = 1
        while step * 2 < z.G:
            value = value + partner(value, step)
            step *= 2
        return value, partner(value, step)

    def neighbours(sent):
        if z.two:
            got = partner(sent[0], 1)
            return got, got
        up = [(i, i + 1) for i in range(devices) if i % z.G != z.G - 1]
        return (
            lax.ppermute(sent[1], AXES, up),
            lax.ppermute(sent[0], AXES, [(j, i) for i, j in up]),
        )

    def shares(values):
        value = jnp.concatenate([one + two for one, two in values], axis=0).astype(BF)
        return [value] + [
            lax.ppermute(value, AXES, [(i, (i // z.G ^ k) * z.G + i % z.G) for i in range(devices)])
            for k in range(1, z.share)
        ]

    def sent(count, channels, lanes_):
        return [((count, channels, lanes_), BF)] * (1 if z.two else 2)

    V, Vc, Z, Zc = z.V, z.Vc, z.Z, z.Zc
    local_rows = z.lz * z.ly
    (mine,) = call(
        lambda *r: mine_body(z, *r), meta, [images, labels], [((devices, local_rows, 128), BF)],
        [pltpu.VMEM((local_rows, 128), F32)],
    )
    everyone = lax.all_to_all(
        mine, AXES, 0, 0
    ).reshape(devices * local_rows, 128)
    flat = jnp.pad(weights, (PAD, ROWS * 128 - PAD - weights.shape[0])).reshape(ROWS, 128)
    tail = jnp.broadcast_to(
        jnp.pad(weights[TAIL_AT:], (0, 1))[:, None], (TAIL_LEN + 1, 128)
    )
    w = prepare(z, meta, flat, tail)
    gains, shifts = w["gains"], w["shifts"]

    def fars(values, base=None):
        return [Far(value, base) for value in values]

    y1, st1, p_img, lab = call(
        lambda *r: first_body(z, *r), meta, [Far(everyone), Far(w["big"])],
        [(((Z + 2) * C1, V), F32), ((72, 128), F32), ((9 * z.ZP, V), BF), ((Z, 8, V), F32)],
        [pltpu.VMEM((devices * local_rows, 128), F32), pltpu.VMEM((z.PY * z.DP, 128), F32)],
    )
    st1 = both(st1)
    parts = [pltpu.VMEM((C2, V), F32), pltpu.VMEM((C2, V), F32)]
    y2, st2, *h2 = call(
        lambda *r: second_body(z, *r), meta, [y1, *st1, gains, shifts, w["second"]],
        [((Z, C2, V), F32), ((2 * C2, 128), F32)] + sent(1, C2, V),
        [pltpu.VMEM((2 * 9 * C1, V), BF), *parts],
    )
    st2, h2 = both(st2), neighbours(h2)
    wide_p = pltpu.VMEM((2 * 9 * C2, V), BF)
    y3, st3, *h3 = call(
        lambda *r: middle_body(z, 1, 2, *r), meta, [y2, *h2, *st2, gains, shifts, w["third"]],
        [((Z, C2, V), F32), ((2 * C2, 128), F32)] + sent(2, C2, V), [wide_p, *parts],
    )
    st3, h3 = both(st3), neighbours(h3)
    skip, pooled, yc, stc, *hc = call(
        lambda *r: coarse_body(z, *r), meta, [y3, *h3, *st3, gains, shifts, w["coarse"]],
        [((Z + 2, C2, V), BF), ((Zc + 2, C2, Vc), BF), ((Zc, C3, Vc), F32), ((2 * C3, 128), F32)]
        + sent(1, C3, Vc),
        [pltpu.VMEM(((Zc + 2) * 9 * C2, Vc), BF)],
    )
    stc, hc = both(stc), neighbours(hc)
    lifted, pre, logits, ym, stm, *hm = call(
        lambda *r: merge_body(z, *r), meta,
        [yc, *hc, *stc, gains, shifts, tail, skip, w["gate"], w["merge"]],
        [((Z + 2, C3, V), BF), ((Z + 2, CG, V), F32), ((Z + 2, 16, V), F32), ((Z, C2, V), F32),
         ((2 * C2, 128), F32)] + sent(1, C2, V),
        [pltpu.VMEM((2 * 9 * 192, V), BF), pltpu.VMEM((2, C3, V), F32), pltpu.VMEM((Zc + 2, C3, Vc), BF),
         pltpu.VMEM((384, V), BF), *parts, pltpu.VMEM((Z + 2, C3, V), BF), pltpu.VMEM((Z + 2, CG, V), F32),
         pltpu.VMEM((Z + 2, 16, V), F32), pltpu.SemaphoreType.DMA((3, Z // 4))],
        hbm_outs=(0, 1, 2),
    )
    stm, hm = both(stm), neighbours(hm)
    yf, stf, *hf = call(
        lambda *r: middle_body(z, 4, 1, *r), meta, [ym, *hm, *stm, gains, shifts, w["final"]],
        [((Z, C2, V), F32), ((2 * C2, 128), F32)] + sent(1, C2, V), [wide_p, *parts],
    )
    stf, hf = both(stf), neighbours(hf)
    counts = fars(st1)
    df, bf, small_head, gc, *hdf = call(
        lambda *r: heads_body(z, *r), meta,
        [yf, *stf, *counts, Far(lab), Far(logits), gains, shifts, tail, w["head"], w["head_t"]],
        [((Z, C2, V), F32), ((2 * C2, 128), F32), ((C2 + 32, 128), F32), ((Z, 16, V), BF)] + sent(1, C2, V),
        [pltpu.VMEM((4 * C2, V), BF)],
    )
    bf, hdf, small_head = both(bf), neighbours(hdf), both(small_head)
    x_wide = pltpu.VMEM(((Z + 4) * C2, V), BF)
    part_rows = 9 * C2 // z.share
    packed = 3 * part_rows // 2
    dk_wide = pltpu.VMEM((part_rows, 192), F32)
    dm, bm, kf, *hdm = call(
        lambda *r: back_body(z, 5, 4, 0, z.share, *r), meta,
        [df, *hdf, yf, *hf, *stf, *bf, ym, *fars(stm), gains, shifts, w["b_final"]],
        [((Z, C2, V), F32), ((2 * C2, 128), F32), ((packed, 128), F32)] + sent(1, C2, V),
        [wide_p, x_wide, dk_wide, *parts],
    )
    bm, hdm, kf = both(bm), neighbours(hdm), both(kf)
    gskip, gcoarse, bc, km, small_gate, *hg = call(
        lambda *r: merge_back_body(z, z.share, *r), meta,
        [dm, *hdm, ym, *fars(hm), *fars(stm), *bm, Far(skip, 1), Far(lifted, 1), Far(pre, 1), Far(gc, 0),
         Far(yc), *fars(hc), *fars(stc), gains, shifts, tail, w["b_merge"], w["gate_t"]],
        [((Z, C2, V), F32), ((Zc + 2, C3, Vc), F32), ((2 * C3, 128), F32), ((3 * packed, 128), F32),
         ((264, 128), F32)] + sent(2, C3, Vc),
        [pltpu.VMEM((6 * 9 * C2, V), BF), pltpu.VMEM((96, V), BF), pltpu.VMEM((512, V), BF),
         pltpu.VMEM((Zc + 2, C3, V // 2), F32), pltpu.VMEM((3 * part_rows + 48, 256), F32),
         pltpu.VMEM((Z, C2, V), F32), pltpu.SemaphoreType.DMA((Z // 4,))],
        hbm_outs=(0,),
    )
    bc, hg, km, small_gate = both(bc), neighbours(hg), both(km), both(small_gate)
    d3, b3, kc, *hd3 = call(
        lambda *r: coarse_back_body(z, z.share, *r), meta,
        [gcoarse, *hg, Far(yc), *fars(hc), *fars(stc), *bc, Far(pooled), Far(gskip, 0), Far(y3, 0), *fars(st3),
         gains, shifts, w["b_coarse"]],
        [((Z, C2, V), F32), ((2 * C2, 128), F32), ((2 * packed, 128), F32)] + sent(1, C2, V),
        [pltpu.VMEM(((Zc + 2) * 9 * C3, Vc), BF), pltpu.VMEM(((Zc + 4) * C2, Vc), BF),
         pltpu.VMEM((2 * part_rows, 192), F32)],
    )
    b3, hd3, kc = both(b3), neighbours(hd3), both(kc)
    d2, b2, k3, *hd2 = call(
        lambda *r: back_body(z, 2, 1, 0, z.share, *r), meta,
        [d3, *hd3, Far(y3, 0), *fars(h3), *fars(st3), *b3, Far(y2, 0), *fars(st2), gains, shifts, w["b_third"]],
        [((Z, C2, V), F32), ((2 * C2, 128), F32), ((packed, 128), F32)] + sent(1, C2, V),
        [wide_p, x_wide, dk_wide, *parts],
    )
    b2, hd2, shared = both(b2), neighbours(hd2), shares([km, kf, kc, both(k3)])
    y1_planes = y1.reshape(Z + 2, C1, V)
    d1, b1, k2 = call(
        lambda *r: back_body(z, 1, 0, 1, 1, *r), meta,
        [d2, *hd2, Far(y2, 0), *fars(h2), *fars(st2), *b2, Far(y1_planes, 1), *fars(st1), gains, shifts,
         w["b_second"], ],
        [((Z, C1, V), F32), ((2 * C1, 128), F32), ((9 * C2, 128), F32)],
        [wide_p, pltpu.VMEM(((Z + 4) * C1, V), BF), pltpu.VMEM((9 * C2, 3 * C1), F32), pltpu.VMEM((C1, V), F32), pltpu.VMEM((C1, V), F32)],
    )
    b1, k2 = both(b1), both(k2)
    (k1,) = call(
        lambda *r: first_back_body(z, *r), meta,
        [d1, Far(y1_planes), Far(p_img), *fars(st1), *b1, gains, shifts, *[Held(part) for part in shared]],
        [((32, 128), F32)], [pltpu.VMEM((Z * C1, V), BF)],
    )
    k1 = both(k1)
    pieces = (k1, k2, small_head, small_gate, b1, b2, b3, bc, bm, bf)
    grad, norm = call(
        lambda *r: gather_body(z, *r), meta,
        fars(shared) + [Far(part) for pair in pieces for part in pair],
        [((ROWS, 128), F32), ((8, 128), F32)],
        [pltpu.VMEM((27 * C3, 128), F32), pltpu.VMEM((27 * C2, 128), F32),
         pltpu.VMEM((ROWS + 8, 128), F32), pltpu.VMEM((2048, 128), F32)]
        + [pltpu.VMEM((z.share, 7 * packed, 128), F32)] + [pltpu.VMEM((27 * C2, 128), F32)] * 2,
    )
    gradient = grad.reshape(ROWS * 128)[: weights.shape[0]]
    grad_norm = norm[0, 0]
    clipped = gradient * jnp.minimum(1.0, CLIP_NORM / (grad_norm + 1e-06))
    moment_one = BETA_ONE * first_moment + (1.0 - BETA_ONE) * clipped
    moment_two = BETA_TWO * second_moment + (1.0 - BETA_TWO) * clipped * clipped
    corrected_one = moment_one / (1.0 - BETA_ONE**STEP)
    corrected_two = moment_two / (1.0 - BETA_TWO**STEP)
    updated = weights - LEARN_RATE * (
        corrected_one / (jnp.sqrt(corrected_two) + ADAM_EPS) + DECAY_RATE * weights
    )
    return (grad_norm, moment_one, moment_two, updated, updated.astype(BF))


def solution(mesh):
    depth, height = mesh.shape["depth"], mesh.shape["height"]

    def step(images, labels, weights, first_moment, second_moment):
        z = Sizes(depth, height, images.shape[1] // depth, images.shape[2] // height, images.shape[3])
        placed = (P(None, "depth", "height", None), P(None, "depth", "height", None), P(), P(), P())
        return jax.shard_map(
            lambda *arrays: local(z, *arrays), mesh=mesh, in_specs=placed,
            out_specs=(P(), P(), P(), P(), P()), check_vma=False,
        )(images, labels, weights, first_moment, second_moment)

    return step
```

```python
import functools
import math

import jax
import jax.numpy as jnp
from jax import lax
from jax.experimental import pallas as pl
from jax.experimental.pallas import tpu as pltpu
from jax.sharding import PartitionSpec as P

C1 = 32
C2 = 64
C3 = 128
CG = 32
CLS = 3
STEP = 10

EPS_NORM = 1e-05
CLIP_NORM = 0.005
LEARN_RATE = 0.02
BETA_ONE = 0.9
BETA_TWO = 0.999
ADAM_EPS = 1e-08
DECAY_RATE = 0.01

BF = jnp.bfloat16
F32 = jnp.float32
AXES = ("depth", "height")
WIDTHS = (C1, C2, C2, C3, C2, C2)
NORM_AT = (0, 32, 96, 160, 288, 352)
VOXELS = 18432
PAD = 160
ROWS = 6552
ROW_FIRST, ROW_SECOND, ROW_THIRD, ROW_COARSE = 0, 8, 440, 1304
ROW_MERGE, ROW_FINAL, ROW_GATE_SKIP, ROW_GATE_COARSE, ROW_TAIL = 3032, 5624, 6488, 6504, 6536
TAIL_AT = 836448
TAIL_LEN = 1479
T_GATE_BIAS, T_SCORE, T_SCORE_BIAS, T_HEAD_FINE, T_BIAS_FINE = 0, 32, 64, 65, 257
T_HEAD_COARSE, T_BIAS_COARSE, T_GAINS, T_SHIFTS = 260, 644, 647, 1063


class Sizes:
    def __init__(self, mesh_depth, mesh_height, local_z, local_y, width):
        self.D, self.H, self.lz, self.ly = mesh_depth, mesh_height, local_z, local_y
        self.planes = mesh_depth * local_z
        self.PY = mesh_height * local_y
        self.V = self.PY * width
        self.nb = self.V // 128
        self.half = self.nb // 2
        self.nbc = self.nb // 4
        self.Vc = self.V // 4
        self.total = self.planes * self.V
        self.G = 2
        while (self.planes // self.G + 2) * self.V > VOXELS:
            self.G *= 2
        self.Z = self.planes // self.G
        self.Zc = self.Z // 2
        self.ZP = -(-(self.Z + 4) // 16) * 16
        self.DP = self.planes - self.Z + self.ZP + 8
        self.two = self.G == 2
        self.share = 4 if mesh_depth * mesh_height // self.G % 4 == 0 else 1


def dot(left, right):
    return lax.dot_general(left, right, (((1,), (0,)), ((), ())), preferred_element_type=F32)


def dot_nt(left, right):
    return lax.dot_general(left, right, (((1,), (1,)), ((), ())), preferred_element_type=F32)


def ds(start, size, multiple=16):
    return pl.ds(start if isinstance(start, int) else pl.multiple_of(start, multiple), size)


def cols(k):
    return slice(k * 128, (k + 1) * 128)


def lanes(channels):
    return lax.broadcasted_iota(jnp.int32, (channels, 128), 1)


def sigmoid(value):
    return 0.5 * jnp.tanh(0.5 * value) + 0.5


def roll(value, steps):
    return pltpu.roll(value, steps % 128, axis=1)


def split_dot(value, matrix):
    high = value.astype(BF)
    low = (value - high.astype(F32)).astype(BF)
    return dot(high, matrix) + dot(low, matrix)


def norm_coefs(sums, gain, shift, channels, count):
    mean = jnp.sum(sums[:channels], axis=1, keepdims=True) / count
    square = jnp.sum(sums[channels : 2 * channels], axis=1, keepdims=True) / count
    inv = lax.rsqrt(square - mean * mean + EPS_NORM)
    full = (channels, 128)
    mean, inv = jnp.broadcast_to(mean, full), jnp.broadcast_to(inv, full)
    factor = inv * gain
    return mean, inv, factor, shift - mean * factor


def grad_coefs(sums, mean, inv, factor, channels, count):
    total = jnp.sum(sums[:channels], axis=1, keepdims=True) / count
    cross = jnp.sum(sums[channels : 2 * channels], axis=1, keepdims=True) / count
    slope = factor * cross * inv
    return slope, slope * mean - factor * total


def run(steps):
    for unused in steps:
        pass


def interleave(first, second, ratio):
    first, second = iter(first), iter(second)
    done = object()
    one = two = None
    while one is not done or two is not done:
        one = next(first, done)
        for unused in range(ratio):
            two = next(second, done)


def place_windows(p_ref, bases, rows, offset, blocks, seg):
    run(window_steps(p_ref, bases, rows, offset, blocks, seg))


def window_steps(p_ref, bases, rows, offset, blocks, seg):
    channels, count = blocks[0].shape[0], len(blocks)
    lane = lanes(channels)
    inner = lane & (seg - 1)
    zero = jnp.zeros((channels, 128), BF)
    blocks = [v.astype(BF) for v in blocks]
    for c in range(3):
        if c == 0:
            low = [jnp.where(inner == 0, zero, roll(v, 1)) for v in blocks]
        elif c == 1:
            low = blocks
        else:
            low = [jnp.where(inner == seg - 1, zero, roll(v, 127)) for v in blocks]
        before = jnp.where(lane < seg, zero, roll(low[-1], seg))
        after = jnp.where(lane >= 128 - seg, zero, roll(low[0], 128 - seg))
        extended = [before] + low + [after]
        for b in range(3):
            for k in range(count):
                for base in bases:
                    p_ref[ds(base + (3 * b + c) * rows + offset, channels), cols(k)] = extended[k + b]
            yield


def pack_wide(out, wide, rows):
    half = rows // 2
    out[:rows, :] = wide[:, :128]
    low = jnp.concatenate([wide[:half, 128:], wide[half:, 128:]], axis=1)
    out[rows : rows + half, :] = low


def unpack_wide(full, full_b, share, width, taps_out, packed, start, rows):
    half = rows // 2
    for m in range(0, rows, 8):
        at = m // width * taps_out + share * width + m % width
        full[at : at + 8, :] = packed[start + m : start + m + 8, :]
        low = start + rows + m % half
        low = packed[low : low + 8, :]
        full_b[at : at + 8, :] = low if m < half else roll(low, 64)


def share_steps(q_ref, bases, share, index, blocks, seg):
    if share == 1:
        return
    width = blocks[0].shape[0] // share
    picked = []
    for value in blocks:
        value = value.astype(BF)
        part = value[:width]
        for k in range(1, share):
            part = jnp.where(index == k, value[k * width : (k + 1) * width], part)
        picked.append(part)
    yield from window_steps(q_ref, tuple(base // share for base in bases), width, 0, picked, seg)


def unrolled(count, times, body):
    while count % times:
        times -= 1

    def step(t, carry):
        for r in range(times):
            body(times * t + r)
        return carry

    if count == times:
        for i in range(count):
            body(i)
    else:
        lax.fori_loop(0, count // times, step, 0)


def fold_sums(values):
    total = values[0]
    for value in values[1:]:
        total = total + value
    return total


CHUNK = 4


class Far:
    def __init__(self, array, base=None):
        self.array, self.base = array, base


class Held:
    def __init__(self, array):
        self.array = array


class Copied:
    def __init__(self, source, target, sems, base):
        self.target, self.copies = target, []
        self.source, self.sems, self.base = source, sems, base

    def copy(self, c):
        if self.base is None:
            return pltpu.make_async_copy(self.source, self.target, self.sems.at[0])
        span = pl.ds(self.base + c * CHUNK, CHUNK)
        return pltpu.make_async_copy(self.source.at[span], self.target.at[span], self.sems.at[c])

    def __getitem__(self, at):
        return self.target[at]

    @property
    def shape(self):
        return self.target.shape


def need(c, *refs):
    for ref in refs:
        if isinstance(ref, Copied):
            ref.copy(c).wait()


def kernel_call(body, meta, ins, outs, scratch=(), far_outs=False, hbm_outs=(), room=12, us=10):
    def size(shape, dtype):
        return math.prod(shape[:-1]) * (-(-shape[-1] // 128) * 128) * jnp.dtype(dtype).itemsize

    scratch = list(scratch)
    own = len(scratch)
    hbm = range(len(outs)) if far_outs else hbm_outs
    held = [isinstance(a, Held) for a in ins]
    far = [a if isinstance(a, (Far, Held)) else None for a in ins]
    arrays = [
        a if f is None else pltpu.with_memory_space_constraint(a.array, pltpu.HBM) for a, f in zip(ins, far)
    ]
    far = [None if h else f for f, h in zip(far, held)]
    chunks = []
    for a in far:
        if a is not None:
            count = 1 if a.base is None else (a.array.shape[0] - 2 * a.base) // CHUNK
            chunks.append(count)
            scratch += [pltpu.VMEM(a.array.shape, a.array.dtype), pltpu.SemaphoreType.DMA((count,))]
    if far_outs:
        scratch += [pltpu.VMEM(*o) for o in outs] + [pltpu.SemaphoreType.DMA((len(outs),))]

    def wrapped(meta_ref, *refs):
        in_refs, out_refs = refs[: len(ins)], refs[len(ins) : len(ins) + len(outs)]
        own_refs, extra = refs[len(ins) + len(outs) :][:own], list(refs[len(ins) + len(outs) + own :])
        given, whole = [], []
        for a, h, ref in zip(far, held, in_refs):
            if h:
                continue
            if a is None:
                given.append(ref)
                continue
            target, sems = extra.pop(0), extra.pop(0)
            copied = Copied(ref, target, sems, a.base)
            if a.base is None:
                copied.copy(0).start()
                whole.append(copied)
                given.append(target)
            else:
                given.append(copied)
        for copied in given:
            if isinstance(copied, Copied):
                for c in range(copied.sems.shape[0]):
                    copied.copy(c).start()
        for copied in whole:
            copied.copy(0).wait()
        if not far_outs:
            body(meta_ref, *given, *out_refs, *own_refs)
            return
        buffers, sems = extra[:-1], extra[-1]
        copies = [
            pltpu.make_async_copy(source, target, sems.at[index])
            for index, (source, target) in enumerate(zip(buffers, out_refs))
        ]
        body(lambda index: copies[index].start(), meta_ref, *given, *buffers, *own_refs)
        for copy in copies:
            copy.wait()

    vmem = sum(size(x.shape, x.dtype) for x in scratch if getattr(x, "memory_space", None) == pltpu.VMEM) + (room << 20)
    return pl.pallas_call(
        wrapped,
        out_shape=[pltpu.HBM(*o) if k in hbm else jax.ShapeDtypeStruct(*o) for k, o in enumerate(outs)],
        in_specs=[pl.BlockSpec(memory_space=pltpu.SMEM)]
        + [pl.BlockSpec(memory_space=pltpu.HBM if a or h else pltpu.VMEM) for a, h in zip(far, held)],
        out_specs=[pl.BlockSpec(memory_space=pltpu.HBM if k in hbm else pltpu.VMEM) for k in range(len(outs))],
        scratch_shapes=scratch,
        compiler_params=pltpu.CompilerParams(vmem_limit_bytes=min(vmem, 63 << 20)),
        cost_estimate=pl.CostEstimate(flops=us * 1000000000, bytes_accessed=1000, transcendentals=0),
    )(meta, *arrays)


def prep_body(z, leave, meta, flat, tail, big, second, third, coarse, merge, final, b_second, b_third,
              b_coarse, b_merge, b_final, gate, gate_t, head, head_t, gains, shifts, stage, stage_b):
    def unroll(row, taps_out, width):
        count = taps_out * width // 128
        if width == 192:
            rows = count // 3
            one, two, three = (flat[pl.ds(row + j, rows, stride=3), :] for j in range(3))
            left = lanes(rows) < 64
            turned = roll(three, 64)
            stage[pl.ds(0, rows, stride=2), :] = one
            stage_b[pl.ds(0, rows, stride=2), :] = two
            stage[pl.ds(1, rows, stride=2), :] = jnp.where(left, roll(two, 64), turned)
            stage_b[pl.ds(1, rows, stride=2), :] = turned
        else:
            pack = 128 // width
            block = flat[row : row + count, :]
            for j in range(pack):
                stage[pl.ds(j, count, stride=pack), :] = roll(block, -j * width) if j else block

    def staged(at, count, width):
        if width <= 128:
            return stage[at : at + count, :width]
        return jnp.concatenate([stage[at : at + count, :], stage_b[at : at + count, : width - 128]], axis=1)

    def forward(out_c, in_c):
        return [
            jnp.concatenate(
                [staged((9 * a + t) * out_c, out_c, in_c) for t in range(9)],
                axis=1,
            )
            for a in range(3)
        ]

    def backward_plane(out_c, in_c, a):
        at = 26 - 9 * a
        return jnp.concatenate(
            [staged((at - t) * out_c, out_c, in_c) for t in range(9)], axis=0
        ).T

    def backward(out_c, in_c):
        return jnp.concatenate(
            [staged((26 - t) * out_c, out_c, in_c) for t in range(27)], axis=0
        ).T

    def double(ref, full, copies, step):
        rows, width = full.shape
        for r in range(copies):
            parts = []
            if r:
                parts.append(jnp.zeros((rows, r * step), F32))
            parts.append(full)
            if r < copies - 1:
                parts.append(jnp.zeros((rows, (copies - 1 - r) * step), F32))
            ref[r * rows : (r + 1) * rows, :] = jnp.concatenate(parts, axis=1).astype(BF)

    block = flat[0:8, :]
    for j in range(4):
        stage[pl.ds(j, 8, stride=4), :] = roll(block, -j * 32) if j else block
    taps = stage[0:32, :32].T.astype(BF)
    tall = jnp.concatenate([taps] * (z.Z + 2), axis=0)
    shape = ((z.Z + 2) * C1, 9 * z.ZP)
    source = lax.broadcasted_iota(jnp.int32, (32, 9 * z.ZP), 0)
    target = lax.broadcasted_iota(jnp.int32, (32, 9 * z.ZP), 1) // z.ZP
    gap = lax.rem(lax.broadcasted_iota(jnp.int32, shape, 1), z.ZP) - (
        lax.broadcasted_iota(jnp.int32, shape, 0) // C1
    )
    total = jnp.zeros(shape, F32)
    for a in range(3):
        spread = dot(tall, jnp.where(source == target + 5 + 9 * a, 1.0, 0.0).astype(BF))
        total = total + jnp.where(gap == a, spread, 0.0)
    big[...] = total.astype(BF)
    leave(0)

    for index, row, ref, b_ref, width in (
        (1, ROW_SECOND, second, b_second, C1),
        (2, ROW_THIRD, third, b_third, C2),
        (5, ROW_FINAL, final, b_final, C2),
    ):
        unroll(row, 27 * C2, width)
        ref[...] = jnp.concatenate(forward(C2, width), axis=0).astype(BF)
        for a in range(3):
            b_ref[a * width : (a + 1) * width, :] = backward_plane(C2, width, a).astype(BF)
        leave(index)
        leave(10 if index == 5 else index + 5)
    unroll(ROW_COARSE, 27 * C3, C2)
    coarse[...] = jnp.concatenate(forward(C3, C2), axis=1).astype(BF)
    double(b_coarse, backward(C3, C2), 2, 9 * C3)
    leave(3)
    leave(8)
    unroll(ROW_MERGE, 27 * C2, C2 + C3)
    merge[...] = jnp.concatenate(forward(C2, C2 + C3), axis=0).astype(BF)
    b_merge[...] = backward(C2, C2 + C3).astype(BF)
    leave(4)
    leave(9)

    unroll(ROW_GATE_SKIP, CG, C2)
    gate_skip = stage[:CG, :C2]
    gate_coarse = flat[ROW_GATE_COARSE : ROW_GATE_COARSE + CG, :]
    lane = lanes(C3)

    def columns(at, channels):
        value = jnp.zeros((channels, 128), F32)
        for k in range(CLS):
            piece = tail[at + k * channels : at + (k + 1) * channels, :]
            value = jnp.where(lane[:channels] == k, piece, value)
        return value

    fine_cols = columns(T_HEAD_FINE, C2)
    coarse_cols = columns(T_HEAD_COARSE, C3)
    head_t[...] = fine_cols[:, :16].astype(BF)
    head[...] = fine_cols.T[:16, :].astype(BF)
    rows = jnp.concatenate(
        [
            jnp.concatenate([gate_skip, gate_coarse], axis=1),
            jnp.concatenate([jnp.zeros((16, C2), F32), coarse_cols.T[:16, :]], axis=1),
        ],
        axis=0,
    )
    gate[...] = rows.astype(BF)
    gate_t[...] = rows.T.astype(BF)
    gains[...] = tail[T_GAINS : T_GAINS + 416, :]
    shifts[...] = tail[T_SHIFTS : T_SHIFTS + 416, :]
    for index in range(11, 17):
        leave(index)


def prepare(z, meta, flat, tail):
    outs = [
        (((z.Z + 2) * C1, 9 * z.ZP), BF),
        ((192, 9 * C1), BF),
        ((192, 9 * C2), BF),
        ((128, 27 * C2), BF),
        ((192, 9 * 192), BF),
        ((192, 9 * C2), BF),
        ((96, 9 * C2), BF),
        ((192, 9 * C2), BF),
        ((128, 36 * C3), BF),
        ((192, 27 * C2), BF),
        ((192, 9 * C2), BF),
        ((48, 192), BF),
        ((192, 48), BF),
        ((16, C2), BF),
        ((C2, 16), BF),
        ((416, 128), F32),
        ((416, 128), F32),
    ]
    names = (
        "big", "second", "third", "coarse", "merge", "final", "b_second", "b_third", "b_coarse",
        "b_merge", "b_final", "gate", "gate_t", "head", "head_t", "gains", "shifts",
    )
    out = kernel_call(
        lambda *refs: prep_body(z, *refs), meta, [flat, tail], outs,
        [pltpu.VMEM((27 * C3, 128), F32), pltpu.VMEM((27 * C2, 128), F32)], far_outs=True,
    )
    return dict(zip(names, out))


def layer_gain(gains, layer):
    return gains[NORM_AT[layer] : NORM_AT[layer] + WIDTHS[layer], :]


def send_planes(z, meta, h_refs, source, count, planes):
    if z.two:
        start = jnp.where(meta[0] == 0, planes - count, 0)
        for j in range(count):
            h_refs[0][j] = source(start + j).astype(BF)
    else:
        for j in range(count):
            h_refs[0][j] = source(j).astype(BF)
            h_refs[1][j] = source(planes - count + j).astype(BF)


UNROLL = CHUNK


def flow(z, build, consume, ratio, fetch=(), leave=None):
    run(build(0, 0, 0))

    def body(t, carry):
        need(t, *fetch)
        for r in range(UNROLL):
            zp = UNROLL * t + r
            interleave(consume(zp, r % 2), build(zp + 1, (r + 1) % 2, None), ratio)
        if leave:
            leave(t)
        return carry

    lax.fori_loop(0, z.Z // UNROLL, body, 0)
    interleave(consume(z.Z, 0), build(z.Z + 1, 1, 1), ratio)
    run(consume(z.Z + 1, 1))


def scatter(zp, weight, window, width, parts, nb, finish):
    part_one, part_two = parts
    at = zp - 2 if isinstance(zp, int) else jnp.maximum(zp - 2, 0)
    for n in range(nb // 2):
        result = dot(weight[...], window[:, 256 * n : 256 * (n + 1)])
        for k in (2 * n, 2 * n + 1):
            piece = result[:, cols(k - 2 * n)]
            finish(at, k, part_one[:, cols(k)] + piece[2 * width :])
            part_one[:, cols(k)] = part_two[:, cols(k)] + piece[width : 2 * width]
            part_two[:, cols(k)] = piece[:width]
        yield


def add_sums(zp, st_ref, channels, first, second):
    first, second = fold_sums(first), fold_sums(second)
    if not isinstance(zp, int):
        first, second = jnp.where(zp >= 2, first, 0.0), jnp.where(zp >= 2, second, 0.0)
    st_ref[:channels, :] += first
    st_ref[channels : 2 * channels, :] += second


def convolve(z, weight, p_ref, parts, rows, channels, y_ref, st_ref, build, leave=None, ratio=3):
    st_ref[...] = jnp.zeros(st_ref.shape, F32)
    for part in parts:
        part[...] = jnp.zeros(part.shape, F32)

    def consume(zp, slot):
        values = []

        def finish(at, k, value):
            y_ref[at, :, cols(k)] = value
            values.append(value)

        window = p_ref.at[slot * rows : (slot + 1) * rows, :]
        yield from scatter(zp, weight, window, channels, parts, z.nb, finish)
        add_sums(zp, st_ref, channels, values, [v * v for v in values])

    flow(z, build, consume, ratio, leave=leave)


def mine_body(z, meta, images, labels, out, rows):
    for i in range(z.lz):
        rows[i * z.ly : (i + 1) * z.ly, :] = jnp.concatenate(
            [images[0, i], labels[0, i].astype(F32)], axis=1
        )
    value = rows[...].astype(BF)
    for i in range(out.shape[0]):
        out[i] = value


def first_body(z, meta, recv, big, y_ref, st_ref, p_ref, lab_ref, wide, rows):
    wide[...] = recv[...].astype(F32)
    rows[...] = jnp.zeros(rows.shape, F32)
    per = z.lz * z.ly
    for hh in range(z.H):
        for yy in range(z.ly):
            for zz in range(z.lz):
                rows[pl.ds((hh * z.ly + yy) * z.DP + 2 + zz, z.D, stride=z.lz), :] = wide[
                    pl.ds(hh * per + zz * z.ly + yy, z.D, stride=z.H * per), :
                ]
    lane = lanes(z.ZP)
    start = pl.multiple_of(meta[0] * z.Z // 8 * 8, 8)

    def source(y):
        if z.Z % 8 == 0:
            return rows[pl.ds(pl.multiple_of(y * z.DP + start, 8), z.ZP), :]
        block = rows[pl.ds(pl.multiple_of(y * z.DP + start, 8), z.ZP + 8), :]
        return jnp.where(lax.rem(meta[0], 2) == 0, block[: z.ZP], block[4 : z.ZP + 4])

    blocks = []
    hits = [jnp.zeros((1, 128), F32) for unused in range(CLS)]
    for k in range(z.nb):
        one, two = source(k), source(k + z.nb)
        blocks.append(jnp.where(lane < 64, one, roll(two, 64)))
        label = jnp.where(lane < 64, roll(one, 64), two)[2 : 2 + z.Z]
        for i in range(z.Z):
            lab_ref[i, :, cols(k)] = jnp.broadcast_to(label[i : i + 1], (8, 128))
        for c in range(CLS):
            hits[c] = hits[c] + jnp.sum(
                jnp.where(label == float(c), 1.0, 0.0), axis=0, keepdims=True
            )
    place_windows(p_ref, (0,), z.ZP, 0, blocks, 64)
    y_ref[...] = dot(big[...], p_ref[...])
    st_ref[...] = jnp.zeros(st_ref.shape, F32)

    def step(i):
        values = [y_ref[ds(C1 + i * C1, C1), cols(k)] for k in range(z.nb)]
        st_ref[:C1, :] += fold_sums(values)
        st_ref[C1 : 2 * C1, :] += fold_sums([v * v for v in values])

    unrolled(z.Z, 4, step)
    row = lax.broadcasted_iota(jnp.int32, (8, 128), 0)
    counts = jnp.zeros((8, 128), F32)
    for c in range(CLS):
        counts = jnp.where(row == c, hits[c], counts)
    st_ref[2 * C1 : 2 * C1 + 8, :] = counts


def second_body(z, meta, y1, sa, sb, gains, shifts, weight, y_ref, st_ref, *rest):
    h_refs, p_ref, parts = rest[:-3], rest[-3], rest[-2:]
    unused, unused, factor, level = norm_coefs(
        sa[...] + sb[...], layer_gain(gains, 0), layer_gain(shifts, 0), C1, z.total
    )

    def build(zp, slot, edge):
        blocks = []
        for k in range(z.nb):
            value = y1[ds(zp * C1, C1), cols(k)] * factor + level
            value = value * sigmoid(value)
            blocks.append(value if edge is None else jnp.where(meta[1 + edge] > 0, value, 0.0))
            if k % 2:
                yield
        yield from window_steps(p_ref, (slot * 9 * C1,), C1, 0, blocks, 64)

    convolve(z, weight, p_ref, parts, 9 * C1, C2, y_ref, st_ref, build)
    send_planes(z, meta, h_refs, lambda i: y_ref[i], 1, z.Z)


def middle_body(z, layer, send, meta, y_in, lo, hi, sa, sb, gains, shifts, weight, y_ref, st_ref, *rest):
    h_refs, p_ref, parts = rest[:-3], rest[-3], rest[-2:]
    unused, unused, factor, level = norm_coefs(
        sa[...] + sb[...], layer_gain(gains, layer), layer_gain(shifts, layer), C2, z.total
    )

    def build(zp, slot, edge):
        if edge is None:
            get = lambda k: y_in[zp - 1, :, cols(k)]
        else:
            get = lambda k: (lo, hi)[edge][0, :, cols(k)].astype(F32)
        blocks = []
        for k in range(z.nb):
            value = get(k) * factor + level
            value = value * sigmoid(value)
            blocks.append(value if edge is None else jnp.where(meta[1 + edge] > 0, value, 0.0))
            if k % 2:
                yield
        yield from window_steps(p_ref, (slot * 9 * C2,), C2, 0, blocks, 64)

    convolve(z, weight, p_ref, parts, 9 * C2, C2, y_ref, st_ref, build)
    send_planes(z, meta, h_refs, lambda i: y_ref[i], send, z.Z)


def pool_matrix(entries):
    row = lax.broadcasted_iota(jnp.int32, (256, 128), 0)
    col = lax.broadcasted_iota(jnp.int32, (256, 128), 1)
    same = (col // 32) == 2 * (lax.rem(row, 128) // 64) + row // 128
    return jnp.where(same, entries(lax.rem(row, 64), lax.rem(col, 32)), 0.0).astype(BF)


def mean_entries(fine, coarse):
    return jnp.where(fine // 2 == coarse, 0.125, 0.0)


def lift_entries(fine, coarse):
    near = fine // 2
    other = jnp.clip(jnp.where(lax.rem(fine, 2) == 0, near - 1, near + 1), 0, 31)
    return jnp.where(coarse == near, 0.75, 0.0) + jnp.where(coarse == other, 0.25, 0.0)


def coarse_body(z, meta, y3, lo, hi, sa, sb, gains, shifts, weight, skip, pooled, y_ref, st_ref, *rest):
    h_refs, p_ref = rest[:-1], rest[-1]
    unused, unused, factor, level = norm_coefs(
        sa[...] + sb[...], layer_gain(gains, 2), layer_gain(shifts, 2), C2, z.total
    )
    matrix = pool_matrix(mean_entries)

    def plane(jp, gets, valid, skip_at):
        sums = []
        for i in range(z.half):
            parts = []
            for index, get in enumerate(gets):
                for k in (2 * i, 2 * i + 1):
                    value = get(k) * factor + level
                    value = value * sigmoid(value)
                    if valid is not None:
                        value = jnp.where(valid > 0, value, 0.0)
                    if skip_at[index] is not None:
                        skip[skip_at[index], :, cols(k)] = value.astype(BF)
                    parts.append(value)
            sums.append(fold_sums(parts))
        blocks = []
        for kc in range(z.nbc):
            pair = jnp.concatenate([sums[kc], sums[kc + z.nbc]], axis=1)
            blocks.append(split_dot(pair, matrix))
        for kc in range(z.nbc):
            pooled[jp, :, cols(kc)] = blocks[kc].astype(BF)
        place_windows(p_ref, (jp * (9 * C2),), C2, 0, blocks, 32)

    plane(0, [lambda k: lo[0, :, cols(k)].astype(F32), lambda k: lo[1, :, cols(k)].astype(F32)],
          meta[1], (None, 0))
    plane(z.Zc + 1, [lambda k: hi[0, :, cols(k)].astype(F32), lambda k: hi[1, :, cols(k)].astype(F32)],
          meta[2], (z.Z + 1, None))

    def step(j):
        plane(j + 1, [lambda k: y3[2 * j, :, cols(k)], lambda k: y3[2 * j + 1, :, cols(k)]],
              None, (2 * j + 1, 2 * j + 2))

    unrolled(z.Zc, 4, step)
    st_ref[...] = jnp.zeros(st_ref.shape, F32)

    def conv(j):
        result = dot(weight[...], p_ref[ds(j * (9 * C2), 27 * C2), :])
        y_ref[j] = result
        values = [result[:, cols(k)] for k in range(z.nbc)]
        st_ref[:C3, :] += fold_sums(values)
        st_ref[C3 : 2 * C3, :] += fold_sums([v * v for v in values])

    unrolled(z.Zc, 8, conv)
    send_planes(z, meta, h_refs, lambda i: y_ref[i], 1, z.Zc)


def merge_body(z, meta, yc, lo, hi, sa, sb, gains, shifts, tail, skip, gate, weight,
               lifted_out, pre_out, logit_out, y_ref, st_ref, *rest):
    h_refs = rest[:-10]
    p_ref, t_ref, act, mixed, part_one, part_two, lifted, pre_ref, logit_ref, sems = rest[-10:]
    unused, unused, factor, level = norm_coefs(
        sa[...] + sb[...], layer_gain(gains, 3), layer_gain(shifts, 3), C3, z.total // 8
    )
    matrix = pool_matrix(lift_entries).astype(F32).T.astype(BF)
    n = z.half

    def coarse_act(get):
        out = []
        for k in range(z.nbc):
            value = get(k) * factor + level
            out.append((value * sigmoid(value)).astype(BF))
        return out

    for k, value in enumerate(coarse_act(lambda k: lo[0, :, cols(k)].astype(F32))):
        act[0, :, cols(k)] = value
    for k, value in enumerate(coarse_act(lambda k: hi[0, :, cols(k)].astype(F32))):
        act[z.Zc + 1, :, cols(k)] = value

    def own(j, carry):
        for k, value in enumerate(coarse_act(lambda k: yc[j, :, cols(k)])):
            act[j + 1, :, cols(k)] = value
        return carry

    lax.fori_loop(0, z.Zc, own, 0)

    @pl.when(meta[1] == 0)
    def low_edge():
        act[0] = act[1]

    @pl.when(meta[2] == 0)
    def high_edge():
        act[z.Zc + 1] = act[z.Zc]

    def spread(jp, slot):
        rows = [None] * n
        for k in range(z.nbc):
            both = dot(act[jp, :, cols(k)], matrix)
            rows[k], rows[k + z.nbc] = both[:, :128], both[:, 128:]
        lane = lanes(C3)
        first, last = rows[0], rows[n - 1]
        before = jnp.where(lane < 64, first, roll(last, 64))
        after = jnp.where(lane < 64, roll(first, 64), last)
        extended = [before] + rows + [after]
        for i in range(n):
            t_ref[slot, :, cols(2 * i)] = 0.25 * extended[i] + 0.75 * extended[i + 1]
            t_ref[slot, :, cols(2 * i + 1)] = 0.75 * extended[i + 1] + 0.25 * extended[i + 2]
            if i % 2:
                yield

    run(spread(0, 0))
    bias = tail[T_GATE_BIAS : T_GATE_BIAS + CG, :]
    score = tail[T_SCORE : T_SCORE + CG, :]
    score_bias = tail[T_SCORE_BIAS : T_SCORE_BIAS + 1, :]

    def build(zp, slot, edge):
        turn = zp % 2 if isinstance(zp, int) else 1 - (slot + 1) % 2
        wa, wb = (0.75, 0.25) if turn == 0 else (0.25, 0.75)
        old = (zp // 2) % 2 if isinstance(zp, int) else lax.rem(zp // 2, 2)
        new = 1 - old
        if turn == 0:
            yield from spread(zp // 2 + 1, new)
        valid = None if edge is None else meta[1 + edge]
        base, row = slot * 9 * 192, slot * 192
        mixed[row : row + C2, :] = skip[zp]
        wide = []
        for k in range(z.nb):
            value = (wa * t_ref[old, :, cols(k)] + wb * t_ref[new, :, cols(k)]).astype(BF)
            mixed[row + C2 : row + 192, cols(k)] = value
            lifted[zp, :, cols(k)] = value
            value = value.astype(F32)
            wide.append(value if valid is None else jnp.where(valid > 0, value, 0.0))
            if k % 2:
                yield
        gated = []
        for n in range(z.half):
            rows = dot(gate[...], mixed[row : row + 192, 256 * n : 256 * (n + 1)])
            logit_ref[zp, :, 256 * n : 256 * (n + 1)] = rows[CG:]
            for k in (2 * n, 2 * n + 1):
                pre = rows[:CG, cols(k - 2 * n)] + bias
                pre_ref[zp, :, cols(k)] = pre
                inner = pre * sigmoid(pre)
                alpha = sigmoid(jnp.sum(score * inner, axis=0, keepdims=True) + score_bias)
                if valid is not None:
                    alpha = jnp.where(valid > 0, alpha, 0.0)
                gated.append(mixed[row : row + C2, cols(k)].astype(F32) * alpha)
            yield
        yield from window_steps(p_ref, (base,), 192, C2, wide, 64)
        yield from window_steps(p_ref, (base,), 192, 0, gated, 64)

    pairs = ((lifted, lifted_out), (pre_ref, pre_out), (logit_ref, logit_out))

    def leaving(t):
        span = pl.ds(4 * t + 1, 4)
        return [
            pltpu.make_async_copy(a.at[span], b.at[span], sems.at[n, t]) for n, (a, b) in enumerate(pairs)
        ]

    def leave(t):
        for copy in leaving(t):
            copy.start()

    convolve(z, weight, p_ref, (part_one, part_two), 9 * 192, C2, y_ref, st_ref, build, leave, ratio=5)
    send_planes(z, meta, h_refs, lambda i: y_ref[i], 1, z.Z)
    for t in range(z.Z // 4):
        for copy in leaving(t):
            copy.wait()


def heads_body(z, meta, yf, sa, sb, ca, cb, lab, logit_ref, gains, shifts, tail, head, head_t,
               d_ref, bs_ref, small, gc_ref, *rest):
    h_refs, acts = rest[:-1], rest[-1]
    mean, inv, factor, level = norm_coefs(
        sa[...] + sb[...], layer_gain(gains, 5), layer_gain(shifts, 5), C2, z.total
    )
    counts = jnp.sum(ca[2 * C1 :] + cb[2 * C1 :], axis=1, keepdims=True)
    row = lax.broadcasted_iota(jnp.int32, (8, 1), 0)
    everything = jnp.sum(jnp.where(row < CLS, counts, 0.0), axis=0, keepdims=True)
    class_weight = jnp.where(row < CLS, 2.0 * everything / (3.0 * counts + everything), 0.0)
    weight_total = jnp.sum(counts * class_weight, axis=0, keepdims=True)
    scaled = class_weight / weight_total
    scaled = jnp.concatenate([scaled, jnp.zeros((8, 1), F32)], axis=0)
    rows16 = lax.broadcasted_iota(jnp.int32, (16, 128), 0)
    pad13 = jnp.zeros((13, 128), F32)
    bias_fine = jnp.concatenate([tail[T_BIAS_FINE : T_BIAS_FINE + 3, :], pad13], axis=0)
    bias_coarse = jnp.concatenate([tail[T_BIAS_COARSE : T_BIAS_COARSE + 3, :], pad13], axis=0)
    bs_ref[...] = jnp.zeros(bs_ref.shape, F32)
    small[...] = jnp.zeros(small.shape, F32)

    def logit_grad(logits, label, times):
        logits = jnp.where(rows16 < CLS, logits, -1e30)
        top = jnp.max(logits, axis=0, keepdims=True)
        terms = jnp.where(rows16 < CLS, jnp.exp(logits - top), 0.0)
        soft = terms / jnp.sum(terms, axis=0, keepdims=True)
        onehot = jnp.where(rows16.astype(F32) == label, 1.0, 0.0)
        weight = jnp.sum(scaled * onehot, axis=0, keepdims=True)
        return ((soft - onehot) * (weight * times)).astype(BF)

    def step(i, slot):
        act = acts.at[slot * C2 : (slot + 1) * C2, :]
        for k in range(z.nb):
            value = yf[i, :, cols(k)] * factor + level
            act[:, cols(k)] = (value * sigmoid(value)).astype(BF)
        logits = dot(head[...], act[...])
        fine, bias_sum, coarse_sum = [], [], []
        for k in range(z.nb):
            label = lab[i, 0:1, cols(k)]
            grad = logit_grad(logits[:, cols(k)] + bias_fine, label, 1.0)
            fine.append(grad)
            bias_sum.append(grad.astype(F32))
            grad = logit_grad(logit_ref[i + 1, :, cols(k)] + bias_coarse, label, 0.5)
            gc_ref[i, :, cols(k)] = grad
            coarse_sum.append(grad.astype(F32))
        fine = jnp.concatenate(fine, axis=1)
        small[:C2, :16] += dot_nt(act[...], fine)
        small[C2 : C2 + 16, :] += fold_sums(bias_sum)
        small[C2 + 16 : C2 + 32, :] += fold_sums(coarse_sum)
        back = dot(head_t[...], fine)
        parts, cross = [], []
        for k in range(z.nb):
            y = yf[i, :, cols(k)]
            pre = y * factor + level
            sig = sigmoid(pre)
            grad = back[:, cols(k)] * (sig * (1.0 + pre * (1.0 - sig)))
            d_ref[i, :, cols(k)] = grad
            parts.append(grad)
            cross.append(grad * ((y - mean) * inv))
        bs_ref[:C2, :] += fold_sums(parts)
        bs_ref[C2:, :] += fold_sums(cross)

    def four(t, carry):
        for r in range(4):
            step(4 * t + r, r)
        return carry

    lax.fori_loop(0, z.Z // 4, four, 0)
    send_planes(z, meta, h_refs, lambda i: d_ref[i], 1, z.Z)


def dy_builder(z, meta, layer, count, refs, p_ref, q_ref, share):
    d, d_lo, d_hi, y, y_lo, y_hi, sums, back, gains, shifts = refs
    channels = WIDTHS[layer]
    mean, inv, factor, unused = norm_coefs(
        sums, layer_gain(gains, layer), layer_gain(shifts, layer), channels, count
    )
    slope, level = grad_coefs(back, mean, inv, factor, channels, count)

    def build(zp, bases, edge):
        get_d, get_y = (lambda k: d[zp - 1, :, cols(k)]), (lambda k: y[zp - 1, :, cols(k)])
        if edge is not None:
            get_d = lambda k: (d_lo, d_hi)[edge][0, :, cols(k)].astype(F32)
            get_y = lambda k: (y_lo[y_lo.shape[0] - 1, :, cols(k)], y_hi[0, :, cols(k)])[edge].astype(F32)
        out = []
        for k in range(z.nb):
            value = factor * get_d(k) - slope * get_y(k) + level
            out.append(value if edge is None else jnp.where(meta[1 + edge] > 0, value, 0.0))
            if k % 2:
                yield
        yield from window_steps(p_ref, bases, channels, 0, out, 64)
        yield from share_steps(q_ref, bases, share, meta[3], out, 64)

    def build_or_edge(zp, bases, last):
        out = []
        own = jnp.minimum(zp - 1, z.Z - 1)
        for k in range(z.nb):
            near_d = jnp.where(last, d_hi[0, :, cols(k)].astype(F32), d[own, :, cols(k)])
            near_y = jnp.where(last, y_hi[0, :, cols(k)].astype(F32), y[own, :, cols(k)])
            value = factor * near_d - slope * near_y + level
            out.append(jnp.where(jnp.logical_and(last, meta[2] == 0), 0.0, value))
            if k % 2:
                yield
        yield from window_steps(p_ref, bases, channels, 0, out, 64)
        yield from share_steps(q_ref, bases, share, meta[3], out, 64)

    build.or_edge = build_or_edge
    return build


def back_body(z, layer, below, y_base, share, meta, d, d_lo, d_hi, y, y_lo, y_hi, sa, sb, ba, bb,
              yb, ua, ub, gains, shifts, weight, *rest):
    d_ref, bs_ref, dk_out = rest[:3]
    h_refs, (p_ref, q_ref, x_ref, dk_ref), parts = rest[3:-6], rest[-6:-2], rest[-2:]
    make = dy_builder(z, meta, layer, z.total,
                       (d, d_lo, d_hi, y, y_lo, y_hi, sa[...] + sb[...], ba[...] + bb[...], gains, shifts),
                      p_ref, q_ref, share)
    width = WIDTHS[below]
    mean, inv, factor, level = norm_coefs(
        ua[...] + ub[...], layer_gain(gains, below), layer_gain(shifts, below), width, z.total
    )
    edge = jnp.zeros((2 * width, z.V), BF)
    x_ref[: 2 * width, :] = edge
    x_ref[(z.Z + 2) * width :, :] = edge
    bs_ref[...] = jnp.zeros(bs_ref.shape, F32)
    rows = 9 * WIDTHS[layer]
    part = rows // share
    dk_ref[...] = jnp.zeros(dk_ref.shape, F32)

    for part_ref in parts:
        part_ref[...] = jnp.zeros(part_ref.shape, F32)

    def build(zp, slot, edge):
        return make(zp, (slot * rows,), edge)

    def consume(zp, slot):
        if not isinstance(zp, int):
            for k in range(z.nb):
                pre = yb[zp + y_base, :, cols(k)] * factor + level
                x_ref[ds((zp + 2) * width, width), cols(k)] = (pre * sigmoid(pre)).astype(BF)
        sums, cross = [], []

        def finish(at, k, value):
            y_value = yb[at + y_base, :, cols(k)]
            pre = y_value * factor + level
            sig = sigmoid(pre)
            grad = value * (sig * (1.0 + pre * (1.0 - sig)))
            d_ref[at, :, cols(k)] = grad
            sums.append(grad)
            cross.append(grad * ((y_value - mean) * inv))

        yield from scatter(zp, weight, p_ref.at[slot * rows : (slot + 1) * rows, :], width, parts, z.nb, finish)
        add_sums(zp, bs_ref, width, sums, cross)
        if share == 1:
            window = p_ref[slot * rows : (slot + 1) * rows, :]
        else:
            window = q_ref[slot * part : (slot + 1) * part, :]
        dk_ref[...] += dot_nt(window, x_ref[ds(zp * width, 3 * width), :])

    flow(z, build, consume, 3, (d, y, yb))
    if width == C2:
        pack_wide(dk_out, dk_ref, part)
    else:
        dk_out[:, : 3 * width] = dk_ref[...]
    if h_refs:
        send_planes(z, meta, h_refs, lambda i: d_ref[i], 1, z.Z)


def merge_back_body(z, share, meta, d, d_lo, d_hi, y, y_lo, y_hi, sa, sb, ba, bb, skip, lifted, pre_ref, gc_ref,
                    yc, yc_lo, yc_hi, ua, ub, gains, shifts, tail, weight, gate_t,
                    gskip_out, gcoarse, bs_ref, dk_out, small, *rest):
    h_refs, (p_ref, q_ref, eg, x_ref, acc, dk_ref, gskip, sems) = rest[:-8], rest[-8:]
    build = dy_builder(z, meta, 4, z.total,
                       (d, d_lo, d_hi, y, y_lo, y_hi, sa[...] + sb[...], ba[...] + bb[...], gains, shifts),
                       p_ref, q_ref, share)
    score = tail[T_SCORE : T_SCORE + CG, :]
    score_bias = tail[T_SCORE_BIAS : T_SCORE_BIAS + 1, :]
    small[...] = jnp.zeros(small.shape, F32)
    dk_ref[...] = jnp.zeros(dk_ref.shape, F32)
    acc[...] = jnp.zeros(acc.shape, F32)
    n = z.half
    lane = lanes(C3)
    rows = 9 * C2
    part = 27 * C2 // share

    def plane(i, r4):
        start = r4 * rows
        turn = (r4 % 2) * 256
        side = (r4 % 2) * 48
        eg[side + CG : side + 48, :] = gc_ref[i]
        x_ref[turn + C2 : turn + 192, :] = lifted[i + 1]
        x_ref[turn + 192 : turn + 256, :] = skip[i + 1]
        wide, e_sum, s_sum, r_sum = [], [], [], []
        for q in range(z.half):
            span = slice(256 * q, 256 * (q + 1))
            result = dot(weight[...], p_ref[start : start + 3 * rows, span])
            alphas = []
            for k in (2 * q, 2 * q + 1):
                piece = result[:C2, cols(k - 2 * q)]
                pre = pre_ref[i + 1, :, cols(k)]
                sig = sigmoid(pre)
                inner = pre * sig
                alpha = sigmoid(jnp.sum(score * inner, axis=0, keepdims=True) + score_bias)
                near = skip[i + 1, :, cols(k)].astype(F32)
                grad = jnp.sum(piece * near, axis=0, keepdims=True)
                grad = grad * alpha * (1.0 - alpha)
                e = (score * grad * (sig * (1.0 + pre * (1.0 - sig)))).astype(BF)
                eg[side : side + CG, cols(k)] = e
                x_ref[turn : turn + C2, cols(k)] = (near * alpha).astype(BF)
                alphas.append(alpha)
                e_sum.append(e.astype(F32))
                s_sum.append(grad * inner)
                r_sum.append(grad)
            extra = dot(gate_t[...], eg[side : side + 48, span])
            for k in (2 * q, 2 * q + 1):
                at = cols(k - 2 * q)
                gskip[i, :, cols(k)] = result[:C2, at] * alphas[k - 2 * q] + extra[:C2, at]
                wide.append(result[C2:, at] + extra[C2:, at])
            yield
        small[192:224, :] += fold_sums(e_sum)
        small[224:256, :] += fold_sums(s_sum)
        small[256:257, :] += fold_sums(r_sum)
        low = [
            0.75 * (wide[2 * m] + wide[2 * m + 1])
            + (0.25 * wide[2 * m + 2] if m < n - 1 else 0.0)
            + (0.25 * wide[2 * m - 1] if m > 0 else 0.0)
            for m in range(n)
        ]
        before, after = 0.25 * wide[0], 0.25 * wide[-1]
        low[0] = low[0] + jnp.where(lane < 64, before, roll(after, 64))
        low[n - 1] = low[n - 1] + jnp.where(lane < 64, roll(before, 64), after)
        j, r = i // 2, r4 % 2
        for m in range(n):
            acc[j + 1, :, cols(m)] += 0.75 * low[m]
            acc[j + 2 * r, :, cols(m)] += 0.25 * low[m]
        yield
        if share == 1:
            window = p_ref[start : start + 3 * rows, :]
        else:
            window = q_ref[start // share : start // share + part, :]
        tall = jnp.concatenate([window, eg[side : side + 48, :]], axis=0)
        dk_ref[...] += dot_nt(tall, x_ref[turn : turn + 256, :])

    need(0, d, y)
    for zp in range(3):
        run(build(zp, (zp * rows,), 0 if zp == 0 else None))

    def four(t, carry):
        need(t, skip, lifted, pre_ref, gc_ref)
        for r in range(4):
            if r == 2:

                @pl.when(t + 1 < z.Z // 4)
                def fetch():
                    need(t + 1, d, y)

            at = (r + 3) % 4
            bases = (at * rows, (at + 4) * rows) if at < 2 else (at * rows,)
            zp = 4 * t + r + 3
            if r < 2:
                steps = build(zp, bases, None)
            else:
                steps = build.or_edge(zp, bases, zp == z.Z + 1)
            interleave(plane(4 * t + r, r), steps, 2)
        leaving(t).start()
        return carry

    def leaving(t):
        span = pl.ds(4 * t, 4)
        return pltpu.make_async_copy(gskip.at[span], gskip_out.at[span], sems.at[t])

    lax.fori_loop(0, z.Z // 4, four, 0)
    pack_wide(dk_out, dk_ref[:part, :192], part)
    tall = dk_ref[part:, :].T
    small[:C2, :48] = tall[192:]
    small[C2:192, :48] = tall[C2:192]

    matrix = pool_matrix(lift_entries)

    def shrink(jp, carry):
        for k in range(z.nbc):
            pair = jnp.concatenate([acc[jp, :, cols(k)], acc[jp, :, cols(k + z.nbc)]], axis=1)
            gcoarse[jp, :, cols(k)] = split_dot(pair, matrix)
        return carry

    lax.fori_loop(0, z.Zc + 2, shrink, 0)

    @pl.when(meta[1] == 0)
    def low_edge():
        gcoarse[1] += gcoarse[0]
        gcoarse[0] = jnp.zeros((C3, z.Vc), F32)

    @pl.when(meta[2] == 0)
    def high_edge():
        gcoarse[z.Zc] += gcoarse[z.Zc + 1]
        gcoarse[z.Zc + 1] = jnp.zeros((C3, z.Vc), F32)

    mean, inv, factor, level = norm_coefs(
        ua[...] + ub[...], layer_gain(gains, 3), layer_gain(shifts, 3), C3, z.total // 8
    )
    bs_ref[...] = jnp.zeros(bs_ref.shape, F32)

    def sums(jp, get):
        for k in range(z.nbc):
            value = get(k)
            pre = value * factor + level
            sig = sigmoid(pre)
            grad = gcoarse[jp, :, cols(k)] * (sig * (1.0 + pre * (1.0 - sig)))
            bs_ref[:C3, :] += grad
            bs_ref[C3:, :] += grad * ((value - mean) * inv)

    sums(0, lambda k: yc_lo[0, :, cols(k)].astype(F32))
    sums(z.Zc + 1, lambda k: yc_hi[0, :, cols(k)].astype(F32))

    def own(j, carry):
        sums(j + 1, lambda k: yc[j, :, cols(k)])
        return carry

    lax.fori_loop(0, z.Zc, own, 0)
    if z.two:
        start = jnp.where(meta[0] == 0, z.Zc, 0)
        for m in range(2):
            h_refs[0][m] = gcoarse[start + m].astype(BF)
    else:
        for m in range(2):
            h_refs[0][m] = gcoarse[m].astype(BF)
            h_refs[1][m] = gcoarse[z.Zc + m].astype(BF)
    for t in range(z.Z // 4):
        leaving(t).wait()


def coarse_back_body(z, share, meta, gcoarse, g_lo, g_hi, yc, yc_lo, yc_hi, sa, sb, ba, bb, pooled, gskip, y3,
                     ua, ub, gains, shifts, weight, d_ref, bs_ref, dk_out, *rest):
    h_refs, (p_ref, x_ref, dk_ref) = rest[:-3], rest[-3:]
    mean, inv, factor, level = norm_coefs(
        sa[...] + sb[...], layer_gain(gains, 3), layer_gain(shifts, 3), C3, z.total // 8
    )
    slope, offset = grad_coefs(ba[...] + bb[...], mean, inv, factor, C3, z.total // 8)

    def plane(jp, get_y, extra, valid):
        out = []
        for k in range(z.nbc):
            value = get_y(k)
            pre = value * factor + level
            sig = sigmoid(pre)
            grad = gcoarse[jp, :, cols(k)] + extra(k)
            grad = grad * (sig * (1.0 + pre * (1.0 - sig)))
            grad = factor * grad - slope * value + offset
            out.append(grad if valid is None else jnp.where(valid > 0, grad, 0.0))
        place_windows(p_ref, (jp * (9 * C3),), C3, 0, out, 32)

    def from_lo(m):
        return lambda k: jnp.where(meta[1] > 0, g_lo[m, :, cols(k)].astype(F32), 0.0)

    def from_hi(m):
        return lambda k: jnp.where(meta[2] > 0, g_hi[m, :, cols(k)].astype(F32), 0.0)

    plane(0, lambda k: yc_lo[0, :, cols(k)].astype(F32), from_lo(0), meta[1])
    plane(1, lambda k: yc[0, :, cols(k)], from_lo(1), None)

    def inner(j):
        plane(j + 2, lambda k: yc[j + 1, :, cols(k)], lambda k: 0.0, None)

    if z.Zc > 2:
        unrolled(z.Zc - 2, 3, inner)
    plane(z.Zc, lambda k: yc[z.Zc - 1, :, cols(k)], from_hi(0), None)
    plane(z.Zc + 1, lambda k: yc_hi[0, :, cols(k)].astype(F32), from_hi(1), meta[2])

    edge = jnp.zeros((2 * C2, z.Vc), BF)
    x_ref[: 2 * C2, :] = edge
    x_ref[(z.Zc + 2) * C2 :, :] = edge

    for j in range(z.Zc):
        x_ref[(j + 2) * C2 : (j + 3) * C2, :] = pooled[j + 1]
    mean, inv, factor, level = norm_coefs(
        ua[...] + ub[...], layer_gain(gains, 2), layer_gain(shifts, 2), C2, z.total
    )
    matrix = pool_matrix(mean_entries).astype(F32).T.astype(BF)
    bs_ref[...] = jnp.zeros(bs_ref.shape, F32)
    rows = 9 * C3

    def step(s, carry):
        need(s, y3, gskip)
        result = dot(weight[...], p_ref[ds(s * (2 * rows), 4 * rows), :])
        parts, cross = [], []
        for r in range(2):
            low = result[r * C2 : (r + 1) * C2]
            spread = [None] * z.half
            for k in range(z.nbc):
                both = split_dot(low[:, cols(k)], matrix)
                spread[k], spread[k + z.nbc] = both[:, :128], both[:, 128:]
            for q in range(2):
                at = 4 * s + 2 * r + q
                for k in range(z.nb):
                    value = y3[at, :, cols(k)]
                    pre = value * factor + level
                    sig = sigmoid(pre)
                    grad = spread[k // 2] + gskip[at, :, cols(k)]
                    grad = grad * (sig * (1.0 + pre * (1.0 - sig)))
                    d_ref[at, :, cols(k)] = grad
                    parts.append(grad)
                    cross.append(grad * ((value - mean) * inv))
        bs_ref[:C2, :] += fold_sums(parts)
        bs_ref[C2:, :] += fold_sums(cross)
        return carry

    lax.fori_loop(0, z.Zc // 2, step, 0)
    part = rows // share

    def kernel_grad(zp):
        window = p_ref[ds(zp * rows + meta[3] * part, part), :]
        return dot_nt(window, x_ref[zp * C2 : (zp + 3) * C2, :])

    dk_ref[...] = fold_sums([kernel_grad(zp) for zp in range(z.Zc + 2)])
    pack_wide(dk_out, dk_ref, part)
    send_planes(z, meta, h_refs, lambda i: d_ref[i], 1, z.Z)


def first_back_body(z, meta, d, y1, p_img, sa, sb, ba, bb, gains, shifts, dk_ref, low):
    mean, inv, factor, unused = norm_coefs(
        sa[...] + sb[...], layer_gain(gains, 0), layer_gain(shifts, 0), C1, z.total
    )
    slope, level = grad_coefs(ba[...] + bb[...], mean, inv, factor, C1, z.total)

    def step(i):
        for k in range(z.nb):
            value = factor * d[i, :, cols(k)] - slope * y1[i + 1, :, cols(k)] + level
            low[ds(i * C1, C1), cols(k)] = value.astype(BF)

    unrolled(z.Z, 4, step)
    table = dot_nt(p_img[...], low[...])
    shape = (9 * z.ZP, z.Z * C1)
    gap = lax.rem(lax.broadcasted_iota(jnp.int32, shape, 0), z.ZP) - (
        lax.broadcasted_iota(jnp.int32, shape, 1) // C1
    )
    dk_ref[...] = jnp.zeros(dk_ref.shape, F32)
    for a in range(3):
        kept = jnp.where(gap == a + 1, table, 0.0)
        folded = fold_sums([kept[:, cols(k)] for k in range(z.Z * C1 // 128)])
        folded = folded + roll(folded, 64)
        folded = folded + roll(folded, 32)
        for t in range(9):
            dk_ref[9 * a + t : 9 * a + t + 1, :] = jnp.sum(
                folded[t * z.ZP : (t + 1) * z.ZP], axis=0, keepdims=True
            )


def gather_body(z, meta, *refs):
    ins, (out, norm), (stage, stage_b, flat, column, quarters, full, full_b) = refs[:-9], refs[-9:-7], refs[-7:]
    shared, ins = ins[: z.share], ins[z.share :]
    pairs = [(ins[2 * j], ins[2 * j + 1]) for j in range(len(ins) // 2)]
    (first, second, small_head, small_gate, b_first, b_second, b_third, b_coarse, b_merge, b_final) = pairs
    for k in range(z.share):
        quarters[jnp.bitwise_xor(meta[3], k)] = shared[k][...].astype(F32)

    def unpack(start, count, taps_out):
        part = count // z.share
        width = part if taps_out == C3 else taps_out // z.share
        for k in range(z.share):
            unpack_wide(full, full_b, k, width, taps_out, quarters.at[k], start, part)

    def total(pair):
        return pair[0][...] + pair[1][...]

    def pack(row, taps_out, width):
        count = taps_out * width // 128
        fold = 128 // width
        lane = lanes(count)
        value = stage[pl.ds(0, count, stride=fold), :]
        for j in range(1, fold):
            part = roll(stage[pl.ds(j, count, stride=fold), :], j * width)
            value = jnp.where(lane < j * width, value, part)
        flat[row : row + count, :] = value

    flat[ROWS : ROWS + 8, :] = jnp.zeros((8, 128), F32)
    stage[0:5, :32] = jnp.zeros((5, 32), F32)
    stage[5:32, :32] = (first[0][...] + first[1][...])[:27, :32]
    pack(ROW_FIRST, 32, 32)
    wide_at = 27 * C2 // z.share * 3 // 2
    for row, out_c, in_c, source in (
        (ROW_SECOND, C2, C1, second),
        (ROW_THIRD, C2, C2, 2 * wide_at),
        (ROW_COARSE, C3, C2, wide_at + wide_at // 3),
        (ROW_FINAL, C2, C2, wide_at),
    ):
        count = 9 * out_c
        if source is second:
            full[:count, :] = total(second)
        else:
            unpack(source, count, out_c)
        for t in range(9):
            span = slice(t * out_c, (t + 1) * out_c)
            for a in range(3):
                at = (9 * a + 8 - t) * out_c
                if a * in_c < 128:
                    stage[at : at + out_c, :in_c] = full[span, a * in_c : (a + 1) * in_c]
                else:
                    stage[at : at + out_c, :in_c] = full_b[span, :in_c]
        pack(row, 27 * out_c, in_c)
    unpack(0, 27 * C2, C2)
    for t in range(27):
        at = (26 - t) * C2
        stage[at : at + C2, :] = full[t * C2 : (t + 1) * C2, :]
        stage_b[at : at + C2, :64] = full_b[t * C2 : (t + 1) * C2, :64]
    half = 27 * C2 // 2
    even, even_b = stage[pl.ds(0, half, stride=2), :], stage_b[pl.ds(0, half, stride=2), :]
    odd, odd_b = stage[pl.ds(1, half, stride=2), :], stage_b[pl.ds(1, half, stride=2), :]
    left = lanes(half) < 64
    odd = roll(odd, 64)
    flat[pl.ds(ROW_MERGE, half, stride=3), :] = even
    flat[pl.ds(ROW_MERGE + 1, half, stride=3), :] = jnp.where(left, even_b, odd)
    flat[pl.ds(ROW_MERGE + 2, half, stride=3), :] = jnp.where(left, odd, roll(odd_b, 64))

    gate = total(small_gate)
    turned = gate[:192].T
    stage[:CG, :C2] = turned[:CG, :C2]
    pack(ROW_GATE_SKIP, CG, C2)
    flat[ROW_GATE_COARSE : ROW_GATE_COARSE + CG, :] = turned[:CG, C2:]
    heads = total(small_head)
    lane = lanes(C3)
    column[TAIL_LEN - 7 :, :] = jnp.zeros((2048 - TAIL_LEN + 7, 128), F32)
    column[T_GATE_BIAS : T_GATE_BIAS + CG, :] = gate[192:224]
    column[T_SCORE : T_SCORE + CG, :] = gate[224:256]
    column[T_SCORE_BIAS : T_SCORE_BIAS + 1, :] = gate[256:257]
    for k in range(CLS):
        at = T_HEAD_FINE + k * C2
        column[at : at + C2, :] = jnp.where(lane[:C2] == k, heads[:C2], 0.0)
        at = T_HEAD_COARSE + k * C3
        column[at : at + C3, :] = jnp.where(lane == CG + k, gate[C2:192], 0.0)
    column[T_BIAS_FINE : T_BIAS_FINE + 3, :] = heads[C2 : C2 + 3]
    column[T_BIAS_COARSE : T_BIAS_COARSE + 3, :] = heads[C2 + 16 : C2 + 19]
    for layer, pair in enumerate((b_first, b_second, b_third, b_coarse, b_merge, b_final)):
        sums = total(pair)
        width = WIDTHS[layer]
        at = T_GAINS + NORM_AT[layer]
        column[at : at + width, :] = sums[width : 2 * width]
        at = T_SHIFTS + NORM_AT[layer]
        column[at : at + width, :] = sums[:width]
    for k in range(16):
        flat[ROW_TAIL + k : ROW_TAIL + k + 1, :] = jnp.sum(
            column[k * 128 : (k + 1) * 128, :].T, axis=0, keepdims=True
        )
    chunk = ROWS // 21
    mask = lanes(chunk) < 96

    def finish(i, acc):
        base = pl.multiple_of(i * chunk, 8)
        block = roll(flat[pl.ds(base, chunk + 8), :], 96)
        out[pl.ds(base, chunk), :] = jnp.where(mask, block[1 : chunk + 1], block[2 : chunk + 2])
        return acc + fold_sums([block[8 * m : 8 * m + 8] * block[8 * m : 8 * m + 8] for m in range(chunk // 8)])

    acc = lax.fori_loop(0, 21, finish, jnp.zeros((8, 128), F32))
    sq = jnp.sum(jnp.sum(acc, axis=1, keepdims=True), axis=0, keepdims=True)
    norm[...] = jnp.broadcast_to(jnp.sqrt(sq), (8, 128))


def local(z, images, labels, weights, first_moment, second_moment):
    devices = z.D * z.H
    linear = lax.axis_index("depth") * z.H + lax.axis_index("height")
    position = lax.rem(linear, z.G)
    meta = jnp.stack(
        [position, (position > 0).astype(jnp.int32), (position < z.G - 1).astype(jnp.int32),
         lax.rem(linear // z.G, z.share)]
    ).astype(jnp.int32)

    call = functools.partial(kernel_call, room=12 if z.V <= 1024 else 18)

    def partner(value, step):
        return lax.ppermute(value, AXES, [(i, i ^ step) for i in range(devices)])

    def both(value):
        step = 1
        while step * 2 < z.G:
            value = value + partner(value, step)
            step *= 2
        return value, partner(value, step)

    def neighbours(sent):
        if z.two:
            got = partner(sent[0], 1)
            return got, got
        up = [(i, i + 1) for i in range(devices) if i % z.G != z.G - 1]
        return (
            lax.ppermute(sent[1], AXES, up),
            lax.ppermute(sent[0], AXES, [(j, i) for i, j in up]),
        )

    def shares(values):
        value = jnp.concatenate([one + two for one, two in values], axis=0).astype(BF)
        return [value] + [
            lax.ppermute(value, AXES, [(i, (i // z.G ^ k) * z.G + i % z.G) for i in range(devices)])
            for k in range(1, z.share)
        ]

    def sent(count, channels, lanes_):
        return [((count, channels, lanes_), BF)] * (1 if z.two else 2)

    V, Vc, Z, Zc = z.V, z.Vc, z.Z, z.Zc
    local_rows = z.lz * z.ly
    (mine,) = call(
        lambda *r: mine_body(z, *r), meta, [images, labels], [((devices, local_rows, 128), BF)],
        [pltpu.VMEM((local_rows, 128), F32)],
    )
    everyone = lax.all_to_all(
        mine, AXES, 0, 0
    ).reshape(devices * local_rows, 128)
    flat = jnp.pad(weights, (PAD, ROWS * 128 - PAD - weights.shape[0])).reshape(ROWS, 128)
    tail = jnp.broadcast_to(
        jnp.pad(weights[TAIL_AT:], (0, 1))[:, None], (TAIL_LEN + 1, 128)
    )
    w = prepare(z, meta, flat, tail)
    gains, shifts = w["gains"], w["shifts"]

    def fars(values, base=None):
        return [Far(value, base) for value in values]

    y1, st1, p_img, lab = call(
        lambda *r: first_body(z, *r), meta, [Far(everyone), Far(w["big"])],
        [(((Z + 2) * C1, V), F32), ((72, 128), F32), ((9 * z.ZP, V), BF), ((Z, 8, V), F32)],
        [pltpu.VMEM((devices * local_rows, 128), F32), pltpu.VMEM((z.PY * z.DP, 128), F32)],
    )
    st1 = both(st1)
    parts = [pltpu.VMEM((C2, V), F32), pltpu.VMEM((C2, V), F32)]
    y2, st2, *h2 = call(
        lambda *r: second_body(z, *r), meta, [y1, *st1, gains, shifts, w["second"]],
        [((Z, C2, V), F32), ((2 * C2, 128), F32)] + sent(1, C2, V),
        [pltpu.VMEM((2 * 9 * C1, V), BF), *parts],
    )
    st2, h2 = both(st2), neighbours(h2)
    wide_p = pltpu.VMEM((2 * 9 * C2, V), BF)
    share_p = pltpu.VMEM((2 * 9 * C2 // z.share, V), BF)
    y3, st3, *h3 = call(
        lambda *r: middle_body(z, 1, 2, *r), meta, [y2, *h2, *st2, gains, shifts, w["third"]],
        [((Z, C2, V), F32), ((2 * C2, 128), F32)] + sent(2, C2, V), [wide_p, *parts],
    )
    st3, h3 = both(st3), neighbours(h3)
    skip, pooled, yc, stc, *hc = call(
        lambda *r: coarse_body(z, *r), meta, [y3, *h3, *st3, gains, shifts, w["coarse"]],
        [((Z + 2, C2, V), BF), ((Zc + 2, C2, Vc), BF), ((Zc, C3, Vc), F32), ((2 * C3, 128), F32)]
        + sent(1, C3, Vc),
        [pltpu.VMEM(((Zc + 2) * 9 * C2, Vc), BF)],
    )
    stc, hc = both(stc), neighbours(hc)
    lifted, pre, logits, ym, stm, *hm = call(
        lambda *r: merge_body(z, *r), meta,
        [yc, *hc, *stc, gains, shifts, tail, skip, w["gate"], w["merge"]],
        [((Z + 2, C3, V), BF), ((Z + 2, CG, V), F32), ((Z + 2, 16, V), F32), ((Z, C2, V), F32),
         ((2 * C2, 128), F32)] + sent(1, C2, V),
        [pltpu.VMEM((2 * 9 * 192, V), BF), pltpu.VMEM((2, C3, V), F32), pltpu.VMEM((Zc + 2, C3, Vc), BF),
         pltpu.VMEM((384, V), BF), *parts, pltpu.VMEM((Z + 2, C3, V), BF), pltpu.VMEM((Z + 2, CG, V), F32),
         pltpu.VMEM((Z + 2, 16, V), F32), pltpu.SemaphoreType.DMA((3, Z // 4))],
        hbm_outs=(0, 1, 2),
    )
    stm, hm = both(stm), neighbours(hm)
    yf, stf, *hf = call(
        lambda *r: middle_body(z, 4, 1, *r), meta, [ym, *hm, *stm, gains, shifts, w["final"]],
        [((Z, C2, V), F32), ((2 * C2, 128), F32)] + sent(1, C2, V), [wide_p, *parts],
    )
    stf, hf = both(stf), neighbours(hf)
    counts = fars(st1)
    df, bf, small_head, gc, *hdf = call(
        lambda *r: heads_body(z, *r), meta,
        [yf, *stf, *counts, Far(lab), Far(logits), gains, shifts, tail, w["head"], w["head_t"]],
        [((Z, C2, V), F32), ((2 * C2, 128), F32), ((C2 + 32, 128), F32), ((Z, 16, V), BF)] + sent(1, C2, V),
        [pltpu.VMEM((4 * C2, V), BF)],
    )
    bf, hdf, small_head = both(bf), neighbours(hdf), both(small_head)
    x_wide = pltpu.VMEM(((Z + 4) * C2, V), BF)
    part_rows = 9 * C2 // z.share
    packed = 3 * part_rows // 2
    dk_wide = pltpu.VMEM((part_rows, 192), F32)
    dm, bm, kf, *hdm = call(
        lambda *r: back_body(z, 5, 4, 0, z.share, *r), meta,
        [df, *hdf, yf, *hf, *stf, *bf, ym, *fars(stm), gains, shifts, w["b_final"]],
        [((Z, C2, V), F32), ((2 * C2, 128), F32), ((packed, 128), F32)] + sent(1, C2, V),
        [wide_p, share_p, x_wide, dk_wide, *parts],
    )
    bm, hdm, kf = both(bm), neighbours(hdm), both(kf)
    gskip, gcoarse, bc, km, small_gate, *hg = call(
        lambda *r: merge_back_body(z, z.share, *r), meta,
        [dm, *hdm, ym, *fars(hm), *fars(stm), *bm, Far(skip, 1), Far(lifted, 1), Far(pre, 1), Far(gc, 0),
         Far(yc), *fars(hc), *fars(stc), gains, shifts, tail, w["b_merge"], w["gate_t"]],
        [((Z, C2, V), F32), ((Zc + 2, C3, Vc), F32), ((2 * C3, 128), F32), ((3 * packed, 128), F32),
         ((264, 128), F32)] + sent(2, C3, Vc),
        [pltpu.VMEM((6 * 9 * C2, V), BF), pltpu.VMEM((6 * 9 * C2 // z.share, V), BF), pltpu.VMEM((96, V), BF), pltpu.VMEM((512, V), BF),
         pltpu.VMEM((Zc + 2, C3, V // 2), F32), pltpu.VMEM((3 * part_rows + 48, 256), F32),
         pltpu.VMEM((Z, C2, V), F32), pltpu.SemaphoreType.DMA((Z // 4,))],
        hbm_outs=(0,),
    )
    bc, hg, km, small_gate = both(bc), neighbours(hg), both(km), both(small_gate)
    d3, b3, kc, *hd3 = call(
        lambda *r: coarse_back_body(z, z.share, *r), meta,
        [gcoarse, *hg, Far(yc), *fars(hc), *fars(stc), *bc, Far(pooled), Far(gskip, 0), Far(y3, 0), *fars(st3),
         gains, shifts, w["b_coarse"]],
        [((Z, C2, V), F32), ((2 * C2, 128), F32), ((2 * packed, 128), F32)] + sent(1, C2, V),
        [pltpu.VMEM(((Zc + 2) * 9 * C3, Vc), BF), pltpu.VMEM(((Zc + 4) * C2, Vc), BF),
         pltpu.VMEM((2 * part_rows, 192), F32)],
    )
    b3, hd3, kc = both(b3), neighbours(hd3), both(kc)
    d2, b2, k3, *hd2 = call(
        lambda *r: back_body(z, 2, 1, 0, z.share, *r), meta,
        [d3, *hd3, Far(y3, 0), *fars(h3), *fars(st3), *b3, Far(y2, 0), *fars(st2), gains, shifts, w["b_third"]],
        [((Z, C2, V), F32), ((2 * C2, 128), F32), ((packed, 128), F32)] + sent(1, C2, V),
        [wide_p, share_p, x_wide, dk_wide, *parts],
    )
    b2, hd2, shared = both(b2), neighbours(hd2), shares([km, kf, kc, both(k3)])
    y1_planes = y1.reshape(Z + 2, C1, V)
    d1, b1, k2 = call(
        lambda *r: back_body(z, 1, 0, 1, 1, *r), meta,
        [d2, *hd2, Far(y2, 0), *fars(h2), *fars(st2), *b2, Far(y1_planes, 1), *fars(st1), gains, shifts,
         w["b_second"], ],
        [((Z, C1, V), F32), ((2 * C1, 128), F32), ((9 * C2, 128), F32)],
        [wide_p, share_p, pltpu.VMEM(((Z + 4) * C1, V), BF), pltpu.VMEM((9 * C2, 3 * C1), F32), pltpu.VMEM((C1, V), F32), pltpu.VMEM((C1, V), F32)],
    )
    b1, k2 = both(b1), both(k2)
    (k1,) = call(
        lambda *r: first_back_body(z, *r), meta,
        [d1, Far(y1_planes), Far(p_img), *fars(st1), *b1, gains, shifts, *[Held(part) for part in shared]],
        [((32, 128), F32)], [pltpu.VMEM((Z * C1, V), BF)],
    )
    k1 = both(k1)
    pieces = (k1, k2, small_head, small_gate, b1, b2, b3, bc, bm, bf)
    grad, norm = call(
        lambda *r: gather_body(z, *r), meta,
        fars(shared) + [Far(part) for pair in pieces for part in pair],
        [((ROWS, 128), F32), ((8, 128), F32)],
        [pltpu.VMEM((27 * C3, 128), F32), pltpu.VMEM((27 * C2, 128), F32),
         pltpu.VMEM((ROWS + 8, 128), F32), pltpu.VMEM((2048, 128), F32)]
        + [pltpu.VMEM((z.share, 7 * packed, 128), F32)] + [pltpu.VMEM((27 * C2, 128), F32)] * 2,
    )
    gradient = grad.reshape(ROWS * 128)[: weights.shape[0]]
    grad_norm = norm[0, 0]
    clipped = gradient * jnp.minimum(1.0, CLIP_NORM / (grad_norm + 1e-06))
    moment_one = BETA_ONE * first_moment + (1.0 - BETA_ONE) * clipped
    moment_two = BETA_TWO * second_moment + (1.0 - BETA_TWO) * clipped * clipped
    corrected_one = moment_one / (1.0 - BETA_ONE**STEP)
    corrected_two = moment_two / (1.0 - BETA_TWO**STEP)
    updated = weights - LEARN_RATE * (
        corrected_one / (jnp.sqrt(corrected_two) + ADAM_EPS) + DECAY_RATE * weights
    )
    return (grad_norm, moment_one, moment_two, updated, updated.astype(BF))


def solution(mesh):
    depth, height = mesh.shape["depth"], mesh.shape["height"]

    def step(images, labels, weights, first_moment, second_moment):
        z = Sizes(depth, height, images.shape[1] // depth, images.shape[2] // height, images.shape[3])
        placed = (P(None, "depth", "height", None), P(None, "depth", "height", None), P(), P(), P())
        return jax.shard_map(
            lambda *arrays: local(z, *arrays), mesh=mesh, in_specs=placed,
            out_specs=(P(), P(), P(), P(), P()), check_vma=False,
        )(images, labels, weights, first_moment, second_moment)

    return step
```

```python
import functools
import math

import jax
import jax.numpy as jnp
from jax import lax
from jax.experimental import pallas as pl
from jax.experimental.pallas import tpu as pltpu
from jax.sharding import PartitionSpec as P

C1 = 32
C2 = 64
C3 = 128
CG = 32
CLS = 3
STEP = 10

EPS_NORM = 1e-05
CLIP_NORM = 0.005
LEARN_RATE = 0.02
BETA_ONE = 0.9
BETA_TWO = 0.999
ADAM_EPS = 1e-08
DECAY_RATE = 0.01

BF = jnp.bfloat16
F32 = jnp.float32
AXES = ("depth", "height")
WIDTHS = (C1, C2, C2, C3, C2, C2)
NORM_AT = (0, 32, 96, 160, 288, 352)
VOXELS = 18432
PAD = 160
ROWS = 6552
ROW_FIRST, ROW_SECOND, ROW_THIRD, ROW_COARSE = 0, 8, 440, 1304
ROW_MERGE, ROW_FINAL, ROW_GATE_SKIP, ROW_GATE_COARSE, ROW_TAIL = 3032, 5624, 6488, 6504, 6536
TAIL_AT = 836448
TAIL_LEN = 1479
T_GATE_BIAS, T_SCORE, T_SCORE_BIAS, T_HEAD_FINE, T_BIAS_FINE = 0, 32, 64, 65, 257
T_HEAD_COARSE, T_BIAS_COARSE, T_GAINS, T_SHIFTS = 260, 644, 647, 1063


class Sizes:
    def __init__(self, mesh_depth, mesh_height, local_z, local_y, width):
        self.D, self.H, self.lz, self.ly = mesh_depth, mesh_height, local_z, local_y
        self.planes = mesh_depth * local_z
        self.PY = mesh_height * local_y
        self.V = self.PY * width
        self.nb = self.V // 128
        self.half = self.nb // 2
        self.nbc = self.nb // 4
        self.Vc = self.V // 4
        self.total = self.planes * self.V
        self.G = 2
        while (self.planes // self.G + 2) * self.V > VOXELS:
            self.G *= 2
        self.Z = self.planes // self.G
        self.Zc = self.Z // 2
        self.ZP = -(-(self.Z + 4) // 16) * 16
        self.DP = self.planes - self.Z + self.ZP + 8
        self.two = self.G == 2
        self.share = 4 if mesh_depth * mesh_height // self.G % 4 == 0 else 1


def dot(left, right):
    return lax.dot_general(left, right, (((1,), (0,)), ((), ())), preferred_element_type=F32)


def dot_nt(left, right):
    return lax.dot_general(left, right, (((1,), (1,)), ((), ())), preferred_element_type=F32)


def ds(start, size, multiple=16):
    return pl.ds(start if isinstance(start, int) else pl.multiple_of(start, multiple), size)


def cols(k):
    return slice(k * 128, (k + 1) * 128)


def lanes(channels):
    return lax.broadcasted_iota(jnp.int32, (channels, 128), 1)


def sigmoid(value):
    return 0.5 * jnp.tanh(0.5 * value) + 0.5


def roll(value, steps):
    return pltpu.roll(value, steps % 128, axis=1)


def split_dot(value, matrix):
    high = value.astype(BF)
    low = (value - high.astype(F32)).astype(BF)
    return dot(high, matrix) + dot(low, matrix)


def norm_coefs(sums, gain, shift, channels, count):
    mean = jnp.sum(sums[:channels], axis=1, keepdims=True) / count
    square = jnp.sum(sums[channels : 2 * channels], axis=1, keepdims=True) / count
    inv = lax.rsqrt(square - mean * mean + EPS_NORM)
    full = (channels, 128)
    mean, inv = jnp.broadcast_to(mean, full), jnp.broadcast_to(inv, full)
    factor = inv * gain
    return mean, inv, factor, shift - mean * factor


def grad_coefs(sums, mean, inv, factor, channels, count):
    total = jnp.sum(sums[:channels], axis=1, keepdims=True) / count
    cross = jnp.sum(sums[channels : 2 * channels], axis=1, keepdims=True) / count
    slope = factor * cross * inv
    return slope, slope * mean - factor * total


def run(steps):
    for unused in steps:
        pass


def interleave(first, second, ratio):
    first, second = iter(first), iter(second)
    done = object()
    one = two = None
    while one is not done or two is not done:
        one = next(first, done)
        for unused in range(ratio):
            two = next(second, done)


def place_windows(p_ref, bases, rows, offset, blocks, seg):
    run(window_steps(p_ref, bases, rows, offset, blocks, seg))


def window_steps(p_ref, bases, rows, offset, blocks, seg):
    channels, count = blocks[0].shape[0], len(blocks)
    lane = lanes(channels)
    inner = lane & (seg - 1)
    zero = jnp.zeros((channels, 128), BF)
    blocks = [v.astype(BF) for v in blocks]
    for c in range(3):
        if c == 0:
            low = [jnp.where(inner == 0, zero, roll(v, 1)) for v in blocks]
        elif c == 1:
            low = blocks
        else:
            low = [jnp.where(inner == seg - 1, zero, roll(v, 127)) for v in blocks]
        before = jnp.where(lane < seg, zero, roll(low[-1], seg))
        after = jnp.where(lane >= 128 - seg, zero, roll(low[0], 128 - seg))
        extended = [before] + low + [after]
        for b in range(3):
            for k in range(count):
                for base in bases:
                    p_ref[ds(base + (3 * b + c) * rows + offset, channels), cols(k)] = extended[k + b]
            yield


def pack_wide(out, wide, rows):
    half = rows // 2
    out[:rows, :] = wide[:, :128]
    low = jnp.concatenate([wide[:half, 128:], wide[half:, 128:]], axis=1)
    out[rows : rows + half, :] = low


def unpack_wide(full, full_b, share, width, taps_out, packed, start, rows):
    half = rows // 2
    for m in range(0, rows, 8):
        at = m // width * taps_out + share * width + m % width
        full[at : at + 8, :] = packed[start + m : start + m + 8, :]
        low = start + rows + m % half
        low = packed[low : low + 8, :]
        full_b[at : at + 8, :] = low if m < half else roll(low, 64)


def share_steps(q_ref, bases, share, index, blocks, seg):
    if share == 1:
        return
    width = blocks[0].shape[0] // share
    picked = []
    for value in blocks:
        value = value.astype(BF)
        part = value[:width]
        for k in range(1, share):
            part = jnp.where(index == k, value[k * width : (k + 1) * width], part)
        picked.append(part)
    yield from window_steps(q_ref, tuple(base // share for base in bases), width, 0, picked, seg)


def unrolled(count, times, body):
    while count % times:
        times -= 1

    def step(t, carry):
        for r in range(times):
            body(times * t + r)
        return carry

    if count == times:
        for i in range(count):
            body(i)
    else:
        lax.fori_loop(0, count // times, step, 0)


def fold_sums(values):
    total = values[0]
    for value in values[1:]:
        total = total + value
    return total


CHUNK = 4


class Far:
    def __init__(self, array, base=None):
        self.array, self.base = array, base


class Held:
    def __init__(self, array):
        self.array = array


class Copied:
    def __init__(self, source, target, sems, base):
        self.target, self.copies = target, []
        self.source, self.sems, self.base = source, sems, base

    def copy(self, c):
        if self.base is None:
            return pltpu.make_async_copy(self.source, self.target, self.sems.at[0])
        span = pl.ds(self.base + c * CHUNK, CHUNK)
        return pltpu.make_async_copy(self.source.at[span], self.target.at[span], self.sems.at[c])

    def __getitem__(self, at):
        return self.target[at]

    @property
    def shape(self):
        return self.target.shape


def need(c, *refs):
    for ref in refs:
        if isinstance(ref, Copied):
            ref.copy(c).wait()


def kernel_call(body, meta, ins, outs, scratch=(), far_outs=False, hbm_outs=(), room=12, us=10):
    def size(shape, dtype):
        return math.prod(shape[:-1]) * (-(-shape[-1] // 128) * 128) * jnp.dtype(dtype).itemsize

    scratch = list(scratch)
    own = len(scratch)
    hbm = range(len(outs)) if far_outs else hbm_outs
    held = [isinstance(a, Held) for a in ins]
    far = [a if isinstance(a, (Far, Held)) else None for a in ins]
    arrays = [
        a if f is None else pltpu.with_memory_space_constraint(a.array, pltpu.HBM) for a, f in zip(ins, far)
    ]
    far = [None if h else f for f, h in zip(far, held)]
    chunks = []
    for a in far:
        if a is not None:
            count = 1 if a.base is None else (a.array.shape[0] - 2 * a.base) // CHUNK
            chunks.append(count)
            scratch += [pltpu.VMEM(a.array.shape, a.array.dtype), pltpu.SemaphoreType.DMA((count,))]
    if far_outs:
        scratch += [pltpu.VMEM(*o) for o in outs] + [pltpu.SemaphoreType.DMA((len(outs),))]

    def wrapped(meta_ref, *refs):
        in_refs, out_refs = refs[: len(ins)], refs[len(ins) : len(ins) + len(outs)]
        own_refs, extra = refs[len(ins) + len(outs) :][:own], list(refs[len(ins) + len(outs) + own :])
        given, whole = [], []
        for a, h, ref in zip(far, held, in_refs):
            if h:
                continue
            if a is None:
                given.append(ref)
                continue
            target, sems = extra.pop(0), extra.pop(0)
            copied = Copied(ref, target, sems, a.base)
            if a.base is None:
                copied.copy(0).start()
                whole.append(copied)
                given.append(target)
            else:
                given.append(copied)
        for copied in given:
            if isinstance(copied, Copied):
                for c in range(copied.sems.shape[0]):
                    copied.copy(c).start()
        for copied in whole:
            copied.copy(0).wait()
        if not far_outs:
            body(meta_ref, *given, *out_refs, *own_refs)
            return
        buffers, sems = extra[:-1], extra[-1]
        copies = [
            pltpu.make_async_copy(source, target, sems.at[index])
            for index, (source, target) in enumerate(zip(buffers, out_refs))
        ]
        body(lambda index: copies[index].start(), meta_ref, *given, *buffers, *own_refs)
        for copy in copies:
            copy.wait()

    vmem = sum(size(x.shape, x.dtype) for x in scratch if getattr(x, "memory_space", None) == pltpu.VMEM) + (room << 20)
    return pl.pallas_call(
        wrapped,
        out_shape=[pltpu.HBM(*o) if k in hbm else jax.ShapeDtypeStruct(*o) for k, o in enumerate(outs)],
        in_specs=[pl.BlockSpec(memory_space=pltpu.SMEM)]
        + [pl.BlockSpec(memory_space=pltpu.HBM if a or h else pltpu.VMEM) for a, h in zip(far, held)],
        out_specs=[pl.BlockSpec(memory_space=pltpu.HBM if k in hbm else pltpu.VMEM) for k in range(len(outs))],
        scratch_shapes=scratch,
        compiler_params=pltpu.CompilerParams(vmem_limit_bytes=min(vmem, 63 << 20)),
        cost_estimate=pl.CostEstimate(flops=us * 1000000000, bytes_accessed=1000, transcendentals=0),
    )(meta, *arrays)


def prep_body(z, leave, meta, flat, tail, big, second, third, coarse, merge, final, b_second, b_third,
              b_coarse, b_merge, b_final, gate, gate_t, head, head_t, gains, shifts, stage, stage_b):
    def unroll(row, taps_out, width):
        count = taps_out * width // 128
        if width == 192:
            rows = count // 3
            one, two, three = (flat[pl.ds(row + j, rows, stride=3), :] for j in range(3))
            left = lanes(rows) < 64
            turned = roll(three, 64)
            stage[pl.ds(0, rows, stride=2), :] = one
            stage_b[pl.ds(0, rows, stride=2), :] = two
            stage[pl.ds(1, rows, stride=2), :] = jnp.where(left, roll(two, 64), turned)
            stage_b[pl.ds(1, rows, stride=2), :] = turned
        else:
            pack = 128 // width
            block = flat[row : row + count, :]
            for j in range(pack):
                stage[pl.ds(j, count, stride=pack), :] = roll(block, -j * width) if j else block

    def staged(at, count, width):
        if width <= 128:
            return stage[at : at + count, :width]
        return jnp.concatenate([stage[at : at + count, :], stage_b[at : at + count, : width - 128]], axis=1)

    def forward(out_c, in_c):
        return [
            jnp.concatenate(
                [staged((9 * a + t) * out_c, out_c, in_c) for t in range(9)],
                axis=1,
            )
            for a in range(3)
        ]

    def backward_plane(out_c, in_c, a):
        at = 26 - 9 * a
        return jnp.concatenate(
            [staged((at - t) * out_c, out_c, in_c) for t in range(9)], axis=0
        ).T

    def backward(out_c, in_c):
        return jnp.concatenate(
            [staged((26 - t) * out_c, out_c, in_c) for t in range(27)], axis=0
        ).T

    def double(ref, full, copies, step):
        rows, width = full.shape
        for r in range(copies):
            parts = []
            if r:
                parts.append(jnp.zeros((rows, r * step), F32))
            parts.append(full)
            if r < copies - 1:
                parts.append(jnp.zeros((rows, (copies - 1 - r) * step), F32))
            ref[r * rows : (r + 1) * rows, :] = jnp.concatenate(parts, axis=1).astype(BF)

    block = flat[0:8, :]
    for j in range(4):
        stage[pl.ds(j, 8, stride=4), :] = roll(block, -j * 32) if j else block
    taps = stage[0:32, :32].T.astype(BF)
    tall = jnp.concatenate([taps] * (z.Z + 2), axis=0)
    shape = ((z.Z + 2) * C1, 9 * z.ZP)
    source = lax.broadcasted_iota(jnp.int32, (32, 9 * z.ZP), 0)
    target = lax.broadcasted_iota(jnp.int32, (32, 9 * z.ZP), 1) // z.ZP
    gap = lax.rem(lax.broadcasted_iota(jnp.int32, shape, 1), z.ZP) - (
        lax.broadcasted_iota(jnp.int32, shape, 0) // C1
    )
    total = jnp.zeros(shape, F32)
    for a in range(3):
        spread = dot(tall, jnp.where(source == target + 5 + 9 * a, 1.0, 0.0).astype(BF))
        total = total + jnp.where(gap == a, spread, 0.0)
    big[...] = total.astype(BF)
    leave(0)

    for index, row, ref, b_ref, width in (
        (1, ROW_SECOND, second, b_second, C1),
        (2, ROW_THIRD, third, b_third, C2),
        (5, ROW_FINAL, final, b_final, C2),
    ):
        unroll(row, 27 * C2, width)
        ref[...] = jnp.concatenate(forward(C2, width), axis=0).astype(BF)
        for a in range(3):
            b_ref[a * width : (a + 1) * width, :] = backward_plane(C2, width, a).astype(BF)
        leave(index)
        leave(10 if index == 5 else index + 5)
    unroll(ROW_COARSE, 27 * C3, C2)
    coarse[...] = jnp.concatenate(forward(C3, C2), axis=1).astype(BF)
    double(b_coarse, backward(C3, C2), 2, 9 * C3)
    leave(3)
    leave(8)
    unroll(ROW_MERGE, 27 * C2, C2 + C3)
    merge[...] = jnp.concatenate(forward(C2, C2 + C3), axis=0).astype(BF)
    b_merge[...] = backward(C2, C2 + C3).astype(BF)
    leave(4)
    leave(9)

    unroll(ROW_GATE_SKIP, CG, C2)
    gate_skip = stage[:CG, :C2]
    gate_coarse = flat[ROW_GATE_COARSE : ROW_GATE_COARSE + CG, :]
    lane = lanes(C3)

    def columns(at, channels):
        value = jnp.zeros((channels, 128), F32)
        for k in range(CLS):
            piece = tail[at + k * channels : at + (k + 1) * channels, :]
            value = jnp.where(lane[:channels] == k, piece, value)
        return value

    fine_cols = columns(T_HEAD_FINE, C2)
    coarse_cols = columns(T_HEAD_COARSE, C3)
    head_t[...] = fine_cols[:, :16].astype(BF)
    head[...] = fine_cols.T[:16, :].astype(BF)
    rows = jnp.concatenate(
        [
            jnp.concatenate([gate_skip, gate_coarse], axis=1),
            jnp.concatenate([jnp.zeros((16, C2), F32), coarse_cols.T[:16, :]], axis=1),
        ],
        axis=0,
    )
    gate[...] = rows.astype(BF)
    gate_t[...] = rows.T.astype(BF)
    gains[...] = tail[T_GAINS : T_GAINS + 416, :]
    shifts[...] = tail[T_SHIFTS : T_SHIFTS + 416, :]
    for index in range(11, 17):
        leave(index)


def prepare(z, meta, flat, tail):
    outs = [
        (((z.Z + 2) * C1, 9 * z.ZP), BF),
        ((192, 9 * C1), BF),
        ((192, 9 * C2), BF),
        ((128, 27 * C2), BF),
        ((192, 9 * 192), BF),
        ((192, 9 * C2), BF),
        ((96, 9 * C2), BF),
        ((192, 9 * C2), BF),
        ((128, 36 * C3), BF),
        ((192, 27 * C2), BF),
        ((192, 9 * C2), BF),
        ((48, 192), BF),
        ((192, 48), BF),
        ((16, C2), BF),
        ((C2, 16), BF),
        ((416, 128), F32),
        ((416, 128), F32),
    ]
    names = (
        "big", "second", "third", "coarse", "merge", "final", "b_second", "b_third", "b_coarse",
        "b_merge", "b_final", "gate", "gate_t", "head", "head_t", "gains", "shifts",
    )
    out = kernel_call(
        lambda *refs: prep_body(z, *refs), meta, [flat, tail], outs,
        [pltpu.VMEM((27 * C3, 128), F32), pltpu.VMEM((27 * C2, 128), F32)], far_outs=True,
    )
    return dict(zip(names, out))


def layer_gain(gains, layer):
    return gains[NORM_AT[layer] : NORM_AT[layer] + WIDTHS[layer], :]


def send_planes(z, meta, h_refs, source, count, planes):
    if z.two:
        start = jnp.where(meta[0] == 0, planes - count, 0)
        for j in range(count):
            h_refs[0][j] = source(start + j).astype(BF)
    else:
        for j in range(count):
            h_refs[0][j] = source(j).astype(BF)
            h_refs[1][j] = source(planes - count + j).astype(BF)


UNROLL = CHUNK


def flow(z, build, consume, ratio, fetch=(), leave=None):
    run(build(0, 0, 0))

    def body(t, carry):
        need(t, *fetch)
        for r in range(UNROLL):
            zp = UNROLL * t + r
            interleave(consume(zp, r % 2), build(zp + 1, (r + 1) % 2, None), ratio)
        if leave:
            leave(t)
        return carry

    lax.fori_loop(0, z.Z // UNROLL, body, 0)
    interleave(consume(z.Z, 0), build(z.Z + 1, 1, 1), ratio)
    run(consume(z.Z + 1, 1))


def scatter(zp, weight, window, width, parts, nb, finish):
    part_one, part_two = parts
    at = zp - 2 if isinstance(zp, int) else jnp.maximum(zp - 2, 0)
    for n in range(nb // 2):
        result = dot(weight[...], window[:, 256 * n : 256 * (n + 1)])
        for k in (2 * n, 2 * n + 1):
            piece = result[:, cols(k - 2 * n)]
            finish(at, k, part_one[:, cols(k)] + piece[2 * width :])
            part_one[:, cols(k)] = part_two[:, cols(k)] + piece[width : 2 * width]
            part_two[:, cols(k)] = piece[:width]
        yield


def add_sums(zp, st_ref, channels, first, second):
    first, second = fold_sums(first), fold_sums(second)
    if not isinstance(zp, int):
        first, second = jnp.where(zp >= 2, first, 0.0), jnp.where(zp >= 2, second, 0.0)
    st_ref[:channels, :] += first
    st_ref[channels : 2 * channels, :] += second


def convolve(z, weight, p_ref, parts, rows, channels, y_ref, st_ref, build, leave=None, ratio=3):
    st_ref[...] = jnp.zeros(st_ref.shape, F32)
    for part in parts:
        part[...] = jnp.zeros(part.shape, F32)

    def consume(zp, slot):
        values = []

        def finish(at, k, value):
            y_ref[at, :, cols(k)] = value
            values.append(value)

        window = p_ref.at[slot * rows : (slot + 1) * rows, :]
        yield from scatter(zp, weight, window, channels, parts, z.nb, finish)
        add_sums(zp, st_ref, channels, values, [v * v for v in values])

    flow(z, build, consume, ratio, leave=leave)


def mine_body(z, meta, images, labels, out, rows):
    for i in range(z.lz):
        rows[i * z.ly : (i + 1) * z.ly, :] = jnp.concatenate(
            [images[0, i], labels[0, i].astype(F32)], axis=1
        )
    value = rows[...].astype(BF)
    for i in range(out.shape[0]):
        out[i] = value


def first_body(z, meta, recv, big, y_ref, st_ref, p_ref, lab_ref, wide, rows):
    wide[...] = recv[...].astype(F32)
    rows[...] = jnp.zeros(rows.shape, F32)
    per = z.lz * z.ly
    for hh in range(z.H):
        for yy in range(z.ly):
            for zz in range(z.lz):
                rows[pl.ds((hh * z.ly + yy) * z.DP + 2 + zz, z.D, stride=z.lz), :] = wide[
                    pl.ds(hh * per + zz * z.ly + yy, z.D, stride=z.H * per), :
                ]
    lane = lanes(z.ZP)
    start = pl.multiple_of(meta[0] * z.Z // 8 * 8, 8)

    def source(y):
        if z.Z % 8 == 0:
            return rows[pl.ds(pl.multiple_of(y * z.DP + start, 8), z.ZP), :]
        block = rows[pl.ds(pl.multiple_of(y * z.DP + start, 8), z.ZP + 8), :]
        return jnp.where(lax.rem(meta[0], 2) == 0, block[: z.ZP], block[4 : z.ZP + 4])

    blocks = []
    hits = [jnp.zeros((1, 128), F32) for unused in range(CLS)]
    for k in range(z.nb):
        one, two = source(k), source(k + z.nb)
        blocks.append(jnp.where(lane < 64, one, roll(two, 64)))
        label = jnp.where(lane < 64, roll(one, 64), two)[2 : 2 + z.Z]
        for i in range(z.Z):
            lab_ref[i, :, cols(k)] = jnp.broadcast_to(label[i : i + 1], (8, 128))
        for c in range(CLS):
            hits[c] = hits[c] + jnp.sum(
                jnp.where(label == float(c), 1.0, 0.0), axis=0, keepdims=True
            )
    place_windows(p_ref, (0,), z.ZP, 0, blocks, 64)
    y_ref[...] = dot(big[...], p_ref[...])
    st_ref[...] = jnp.zeros(st_ref.shape, F32)

    def step(i):
        values = [y_ref[ds(C1 + i * C1, C1), cols(k)] for k in range(z.nb)]
        st_ref[:C1, :] += fold_sums(values)
        st_ref[C1 : 2 * C1, :] += fold_sums([v * v for v in values])

    unrolled(z.Z, 4, step)
    row = lax.broadcasted_iota(jnp.int32, (8, 128), 0)
    counts = jnp.zeros((8, 128), F32)
    for c in range(CLS):
        counts = jnp.where(row == c, hits[c], counts)
    st_ref[2 * C1 : 2 * C1 + 8, :] = counts


def second_body(z, meta, y1, sa, sb, gains, shifts, weight, y_ref, st_ref, *rest):
    h_refs, p_ref, parts = rest[:-3], rest[-3], rest[-2:]
    unused, unused, factor, level = norm_coefs(
        sa[...] + sb[...], layer_gain(gains, 0), layer_gain(shifts, 0), C1, z.total
    )

    def build(zp, slot, edge):
        blocks = []
        for k in range(z.nb):
            value = y1[ds(zp * C1, C1), cols(k)] * factor + level
            value = value * sigmoid(value)
            blocks.append(value if edge is None else jnp.where(meta[1 + edge] > 0, value, 0.0))
            if k % 2:
                yield
        yield from window_steps(p_ref, (slot * 9 * C1,), C1, 0, blocks, 64)

    convolve(z, weight, p_ref, parts, 9 * C1, C2, y_ref, st_ref, build)
    send_planes(z, meta, h_refs, lambda i: y_ref[i], 1, z.Z)


def middle_body(z, layer, send, meta, y_in, lo, hi, sa, sb, gains, shifts, weight, y_ref, st_ref, *rest):
    h_refs, p_ref, parts = rest[:-3], rest[-3], rest[-2:]
    unused, unused, factor, level = norm_coefs(
        sa[...] + sb[...], layer_gain(gains, layer), layer_gain(shifts, layer), C2, z.total
    )

    def build(zp, slot, edge):
        if edge is None:
            get = lambda k: y_in[zp - 1, :, cols(k)]
        else:
            get = lambda k: (lo, hi)[edge][0, :, cols(k)].astype(F32)
        blocks = []
        for k in range(z.nb):
            value = get(k) * factor + level
            value = value * sigmoid(value)
            blocks.append(value if edge is None else jnp.where(meta[1 + edge] > 0, value, 0.0))
            if k % 2:
                yield
        yield from window_steps(p_ref, (slot * 9 * C2,), C2, 0, blocks, 64)

    convolve(z, weight, p_ref, parts, 9 * C2, C2, y_ref, st_ref, build)
    send_planes(z, meta, h_refs, lambda i: y_ref[i], send, z.Z)


def pool_matrix(entries):
    row = lax.broadcasted_iota(jnp.int32, (256, 128), 0)
    col = lax.broadcasted_iota(jnp.int32, (256, 128), 1)
    same = (col // 32) == 2 * (lax.rem(row, 128) // 64) + row // 128
    return jnp.where(same, entries(lax.rem(row, 64), lax.rem(col, 32)), 0.0).astype(BF)


def mean_entries(fine, coarse):
    return jnp.where(fine // 2 == coarse, 0.125, 0.0)


def lift_entries(fine, coarse):
    near = fine // 2
    other = jnp.clip(jnp.where(lax.rem(fine, 2) == 0, near - 1, near + 1), 0, 31)
    return jnp.where(coarse == near, 0.75, 0.0) + jnp.where(coarse == other, 0.25, 0.0)


def coarse_body(z, meta, y3, lo, hi, sa, sb, gains, shifts, weight, skip, pooled, y_ref, st_ref, *rest):
    h_refs, p_ref = rest[:-1], rest[-1]
    unused, unused, factor, level = norm_coefs(
        sa[...] + sb[...], layer_gain(gains, 2), layer_gain(shifts, 2), C2, z.total
    )
    matrix = pool_matrix(mean_entries)

    def plane(jp, gets, valid, skip_at):
        sums = []
        for i in range(z.half):
            parts = []
            for index, get in enumerate(gets):
                for k in (2 * i, 2 * i + 1):
                    value = get(k) * factor + level
                    value = value * sigmoid(value)
                    if valid is not None:
                        value = jnp.where(valid > 0, value, 0.0)
                    if skip_at[index] is not None:
                        skip[skip_at[index], :, cols(k)] = value.astype(BF)
                    parts.append(value)
            sums.append(fold_sums(parts))
        blocks = []
        for kc in range(z.nbc):
            pair = jnp.concatenate([sums[kc], sums[kc + z.nbc]], axis=1)
            blocks.append(split_dot(pair, matrix))
        for kc in range(z.nbc):
            pooled[jp, :, cols(kc)] = blocks[kc].astype(BF)
        place_windows(p_ref, (jp * (9 * C2),), C2, 0, blocks, 32)

    plane(0, [lambda k: lo[0, :, cols(k)].astype(F32), lambda k: lo[1, :, cols(k)].astype(F32)],
          meta[1], (None, 0))
    plane(z.Zc + 1, [lambda k: hi[0, :, cols(k)].astype(F32), lambda k: hi[1, :, cols(k)].astype(F32)],
          meta[2], (z.Z + 1, None))

    def step(j):
        plane(j + 1, [lambda k: y3[2 * j, :, cols(k)], lambda k: y3[2 * j + 1, :, cols(k)]],
              None, (2 * j + 1, 2 * j + 2))

    unrolled(z.Zc, 4, step)
    st_ref[...] = jnp.zeros(st_ref.shape, F32)

    def conv(j):
        result = dot(weight[...], p_ref[ds(j * (9 * C2), 27 * C2), :])
        y_ref[j] = result
        values = [result[:, cols(k)] for k in range(z.nbc)]
        st_ref[:C3, :] += fold_sums(values)
        st_ref[C3 : 2 * C3, :] += fold_sums([v * v for v in values])

    unrolled(z.Zc, 8, conv)
    send_planes(z, meta, h_refs, lambda i: y_ref[i], 1, z.Zc)


def merge_body(z, meta, yc, lo, hi, sa, sb, gains, shifts, tail, skip, gate, weight,
               lifted_out, pre_out, logit_out, y_ref, st_ref, *rest):
    h_refs = rest[:-10]
    p_ref, t_ref, act, mixed, part_one, part_two, lifted, pre_ref, logit_ref, sems = rest[-10:]
    unused, unused, factor, level = norm_coefs(
        sa[...] + sb[...], layer_gain(gains, 3), layer_gain(shifts, 3), C3, z.total // 8
    )
    matrix = pool_matrix(lift_entries).astype(F32).T.astype(BF)
    n = z.half

    def coarse_act(get):
        out = []
        for k in range(z.nbc):
            value = get(k) * factor + level
            out.append((value * sigmoid(value)).astype(BF))
        return out

    for k, value in enumerate(coarse_act(lambda k: lo[0, :, cols(k)].astype(F32))):
        act[0, :, cols(k)] = value
    for k, value in enumerate(coarse_act(lambda k: hi[0, :, cols(k)].astype(F32))):
        act[z.Zc + 1, :, cols(k)] = value

    def own(j, carry):
        for k, value in enumerate(coarse_act(lambda k: yc[j, :, cols(k)])):
            act[j + 1, :, cols(k)] = value
        return carry

    lax.fori_loop(0, z.Zc, own, 0)

    @pl.when(meta[1] == 0)
    def low_edge():
        act[0] = act[1]

    @pl.when(meta[2] == 0)
    def high_edge():
        act[z.Zc + 1] = act[z.Zc]

    def spread(jp, slot):
        rows = [None] * n
        for k in range(z.nbc):
            both = dot(act[jp, :, cols(k)], matrix)
            rows[k], rows[k + z.nbc] = both[:, :128], both[:, 128:]
        lane = lanes(C3)
        first, last = rows[0], rows[n - 1]
        before = jnp.where(lane < 64, first, roll(last, 64))
        after = jnp.where(lane < 64, roll(first, 64), last)
        extended = [before] + rows + [after]
        for i in range(n):
            t_ref[slot, :, cols(2 * i)] = 0.25 * extended[i] + 0.75 * extended[i + 1]
            t_ref[slot, :, cols(2 * i + 1)] = 0.75 * extended[i + 1] + 0.25 * extended[i + 2]
            if i % 2:
                yield

    run(spread(0, 0))
    bias = tail[T_GATE_BIAS : T_GATE_BIAS + CG, :]
    score = tail[T_SCORE : T_SCORE + CG, :]
    score_bias = tail[T_SCORE_BIAS : T_SCORE_BIAS + 1, :]

    def build(zp, slot, edge):
        turn = zp % 2 if isinstance(zp, int) else 1 - (slot + 1) % 2
        wa, wb = (0.75, 0.25) if turn == 0 else (0.25, 0.75)
        old = (zp // 2) % 2 if isinstance(zp, int) else lax.rem(zp // 2, 2)
        new = 1 - old
        if turn == 0:
            yield from spread(zp // 2 + 1, new)
        valid = None if edge is None else meta[1 + edge]
        base, row = slot * 9 * 192, slot * 192
        mixed[row : row + C2, :] = skip[zp]
        wide = []
        for k in range(z.nb):
            value = (wa * t_ref[old, :, cols(k)] + wb * t_ref[new, :, cols(k)]).astype(BF)
            mixed[row + C2 : row + 192, cols(k)] = value
            lifted[zp, :, cols(k)] = value
            value = value.astype(F32)
            wide.append(value if valid is None else jnp.where(valid > 0, value, 0.0))
            if k % 2:
                yield
        gated = []
        for n in range(z.half):
            rows = dot(gate[...], mixed[row : row + 192, 256 * n : 256 * (n + 1)])
            logit_ref[zp, :, 256 * n : 256 * (n + 1)] = rows[CG:]
            for k in (2 * n, 2 * n + 1):
                pre = rows[:CG, cols(k - 2 * n)] + bias
                pre_ref[zp, :, cols(k)] = pre
                inner = pre * sigmoid(pre)
                alpha = sigmoid(jnp.sum(score * inner, axis=0, keepdims=True) + score_bias)
                if valid is not None:
                    alpha = jnp.where(valid > 0, alpha, 0.0)
                gated.append(mixed[row : row + C2, cols(k)].astype(F32) * alpha)
            yield
        yield from window_steps(p_ref, (base,), 192, C2, wide, 64)
        yield from window_steps(p_ref, (base,), 192, 0, gated, 64)

    pairs = ((lifted, lifted_out), (pre_ref, pre_out), (logit_ref, logit_out))

    def leaving(t):
        span = pl.ds(4 * t + 1, 4)
        return [
            pltpu.make_async_copy(a.at[span], b.at[span], sems.at[n, t]) for n, (a, b) in enumerate(pairs)
        ]

    def leave(t):
        for copy in leaving(t):
            copy.start()

    convolve(z, weight, p_ref, (part_one, part_two), 9 * 192, C2, y_ref, st_ref, build, leave, ratio=5)
    send_planes(z, meta, h_refs, lambda i: y_ref[i], 1, z.Z)
    for t in range(z.Z // 4):
        for copy in leaving(t):
            copy.wait()


def heads_body(z, meta, yf, sa, sb, ca, cb, lab, logit_ref, gains, shifts, tail, head, head_t,
               d_ref, bs_ref, small, gc_ref, *rest):
    h_refs, acts = rest[:-1], rest[-1]
    mean, inv, factor, level = norm_coefs(
        sa[...] + sb[...], layer_gain(gains, 5), layer_gain(shifts, 5), C2, z.total
    )
    counts = jnp.sum(ca[2 * C1 :] + cb[2 * C1 :], axis=1, keepdims=True)
    row = lax.broadcasted_iota(jnp.int32, (8, 1), 0)
    everything = jnp.sum(jnp.where(row < CLS, counts, 0.0), axis=0, keepdims=True)
    class_weight = jnp.where(row < CLS, 2.0 * everything / (3.0 * counts + everything), 0.0)
    weight_total = jnp.sum(counts * class_weight, axis=0, keepdims=True)
    scaled = class_weight / weight_total
    scaled = jnp.concatenate([scaled, jnp.zeros((8, 1), F32)], axis=0)
    rows16 = lax.broadcasted_iota(jnp.int32, (16, 128), 0)
    pad13 = jnp.zeros((13, 128), F32)
    bias_fine = jnp.concatenate([tail[T_BIAS_FINE : T_BIAS_FINE + 3, :], pad13], axis=0)
    bias_coarse = jnp.concatenate([tail[T_BIAS_COARSE : T_BIAS_COARSE + 3, :], pad13], axis=0)
    bs_ref[...] = jnp.zeros(bs_ref.shape, F32)
    small[...] = jnp.zeros(small.shape, F32)

    def logit_grad(logits, label, times):
        logits = jnp.where(rows16 < CLS, logits, -1e30)
        top = jnp.max(logits, axis=0, keepdims=True)
        terms = jnp.where(rows16 < CLS, jnp.exp(logits - top), 0.0)
        soft = terms / jnp.sum(terms, axis=0, keepdims=True)
        onehot = jnp.where(rows16.astype(F32) == label, 1.0, 0.0)
        weight = jnp.sum(scaled * onehot, axis=0, keepdims=True)
        return ((soft - onehot) * (weight * times)).astype(BF)

    def step(i, slot):
        act = acts.at[slot * C2 : (slot + 1) * C2, :]
        for k in range(z.nb):
            value = yf[i, :, cols(k)] * factor + level
            act[:, cols(k)] = (value * sigmoid(value)).astype(BF)
        logits = dot(head[...], act[...])
        fine, bias_sum, coarse_sum = [], [], []
        for k in range(z.nb):
            label = lab[i, 0:1, cols(k)]
            grad = logit_grad(logits[:, cols(k)] + bias_fine, label, 1.0)
            fine.append(grad)
            bias_sum.append(grad.astype(F32))
            grad = logit_grad(logit_ref[i + 1, :, cols(k)] + bias_coarse, label, 0.5)
            gc_ref[i, :, cols(k)] = grad
            coarse_sum.append(grad.astype(F32))
        fine = jnp.concatenate(fine, axis=1)
        small[:C2, :16] += dot_nt(act[...], fine)
        small[C2 : C2 + 16, :] += fold_sums(bias_sum)
        small[C2 + 16 : C2 + 32, :] += fold_sums(coarse_sum)
        back = dot(head_t[...], fine)
        parts, cross = [], []
        for k in range(z.nb):
            y = yf[i, :, cols(k)]
            pre = y * factor + level
            sig = sigmoid(pre)
            grad = back[:, cols(k)] * (sig * (1.0 + pre * (1.0 - sig)))
            d_ref[i, :, cols(k)] = grad
            parts.append(grad)
            cross.append(grad * ((y - mean) * inv))
        bs_ref[:C2, :] += fold_sums(parts)
        bs_ref[C2:, :] += fold_sums(cross)

    def four(t, carry):
        for r in range(4):
            step(4 * t + r, r)
        return carry

    lax.fori_loop(0, z.Z // 4, four, 0)
    send_planes(z, meta, h_refs, lambda i: d_ref[i], 1, z.Z)


def dy_builder(z, meta, layer, count, refs, p_ref, q_ref, share):
    d, d_lo, d_hi, y, y_lo, y_hi, sums, back, gains, shifts = refs
    channels = WIDTHS[layer]
    mean, inv, factor, unused = norm_coefs(
        sums, layer_gain(gains, layer), layer_gain(shifts, layer), channels, count
    )
    slope, level = grad_coefs(back, mean, inv, factor, channels, count)

    def build(zp, bases, edge):
        get_d, get_y = (lambda k: d[zp - 1, :, cols(k)]), (lambda k: y[zp - 1, :, cols(k)])
        if edge is not None:
            get_d = lambda k: (d_lo, d_hi)[edge][0, :, cols(k)].astype(F32)
            get_y = lambda k: (y_lo[y_lo.shape[0] - 1, :, cols(k)], y_hi[0, :, cols(k)])[edge].astype(F32)
        out = []
        for k in range(z.nb):
            value = factor * get_d(k) - slope * get_y(k) + level
            out.append(value if edge is None else jnp.where(meta[1 + edge] > 0, value, 0.0))
            if k % 2:
                yield
        yield from window_steps(p_ref, bases, channels, 0, out, 64)
        yield from share_steps(q_ref, bases, share, meta[3], out, 64)

    def build_or_edge(zp, bases, last):
        out = []
        own = jnp.minimum(zp - 1, z.Z - 1)
        for k in range(z.nb):
            near_d = jnp.where(last, d_hi[0, :, cols(k)].astype(F32), d[own, :, cols(k)])
            near_y = jnp.where(last, y_hi[0, :, cols(k)].astype(F32), y[own, :, cols(k)])
            value = factor * near_d - slope * near_y + level
            out.append(jnp.where(jnp.logical_and(last, meta[2] == 0), 0.0, value))
            if k % 2:
                yield
        yield from window_steps(p_ref, bases, channels, 0, out, 64)
        yield from share_steps(q_ref, bases, share, meta[3], out, 64)

    build.or_edge = build_or_edge
    return build


def back_body(z, layer, below, y_base, share, meta, d, d_lo, d_hi, y, y_lo, y_hi, sa, sb, ba, bb,
              yb, ua, ub, gains, shifts, weight, *rest):
    d_ref, bs_ref, dk_out = rest[:3]
    h_refs, (p_ref, q_ref, x_ref, dk_ref), parts = rest[3:-6], rest[-6:-2], rest[-2:]
    make = dy_builder(z, meta, layer, z.total,
                       (d, d_lo, d_hi, y, y_lo, y_hi, sa[...] + sb[...], ba[...] + bb[...], gains, shifts),
                      p_ref, q_ref, share)
    width = WIDTHS[below]
    mean, inv, factor, level = norm_coefs(
        ua[...] + ub[...], layer_gain(gains, below), layer_gain(shifts, below), width, z.total
    )
    edge = jnp.zeros((2 * width, z.V), BF)
    x_ref[: 2 * width, :] = edge
    x_ref[(z.Z + 2) * width :, :] = edge
    bs_ref[...] = jnp.zeros(bs_ref.shape, F32)
    rows = 9 * WIDTHS[layer]
    part = rows // share
    dk_ref[...] = jnp.zeros(dk_ref.shape, F32)

    for part_ref in parts:
        part_ref[...] = jnp.zeros(part_ref.shape, F32)

    def build(zp, slot, edge):
        return make(zp, (slot * rows,), edge)

    def consume(zp, slot):
        if not isinstance(zp, int):
            for k in range(z.nb):
                pre = yb[zp + y_base, :, cols(k)] * factor + level
                x_ref[ds((zp + 2) * width, width), cols(k)] = (pre * sigmoid(pre)).astype(BF)
        sums, cross = [], []

        def finish(at, k, value):
            y_value = yb[at + y_base, :, cols(k)]
            pre = y_value * factor + level
            sig = sigmoid(pre)
            grad = value * (sig * (1.0 + pre * (1.0 - sig)))
            d_ref[at, :, cols(k)] = grad
            sums.append(grad)
            cross.append(grad * ((y_value - mean) * inv))

        yield from scatter(zp, weight, p_ref.at[slot * rows : (slot + 1) * rows, :], width, parts, z.nb, finish)
        add_sums(zp, bs_ref, width, sums, cross)
        if share == 1:
            window = p_ref[slot * rows : (slot + 1) * rows, :]
        else:
            window = q_ref[slot * part : (slot + 1) * part, :]
        dk_ref[...] += dot_nt(window, x_ref[ds(zp * width, 3 * width), :])

    flow(z, build, consume, 3, (d, y, yb))
    if width == C2:
        pack_wide(dk_out, dk_ref, part)
    else:
        dk_out[:, : 3 * width] = dk_ref[...]
    if h_refs:
        send_planes(z, meta, h_refs, lambda i: d_ref[i], 1, z.Z)


def merge_back_body(z, share, meta, d, d_lo, d_hi, y, y_lo, y_hi, sa, sb, ba, bb, skip, lifted, pre_ref, gc_ref,
                    yc, yc_lo, yc_hi, ua, ub, gains, shifts, tail, weight, gate_t,
                    gskip_out, gcoarse, bs_ref, dk_out, small, *rest):
    h_refs, (p_ref, q_ref, eg, x_ref, acc, dk_ref, gskip, sems) = rest[:-8], rest[-8:]
    build = dy_builder(z, meta, 4, z.total,
                       (d, d_lo, d_hi, y, y_lo, y_hi, sa[...] + sb[...], ba[...] + bb[...], gains, shifts),
                       p_ref, q_ref, share)
    score = tail[T_SCORE : T_SCORE + CG, :]
    score_bias = tail[T_SCORE_BIAS : T_SCORE_BIAS + 1, :]
    small[...] = jnp.zeros(small.shape, F32)
    dk_ref[...] = jnp.zeros(dk_ref.shape, F32)
    acc[...] = jnp.zeros(acc.shape, F32)
    n = z.half
    lane = lanes(C3)
    rows = 9 * C2
    part = 27 * C2 // share

    def plane(i, r4):
        start = r4 * rows
        turn = (r4 % 2) * 256
        side = (r4 % 2) * 48
        eg[side + CG : side + 48, :] = gc_ref[i]
        x_ref[turn + C2 : turn + 192, :] = lifted[i + 1]
        x_ref[turn + 192 : turn + 256, :] = skip[i + 1]
        wide, e_sum, s_sum, r_sum = [], [], [], []
        for q in range(z.half):
            span = slice(256 * q, 256 * (q + 1))
            result = dot(weight[...], p_ref[start : start + 3 * rows, span])
            alphas = []
            for k in (2 * q, 2 * q + 1):
                piece = result[:C2, cols(k - 2 * q)]
                pre = pre_ref[i + 1, :, cols(k)]
                sig = sigmoid(pre)
                inner = pre * sig
                alpha = sigmoid(jnp.sum(score * inner, axis=0, keepdims=True) + score_bias)
                near = skip[i + 1, :, cols(k)].astype(F32)
                grad = jnp.sum(piece * near, axis=0, keepdims=True)
                grad = grad * alpha * (1.0 - alpha)
                e = (score * grad * (sig * (1.0 + pre * (1.0 - sig)))).astype(BF)
                eg[side : side + CG, cols(k)] = e
                x_ref[turn : turn + C2, cols(k)] = (near * alpha).astype(BF)
                alphas.append(alpha)
                e_sum.append(e.astype(F32))
                s_sum.append(grad * inner)
                r_sum.append(grad)
            extra = dot(gate_t[...], eg[side : side + 48, span])
            for k in (2 * q, 2 * q + 1):
                at = cols(k - 2 * q)
                gskip[i, :, cols(k)] = result[:C2, at] * alphas[k - 2 * q] + extra[:C2, at]
                wide.append(result[C2:, at] + extra[C2:, at])
            yield
        small[192:224, :] += fold_sums(e_sum)
        small[224:256, :] += fold_sums(s_sum)
        small[256:257, :] += fold_sums(r_sum)
        low = [
            0.75 * (wide[2 * m] + wide[2 * m + 1])
            + (0.25 * wide[2 * m + 2] if m < n - 1 else 0.0)
            + (0.25 * wide[2 * m - 1] if m > 0 else 0.0)
            for m in range(n)
        ]
        before, after = 0.25 * wide[0], 0.25 * wide[-1]
        low[0] = low[0] + jnp.where(lane < 64, before, roll(after, 64))
        low[n - 1] = low[n - 1] + jnp.where(lane < 64, roll(before, 64), after)
        j, r = i // 2, r4 % 2
        for m in range(n):
            acc[j + 1, :, cols(m)] += 0.75 * low[m]
            acc[j + 2 * r, :, cols(m)] += 0.25 * low[m]
        yield
        if share == 1:
            window = p_ref[start : start + 3 * rows, :]
        else:
            window = q_ref[start // share : start // share + part, :]
        tall = jnp.concatenate([window, eg[side : side + 48, :]], axis=0)
        dk_ref[...] += dot_nt(tall, x_ref[turn : turn + 256, :])

    need(0, d, y)
    for zp in range(3):
        run(build(zp, (zp * rows,), 0 if zp == 0 else None))

    def four(t, carry):
        need(t, skip, lifted, pre_ref, gc_ref)
        for r in range(4):
            if r == 2:

                @pl.when(t + 1 < z.Z // 4)
                def fetch():
                    need(t + 1, d, y)

            at = (r + 3) % 4
            bases = (at * rows, (at + 4) * rows) if at < 2 else (at * rows,)
            zp = 4 * t + r + 3
            if r < 2:
                steps = build(zp, bases, None)
            else:
                steps = build.or_edge(zp, bases, zp == z.Z + 1)
            interleave(plane(4 * t + r, r), steps, 2)
        leaving(t).start()
        return carry

    def leaving(t):
        span = pl.ds(4 * t, 4)
        return pltpu.make_async_copy(gskip.at[span], gskip_out.at[span], sems.at[t])

    lax.fori_loop(0, z.Z // 4, four, 0)
    pack_wide(dk_out, dk_ref[:part, :192], part)
    tall = dk_ref[part:, :].T
    small[:C2, :48] = tall[192:]
    small[C2:192, :48] = tall[C2:192]

    matrix = pool_matrix(lift_entries)

    def shrink(jp, carry):
        for k in range(z.nbc):
            pair = jnp.concatenate([acc[jp, :, cols(k)], acc[jp, :, cols(k + z.nbc)]], axis=1)
            gcoarse[jp, :, cols(k)] = split_dot(pair, matrix)
        return carry

    lax.fori_loop(0, z.Zc + 2, shrink, 0)

    @pl.when(meta[1] == 0)
    def low_edge():
        gcoarse[1] += gcoarse[0]
        gcoarse[0] = jnp.zeros((C3, z.Vc), F32)

    @pl.when(meta[2] == 0)
    def high_edge():
        gcoarse[z.Zc] += gcoarse[z.Zc + 1]
        gcoarse[z.Zc + 1] = jnp.zeros((C3, z.Vc), F32)

    mean, inv, factor, level = norm_coefs(
        ua[...] + ub[...], layer_gain(gains, 3), layer_gain(shifts, 3), C3, z.total // 8
    )
    bs_ref[...] = jnp.zeros(bs_ref.shape, F32)

    def sums(jp, get):
        for k in range(z.nbc):
            value = get(k)
            pre = value * factor + level
            sig = sigmoid(pre)
            grad = gcoarse[jp, :, cols(k)] * (sig * (1.0 + pre * (1.0 - sig)))
            bs_ref[:C3, :] += grad
            bs_ref[C3:, :] += grad * ((value - mean) * inv)

    sums(0, lambda k: yc_lo[0, :, cols(k)].astype(F32))
    sums(z.Zc + 1, lambda k: yc_hi[0, :, cols(k)].astype(F32))

    def own(j, carry):
        sums(j + 1, lambda k: yc[j, :, cols(k)])
        return carry

    lax.fori_loop(0, z.Zc, own, 0)
    if z.two:
        start = jnp.where(meta[0] == 0, z.Zc, 0)
        for m in range(2):
            h_refs[0][m] = gcoarse[start + m].astype(BF)
    else:
        for m in range(2):
            h_refs[0][m] = gcoarse[m].astype(BF)
            h_refs[1][m] = gcoarse[z.Zc + m].astype(BF)
    for t in range(z.Z // 4):
        leaving(t).wait()


def coarse_back_body(z, share, meta, gcoarse, g_lo, g_hi, yc, yc_lo, yc_hi, sa, sb, ba, bb, pooled, gskip, y3,
                     ua, ub, gains, shifts, weight, d_ref, bs_ref, dk_out, *rest):
    h_refs, (p_ref, x_ref, dk_ref) = rest[:-3], rest[-3:]
    mean, inv, factor, level = norm_coefs(
        sa[...] + sb[...], layer_gain(gains, 3), layer_gain(shifts, 3), C3, z.total // 8
    )
    slope, offset = grad_coefs(ba[...] + bb[...], mean, inv, factor, C3, z.total // 8)

    def plane(jp, get_y, extra, valid):
        out = []
        for k in range(z.nbc):
            value = get_y(k)
            pre = value * factor + level
            sig = sigmoid(pre)
            grad = gcoarse[jp, :, cols(k)] + extra(k)
            grad = grad * (sig * (1.0 + pre * (1.0 - sig)))
            grad = factor * grad - slope * value + offset
            out.append(grad if valid is None else jnp.where(valid > 0, grad, 0.0))
        place_windows(p_ref, (jp * (9 * C3),), C3, 0, out, 32)

    def from_lo(m):
        return lambda k: jnp.where(meta[1] > 0, g_lo[m, :, cols(k)].astype(F32), 0.0)

    def from_hi(m):
        return lambda k: jnp.where(meta[2] > 0, g_hi[m, :, cols(k)].astype(F32), 0.0)

    plane(0, lambda k: yc_lo[0, :, cols(k)].astype(F32), from_lo(0), meta[1])
    plane(1, lambda k: yc[0, :, cols(k)], from_lo(1), None)

    def inner(j):
        plane(j + 2, lambda k: yc[j + 1, :, cols(k)], lambda k: 0.0, None)

    if z.Zc > 2:
        unrolled(z.Zc - 2, 3, inner)
    plane(z.Zc, lambda k: yc[z.Zc - 1, :, cols(k)], from_hi(0), None)
    plane(z.Zc + 1, lambda k: yc_hi[0, :, cols(k)].astype(F32), from_hi(1), meta[2])

    edge = jnp.zeros((2 * C2, z.Vc), BF)
    x_ref[: 2 * C2, :] = edge
    x_ref[(z.Zc + 2) * C2 :, :] = edge

    for j in range(z.Zc):
        x_ref[(j + 2) * C2 : (j + 3) * C2, :] = pooled[j + 1]
    mean, inv, factor, level = norm_coefs(
        ua[...] + ub[...], layer_gain(gains, 2), layer_gain(shifts, 2), C2, z.total
    )
    matrix = pool_matrix(mean_entries).astype(F32).T.astype(BF)
    bs_ref[...] = jnp.zeros(bs_ref.shape, F32)
    rows = 9 * C3

    def step(s, carry):
        need(s, y3, gskip)
        result = dot(weight[...], p_ref[ds(s * (2 * rows), 4 * rows), :])
        parts, cross = [], []
        for r in range(2):
            low = result[r * C2 : (r + 1) * C2]
            spread = [None] * z.half
            for k in range(z.nbc):
                both = split_dot(low[:, cols(k)], matrix)
                spread[k], spread[k + z.nbc] = both[:, :128], both[:, 128:]
            for q in range(2):
                at = 4 * s + 2 * r + q
                for k in range(z.nb):
                    value = y3[at, :, cols(k)]
                    pre = value * factor + level
                    sig = sigmoid(pre)
                    grad = spread[k // 2] + gskip[at, :, cols(k)]
                    grad = grad * (sig * (1.0 + pre * (1.0 - sig)))
                    d_ref[at, :, cols(k)] = grad
                    parts.append(grad)
                    cross.append(grad * ((value - mean) * inv))
        bs_ref[:C2, :] += fold_sums(parts)
        bs_ref[C2:, :] += fold_sums(cross)
        return carry

    lax.fori_loop(0, z.Zc // 2, step, 0)
    part = rows // share

    def kernel_grad(zp):
        window = p_ref[ds(zp * rows + meta[3] * part, part), :]
        return dot_nt(window, x_ref[zp * C2 : (zp + 3) * C2, :])

    dk_ref[...] = fold_sums([kernel_grad(zp) for zp in range(z.Zc + 2)])
    pack_wide(dk_out, dk_ref, part)
    send_planes(z, meta, h_refs, lambda i: d_ref[i], 1, z.Z)


def first_back_body(z, meta, d, y1, p_img, sa, sb, ba, bb, gains, shifts, dk_ref, low):
    mean, inv, factor, unused = norm_coefs(
        sa[...] + sb[...], layer_gain(gains, 0), layer_gain(shifts, 0), C1, z.total
    )
    slope, level = grad_coefs(ba[...] + bb[...], mean, inv, factor, C1, z.total)

    def step(i):
        for k in range(z.nb):
            value = factor * d[i, :, cols(k)] - slope * y1[i + 1, :, cols(k)] + level
            low[ds(i * C1, C1), cols(k)] = value.astype(BF)

    unrolled(z.Z, 4, step)
    table = dot_nt(p_img[...], low[...])
    shape = (9 * z.ZP, z.Z * C1)
    gap = lax.rem(lax.broadcasted_iota(jnp.int32, shape, 0), z.ZP) - (
        lax.broadcasted_iota(jnp.int32, shape, 1) // C1
    )
    dk_ref[...] = jnp.zeros(dk_ref.shape, F32)
    for a in range(3):
        kept = jnp.where(gap == a + 1, table, 0.0)
        folded = fold_sums([kept[:, cols(k)] for k in range(z.Z * C1 // 128)])
        folded = folded + roll(folded, 64)
        folded = folded + roll(folded, 32)
        for t in range(9):
            dk_ref[9 * a + t : 9 * a + t + 1, :] = jnp.sum(
                folded[t * z.ZP : (t + 1) * z.ZP], axis=0, keepdims=True
            )


def gather_body(z, meta, *refs):
    ins, (out, norm), (stage, stage_b, flat, column, quarters, full, full_b) = refs[:-9], refs[-9:-7], refs[-7:]
    shared, ins = ins[: z.share], ins[z.share :]
    pairs = [(ins[2 * j], ins[2 * j + 1]) for j in range(len(ins) // 2)]
    (first, second, small_head, small_gate, b_first, b_second, b_third, b_coarse, b_merge, b_final) = pairs
    for k in range(z.share):
        quarters[jnp.bitwise_xor(meta[3], k)] = shared[k][...].astype(F32)

    def unpack(start, count, taps_out):
        part = count // z.share
        width = part if taps_out == C3 else taps_out // z.share
        for k in range(z.share):
            unpack_wide(full, full_b, k, width, taps_out, quarters.at[k], start, part)

    def total(pair):
        return pair[0][...] + pair[1][...]

    def pack(row, taps_out, width):
        count = taps_out * width // 128
        fold = 128 // width
        lane = lanes(count)
        value = stage[pl.ds(0, count, stride=fold), :]
        for j in range(1, fold):
            part = roll(stage[pl.ds(j, count, stride=fold), :], j * width)
            value = jnp.where(lane < j * width, value, part)
        flat[row : row + count, :] = value

    flat[ROWS : ROWS + 8, :] = jnp.zeros((8, 128), F32)
    stage[0:5, :32] = jnp.zeros((5, 32), F32)
    stage[5:32, :32] = (first[0][...] + first[1][...])[:27, :32]
    pack(ROW_FIRST, 32, 32)
    wide_at = 27 * C2 // z.share * 3 // 2
    for row, out_c, in_c, source in (
        (ROW_SECOND, C2, C1, second),
        (ROW_THIRD, C2, C2, 2 * wide_at),
        (ROW_COARSE, C3, C2, wide_at + wide_at // 3),
        (ROW_FINAL, C2, C2, wide_at),
    ):
        count = 9 * out_c
        if source is second:
            full[:count, :] = total(second)
        else:
            unpack(source, count, out_c)
        for t in range(9):
            span = slice(t * out_c, (t + 1) * out_c)
            for a in range(3):
                at = (9 * a + 8 - t) * out_c
                if a * in_c < 128:
                    stage[at : at + out_c, :in_c] = full[span, a * in_c : (a + 1) * in_c]
                else:
                    stage[at : at + out_c, :in_c] = full_b[span, :in_c]
        pack(row, 27 * out_c, in_c)
    unpack(0, 27 * C2, C2)
    for t in range(27):
        at = (26 - t) * C2
        stage[at : at + C2, :] = full[t * C2 : (t + 1) * C2, :]
        stage_b[at : at + C2, :64] = full_b[t * C2 : (t + 1) * C2, :64]
    half = 27 * C2 // 2
    even, even_b = stage[pl.ds(0, half, stride=2), :], stage_b[pl.ds(0, half, stride=2), :]
    odd, odd_b = stage[pl.ds(1, half, stride=2), :], stage_b[pl.ds(1, half, stride=2), :]
    left = lanes(half) < 64
    odd = roll(odd, 64)
    flat[pl.ds(ROW_MERGE, half, stride=3), :] = even
    flat[pl.ds(ROW_MERGE + 1, half, stride=3), :] = jnp.where(left, even_b, odd)
    flat[pl.ds(ROW_MERGE + 2, half, stride=3), :] = jnp.where(left, odd, roll(odd_b, 64))

    gate = total(small_gate)
    turned = gate[:192].T
    stage[:CG, :C2] = turned[:CG, :C2]
    pack(ROW_GATE_SKIP, CG, C2)
    flat[ROW_GATE_COARSE : ROW_GATE_COARSE + CG, :] = turned[:CG, C2:]
    heads = total(small_head)
    lane = lanes(C3)
    column[TAIL_LEN - 7 :, :] = jnp.zeros((2048 - TAIL_LEN + 7, 128), F32)
    column[T_GATE_BIAS : T_GATE_BIAS + CG, :] = gate[192:224]
    column[T_SCORE : T_SCORE + CG, :] = gate[224:256]
    column[T_SCORE_BIAS : T_SCORE_BIAS + 1, :] = gate[256:257]
    for k in range(CLS):
        at = T_HEAD_FINE + k * C2
        column[at : at + C2, :] = jnp.where(lane[:C2] == k, heads[:C2], 0.0)
        at = T_HEAD_COARSE + k * C3
        column[at : at + C3, :] = jnp.where(lane == CG + k, gate[C2:192], 0.0)
    column[T_BIAS_FINE : T_BIAS_FINE + 3, :] = heads[C2 : C2 + 3]
    column[T_BIAS_COARSE : T_BIAS_COARSE + 3, :] = heads[C2 + 16 : C2 + 19]
    for layer, pair in enumerate((b_first, b_second, b_third, b_coarse, b_merge, b_final)):
        sums = total(pair)
        width = WIDTHS[layer]
        at = T_GAINS + NORM_AT[layer]
        column[at : at + width, :] = sums[width : 2 * width]
        at = T_SHIFTS + NORM_AT[layer]
        column[at : at + width, :] = sums[:width]
    for k in range(16):
        flat[ROW_TAIL + k : ROW_TAIL + k + 1, :] = jnp.sum(
            column[k * 128 : (k + 1) * 128, :].T, axis=0, keepdims=True
        )
    chunk = ROWS // 21
    mask = lanes(chunk) < 96

    def finish(i, acc):
        base = pl.multiple_of(i * chunk, 8)
        block = roll(flat[pl.ds(base, chunk + 8), :], 96)
        out[pl.ds(base, chunk), :] = jnp.where(mask, block[1 : chunk + 1], block[2 : chunk + 2])
        return acc + fold_sums([block[8 * m : 8 * m + 8] * block[8 * m : 8 * m + 8] for m in range(chunk // 8)])

    acc = lax.fori_loop(0, 21, finish, jnp.zeros((8, 128), F32))
    sq = jnp.sum(jnp.sum(acc, axis=1, keepdims=True), axis=0, keepdims=True)
    norm[...] = jnp.broadcast_to(jnp.sqrt(sq), (8, 128))


def local(z, images, labels, weights, first_moment, second_moment):
    devices = z.D * z.H
    linear = lax.axis_index("depth") * z.H + lax.axis_index("height")
    position = lax.rem(linear, z.G)
    meta = jnp.stack(
        [position, (position > 0).astype(jnp.int32), (position < z.G - 1).astype(jnp.int32),
         lax.rem(linear // z.G, z.share)]
    ).astype(jnp.int32)

    call = functools.partial(kernel_call, room=12 if z.V <= 1024 else 18)

    def partner(value, step):
        return lax.ppermute(value, AXES, [(i, i ^ step) for i in range(devices)])

    def both(value):
        step = 1
        while step * 2 < z.G:
            value = value + partner(value, step)
            step *= 2
        return value, partner(value, step)

    def neighbours(sent):
        if z.two:
            got = partner(sent[0], 1)
            return got, got
        up = [(i, i + 1) for i in range(devices) if i % z.G != z.G - 1]
        return (
            lax.ppermute(sent[1], AXES, up),
            lax.ppermute(sent[0], AXES, [(j, i) for i, j in up]),
        )

    def shares(values):
        value = jnp.concatenate([one + two for one, two in values], axis=0).astype(BF)
        return [value] + [
            lax.ppermute(value, AXES, [(i, (i // z.G ^ k) * z.G + i % z.G) for i in range(devices)])
            for k in range(1, z.share)
        ]

    def sent(count, channels, lanes_):
        return [((count, channels, lanes_), BF)] * (1 if z.two else 2)

    V, Vc, Z, Zc = z.V, z.Vc, z.Z, z.Zc
    local_rows = z.lz * z.ly
    (mine,) = call(
        lambda *r: mine_body(z, *r), meta, [images, labels], [((devices, local_rows, 128), BF)],
        [pltpu.VMEM((local_rows, 128), F32)],
    )
    everyone = lax.all_to_all(
        mine, AXES, 0, 0
    ).reshape(devices * local_rows, 128)
    flat = jnp.pad(weights, (PAD, ROWS * 128 - PAD - weights.shape[0])).reshape(ROWS, 128)
    tail = jnp.broadcast_to(
        jnp.pad(weights[TAIL_AT:], (0, 1))[:, None], (TAIL_LEN + 1, 128)
    )
    w = prepare(z, meta, flat, tail)
    gains, shifts = w["gains"], w["shifts"]

    def fars(values, base=None):
        return [Far(value, base) for value in values]

    y1, st1, p_img, lab = call(
        lambda *r: first_body(z, *r), meta, [Far(everyone), Far(w["big"])],
        [(((Z + 2) * C1, V), F32), ((72, 128), F32), ((9 * z.ZP, V), BF), ((Z, 8, V), F32)],
        [pltpu.VMEM((devices * local_rows, 128), F32), pltpu.VMEM((z.PY * z.DP, 128), F32)],
    )
    st1 = both(st1)
    parts = [pltpu.VMEM((C2, V), F32), pltpu.VMEM((C2, V), F32)]
    y2, st2, *h2 = call(
        lambda *r: second_body(z, *r), meta, [y1, *st1, gains, shifts, w["second"]],
        [((Z, C2, V), F32), ((2 * C2, 128), F32)] + sent(1, C2, V),
        [pltpu.VMEM((2 * 9 * C1, V), BF), *parts],
    )
    st2, h2 = both(st2), neighbours(h2)
    wide_p = pltpu.VMEM((2 * 9 * C2, V), BF)
    share_p = pltpu.VMEM((2 * 9 * C2 // z.share, V), BF)
    y3, st3, *h3 = call(
        lambda *r: middle_body(z, 1, 2, *r), meta, [y2, *h2, *st2, gains, shifts, w["third"]],
        [((Z, C2, V), F32), ((2 * C2, 128), F32)] + sent(2, C2, V), [wide_p, *parts],
    )
    st3, h3 = both(st3), neighbours(h3)
    skip, pooled, yc, stc, *hc = call(
        lambda *r: coarse_body(z, *r), meta, [y3, *h3, *st3, gains, shifts, w["coarse"]],
        [((Z + 2, C2, V), BF), ((Zc + 2, C2, Vc), BF), ((Zc, C3, Vc), F32), ((2 * C3, 128), F32)]
        + sent(1, C3, Vc),
        [pltpu.VMEM(((Zc + 2) * 9 * C2, Vc), BF)],
    )
    stc, hc = both(stc), neighbours(hc)
    lifted, pre, logits, ym, stm, *hm = call(
        lambda *r: merge_body(z, *r), meta,
        [yc, *hc, *stc, gains, shifts, tail, skip, w["gate"], w["merge"]],
        [((Z + 2, C3, V), BF), ((Z + 2, CG, V), F32), ((Z + 2, 16, V), F32), ((Z, C2, V), F32),
         ((2 * C2, 128), F32)] + sent(1, C2, V),
        [pltpu.VMEM((2 * 9 * 192, V), BF), pltpu.VMEM((2, C3, V), F32), pltpu.VMEM((Zc + 2, C3, Vc), BF),
         pltpu.VMEM((384, V), BF), *parts, pltpu.VMEM((Z + 2, C3, V), BF), pltpu.VMEM((Z + 2, CG, V), F32),
         pltpu.VMEM((Z + 2, 16, V), F32), pltpu.SemaphoreType.DMA((3, Z // 4))],
        hbm_outs=(0, 1, 2),
    )
    stm, hm = both(stm), neighbours(hm)
    yf, stf, *hf = call(
        lambda *r: middle_body(z, 4, 1, *r), meta, [ym, *hm, *stm, gains, shifts, w["final"]],
        [((Z, C2, V), F32), ((2 * C2, 128), F32)] + sent(1, C2, V), [wide_p, *parts],
    )
    stf, hf = both(stf), neighbours(hf)
    counts = fars(st1)
    df, bf, small_head, gc, *hdf = call(
        lambda *r: heads_body(z, *r), meta,
        [yf, *stf, *counts, Far(lab), Far(logits), gains, shifts, tail, w["head"], w["head_t"]],
        [((Z, C2, V), F32), ((2 * C2, 128), F32), ((C2 + 32, 128), F32), ((Z, 16, V), BF)] + sent(1, C2, V),
        [pltpu.VMEM((4 * C2, V), BF)],
    )
    bf, hdf, small_head = both(bf), neighbours(hdf), both(small_head)
    x_wide = pltpu.VMEM(((Z + 4) * C2, V), BF)
    part_rows = 9 * C2 // z.share
    packed = 3 * part_rows // 2
    dk_wide = pltpu.VMEM((part_rows, 192), F32)
    dm, bm, kf, *hdm = call(
        lambda *r: back_body(z, 5, 4, 0, z.share, *r), meta,
        [df, *hdf, yf, *hf, *stf, *bf, ym, *stm, gains, shifts, w["b_final"]],
        [((Z, C2, V), F32), ((2 * C2, 128), F32), ((packed, 128), F32)] + sent(1, C2, V),
        [wide_p, share_p, x_wide, dk_wide, *parts],
    )
    bm, hdm, kf = both(bm), neighbours(hdm), both(kf)
    gskip, gcoarse, bc, km, small_gate, *hg = call(
        lambda *r: merge_back_body(z, z.share, *r), meta,
        [dm, *hdm, ym, *hm, *stm, *bm, Far(skip, 1), Far(lifted, 1), Far(pre, 1), Far(gc, 0),
         Far(yc), *hc, *stc, gains, shifts, tail, w["b_merge"], w["gate_t"]],
        [((Z, C2, V), F32), ((Zc + 2, C3, Vc), F32), ((2 * C3, 128), F32), ((3 * packed, 128), F32),
         ((264, 128), F32)] + sent(2, C3, Vc),
        [pltpu.VMEM((6 * 9 * C2, V), BF), pltpu.VMEM((6 * 9 * C2 // z.share, V), BF), pltpu.VMEM((96, V), BF), pltpu.VMEM((512, V), BF),
         pltpu.VMEM((Zc + 2, C3, V // 2), F32), pltpu.VMEM((3 * part_rows + 48, 256), F32),
         pltpu.VMEM((Z, C2, V), F32), pltpu.SemaphoreType.DMA((Z // 4,))],
        hbm_outs=(0,),
    )
    bc, hg, km, small_gate = both(bc), neighbours(hg), both(km), both(small_gate)
    d3, b3, kc, *hd3 = call(
        lambda *r: coarse_back_body(z, z.share, *r), meta,
        [gcoarse, *hg, Far(yc), *hc, *stc, *bc, Far(pooled), Far(gskip, 0), Far(y3, 0), *st3,
         gains, shifts, w["b_coarse"]],
        [((Z, C2, V), F32), ((2 * C2, 128), F32), ((2 * packed, 128), F32)] + sent(1, C2, V),
        [pltpu.VMEM(((Zc + 2) * 9 * C3, Vc), BF), pltpu.VMEM(((Zc + 4) * C2, Vc), BF),
         pltpu.VMEM((2 * part_rows, 192), F32)],
    )
    b3, hd3, kc = both(b3), neighbours(hd3), both(kc)
    d2, b2, k3, *hd2 = call(
        lambda *r: back_body(z, 2, 1, 0, z.share, *r), meta,
        [d3, *hd3, Far(y3, 0), *h3, *st3, *b3, Far(y2, 0), *st2, gains, shifts, w["b_third"]],
        [((Z, C2, V), F32), ((2 * C2, 128), F32), ((packed, 128), F32)] + sent(1, C2, V),
        [wide_p, share_p, x_wide, dk_wide, *parts],
    )
    b2, hd2, shared = both(b2), neighbours(hd2), shares([km, kf, kc, both(k3)])
    y1_planes = y1.reshape(Z + 2, C1, V)
    d1, b1, k2 = call(
        lambda *r: back_body(z, 1, 0, 1, 1, *r), meta,
        [d2, *hd2, Far(y2, 0), *h2, *st2, *b2, Far(y1_planes, 1), *st1, gains, shifts,
         w["b_second"], ],
        [((Z, C1, V), F32), ((2 * C1, 128), F32), ((9 * C2, 128), F32)],
        [wide_p, share_p, pltpu.VMEM(((Z + 4) * C1, V), BF), pltpu.VMEM((9 * C2, 3 * C1), F32), pltpu.VMEM((C1, V), F32), pltpu.VMEM((C1, V), F32)],
    )
    b1, k2 = both(b1), both(k2)
    (k1,) = call(
        lambda *r: first_back_body(z, *r), meta,
        [d1, Far(y1_planes), Far(p_img), *fars(st1), *b1, gains, shifts, *[Held(part) for part in shared]],
        [((32, 128), F32)], [pltpu.VMEM((Z * C1, V), BF)],
    )
    k1 = both(k1)
    pieces = (k1, k2, small_head, small_gate, b1, b2, b3, bc, bm, bf)
    grad, norm = call(
        lambda *r: gather_body(z, *r), meta,
        fars(shared) + [Far(part) for pair in pieces for part in pair],
        [((ROWS, 128), F32), ((8, 128), F32)],
        [pltpu.VMEM((27 * C3, 128), F32), pltpu.VMEM((27 * C2, 128), F32),
         pltpu.VMEM((ROWS + 8, 128), F32), pltpu.VMEM((2048, 128), F32)]
        + [pltpu.VMEM((z.share, 7 * packed, 128), F32)] + [pltpu.VMEM((27 * C2, 128), F32)] * 2,
    )
    gradient = grad.reshape(ROWS * 128)[: weights.shape[0]]
    grad_norm = norm[0, 0]
    clipped = gradient * jnp.minimum(1.0, CLIP_NORM / (grad_norm + 1e-06))
    moment_one = BETA_ONE * first_moment + (1.0 - BETA_ONE) * clipped
    moment_two = BETA_TWO * second_moment + (1.0 - BETA_TWO) * clipped * clipped
    corrected_one = moment_one / (1.0 - BETA_ONE**STEP)
    corrected_two = moment_two / (1.0 - BETA_TWO**STEP)
    updated = weights - LEARN_RATE * (
        corrected_one / (jnp.sqrt(corrected_two) + ADAM_EPS) + DECAY_RATE * weights
    )
    return (grad_norm, moment_one, moment_two, updated, updated.astype(BF))


def solution(mesh):
    depth, height = mesh.shape["depth"], mesh.shape["height"]

    def step(images, labels, weights, first_moment, second_moment):
        z = Sizes(depth, height, images.shape[1] // depth, images.shape[2] // height, images.shape[3])
        placed = (P(None, "depth", "height", None), P(None, "depth", "height", None), P(), P(), P())
        return jax.shard_map(
            lambda *arrays: local(z, *arrays), mesh=mesh, in_specs=placed,
            out_specs=(P(), P(), P(), P(), P()), check_vma=False,
        )(images, labels, weights, first_moment, second_moment)

    return step
```

```python
import functools
import math

import jax
import jax.numpy as jnp
from jax import lax
from jax.experimental import pallas as pl
from jax.experimental.pallas import tpu as pltpu
from jax.sharding import PartitionSpec as P

C1 = 32
C2 = 64
C3 = 128
CG = 32
CLS = 3
STEP = 10

EPS_NORM = 1e-05
CLIP_NORM = 0.005
LEARN_RATE = 0.02
BETA_ONE = 0.9
BETA_TWO = 0.999
ADAM_EPS = 1e-08
DECAY_RATE = 0.01

BF = jnp.bfloat16
F32 = jnp.float32
AXES = ("depth", "height")
WIDTHS = (C1, C2, C2, C3, C2, C2)
NORM_AT = (0, 32, 96, 160, 288, 352)
VOXELS = 18432
PAD = 160
ROWS = 6552
ROW_FIRST, ROW_SECOND, ROW_THIRD, ROW_COARSE = 0, 8, 440, 1304
ROW_MERGE, ROW_FINAL, ROW_GATE_SKIP, ROW_GATE_COARSE, ROW_TAIL = 3032, 5624, 6488, 6504, 6536
TAIL_AT = 836448
TAIL_LEN = 1479
T_GATE_BIAS, T_SCORE, T_SCORE_BIAS, T_HEAD_FINE, T_BIAS_FINE = 0, 32, 64, 65, 257
T_HEAD_COARSE, T_BIAS_COARSE, T_GAINS, T_SHIFTS = 260, 644, 647, 1063


class Sizes:
    def __init__(self, mesh_depth, mesh_height, local_z, local_y, width):
        self.D, self.H, self.lz, self.ly = mesh_depth, mesh_height, local_z, local_y
        self.planes = mesh_depth * local_z
        self.PY = mesh_height * local_y
        self.V = self.PY * width
        self.nb = self.V // 128
        self.half = self.nb // 2
        self.nbc = self.nb // 4
        self.Vc = self.V // 4
        self.total = self.planes * self.V
        self.G = 2
        while (self.planes // self.G + 2) * self.V > VOXELS:
            self.G *= 2
        self.Z = self.planes // self.G
        self.Zc = self.Z // 2
        self.ZP = -(-(self.Z + 4) // 16) * 16
        self.DP = self.planes - self.Z + self.ZP + 8
        self.two = self.G == 2
        self.share = 4 if mesh_depth * mesh_height // self.G % 4 == 0 else 1


def dot(left, right):
    return lax.dot_general(left, right, (((1,), (0,)), ((), ())), preferred_element_type=F32)


def dot_nt(left, right):
    return lax.dot_general(left, right, (((1,), (1,)), ((), ())), preferred_element_type=F32)


def ds(start, size, multiple=16):
    return pl.ds(start if isinstance(start, int) else pl.multiple_of(start, multiple), size)


def cols(k):
    return slice(k * 128, (k + 1) * 128)


def lanes(channels):
    return lax.broadcasted_iota(jnp.int32, (channels, 128), 1)


def sigmoid(value):
    return 0.5 * jnp.tanh(0.5 * value) + 0.5


def roll(value, steps):
    return pltpu.roll(value, steps % 128, axis=1)


def split_dot(value, matrix):
    high = value.astype(BF)
    low = (value - high.astype(F32)).astype(BF)
    return dot(high, matrix) + dot(low, matrix)


def norm_coefs(sums, gain, shift, channels, count):
    mean = jnp.sum(sums[:channels], axis=1, keepdims=True) / count
    square = jnp.sum(sums[channels : 2 * channels], axis=1, keepdims=True) / count
    inv = lax.rsqrt(square - mean * mean + EPS_NORM)
    full = (channels, 128)
    mean, inv = jnp.broadcast_to(mean, full), jnp.broadcast_to(inv, full)
    factor = inv * gain
    return mean, inv, factor, shift - mean * factor


def grad_coefs(sums, mean, inv, factor, channels, count):
    total = jnp.sum(sums[:channels], axis=1, keepdims=True) / count
    cross = jnp.sum(sums[channels : 2 * channels], axis=1, keepdims=True) / count
    slope = factor * cross * inv
    return slope, slope * mean - factor * total


def run(steps):
    for unused in steps:
        pass


def interleave(first, second, ratio):
    first, second = iter(first), iter(second)
    done = object()
    one = two = None
    while one is not done or two is not done:
        one = next(first, done)
        for unused in range(ratio):
            two = next(second, done)


def place_windows(p_ref, bases, rows, offset, blocks, seg):
    run(window_steps(p_ref, bases, rows, offset, blocks, seg))


def window_steps(p_ref, bases, rows, offset, blocks, seg):
    channels, count = blocks[0].shape[0], len(blocks)
    lane = lanes(channels)
    inner = lane & (seg - 1)
    zero = jnp.zeros((channels, 128), BF)
    blocks = [v.astype(BF) for v in blocks]
    for c in range(3):
        if c == 0:
            low = [jnp.where(inner == 0, zero, roll(v, 1)) for v in blocks]
        elif c == 1:
            low = blocks
        else:
            low = [jnp.where(inner == seg - 1, zero, roll(v, 127)) for v in blocks]
        before = jnp.where(lane < seg, zero, roll(low[-1], seg))
        after = jnp.where(lane >= 128 - seg, zero, roll(low[0], 128 - seg))
        extended = [before] + low + [after]
        for b in range(3):
            for k in range(count):
                for base in bases:
                    p_ref[ds(base + (3 * b + c) * rows + offset, channels), cols(k)] = extended[k + b]
            yield


def pack_wide(out, wide, rows):
    half = rows // 2
    out[:rows, :] = wide[:, :128]
    low = jnp.concatenate([wide[:half, 128:], wide[half:, 128:]], axis=1)
    out[rows : rows + half, :] = low


def unpack_wide(full, full_b, share, width, taps_out, packed, start, rows):
    half = rows // 2
    for m in range(0, rows, 8):
        at = m // width * taps_out + share * width + m % width
        full[at : at + 8, :] = packed[start + m : start + m + 8, :]
        low = start + rows + m % half
        low = packed[low : low + 8, :]
        full_b[at : at + 8, :] = low if m < half else roll(low, 64)


def share_steps(q_ref, bases, share, index, blocks, seg):
    if share == 1:
        return
    width = blocks[0].shape[0] // share
    picked = []
    for value in blocks:
        value = value.astype(BF)
        part = value[:width]
        for k in range(1, share):
            part = jnp.where(index == k, value[k * width : (k + 1) * width], part)
        picked.append(part)
    yield from window_steps(q_ref, tuple(base // share for base in bases), width, 0, picked, seg)


def unrolled(count, times, body):
    while count % times:
        times -= 1

    def step(t, carry):
        for r in range(times):
            body(times * t + r)
        return carry

    if count == times:
        for i in range(count):
            body(i)
    else:
        lax.fori_loop(0, count // times, step, 0)


def fold_sums(values):
    total = values[0]
    for value in values[1:]:
        total = total + value
    return total


CHUNK = 4


class Far:
    def __init__(self, array, base=None):
        self.array, self.base = array, base


class Held:
    def __init__(self, array):
        self.array = array


class Copied:
    def __init__(self, source, target, sems, base):
        self.target, self.copies = target, []
        self.source, self.sems, self.base = source, sems, base

    def copy(self, c):
        if self.base is None:
            return pltpu.make_async_copy(self.source, self.target, self.sems.at[0])
        span = pl.ds(self.base + c * CHUNK, CHUNK)
        return pltpu.make_async_copy(self.source.at[span], self.target.at[span], self.sems.at[c])

    def __getitem__(self, at):
        return self.target[at]

    @property
    def shape(self):
        return self.target.shape


def need(c, *refs):
    for ref in refs:
        if isinstance(ref, Copied):
            ref.copy(c).wait()


def kernel_call(body, meta, ins, outs, scratch=(), far_outs=False, hbm_outs=(), room=12, us=10):
    def size(shape, dtype):
        return math.prod(shape[:-1]) * (-(-shape[-1] // 128) * 128) * jnp.dtype(dtype).itemsize

    scratch = list(scratch)
    own = len(scratch)
    hbm = range(len(outs)) if far_outs else hbm_outs
    held = [isinstance(a, Held) for a in ins]
    far = [a if isinstance(a, (Far, Held)) else None for a in ins]
    arrays = [
        a if f is None else pltpu.with_memory_space_constraint(a.array, pltpu.HBM) for a, f in zip(ins, far)
    ]
    far = [None if h else f for f, h in zip(far, held)]
    chunks = []
    for a in far:
        if a is not None:
            count = 1 if a.base is None else (a.array.shape[0] - 2 * a.base) // CHUNK
            chunks.append(count)
            scratch += [pltpu.VMEM(a.array.shape, a.array.dtype), pltpu.SemaphoreType.DMA((count,))]
    if far_outs:
        scratch += [pltpu.VMEM(*o) for o in outs] + [pltpu.SemaphoreType.DMA((len(outs),))]

    def wrapped(meta_ref, *refs):
        in_refs, out_refs = refs[: len(ins)], refs[len(ins) : len(ins) + len(outs)]
        own_refs, extra = refs[len(ins) + len(outs) :][:own], list(refs[len(ins) + len(outs) + own :])
        given, whole = [], []
        for a, h, ref in zip(far, held, in_refs):
            if h:
                continue
            if a is None:
                given.append(ref)
                continue
            target, sems = extra.pop(0), extra.pop(0)
            copied = Copied(ref, target, sems, a.base)
            if a.base is None:
                copied.copy(0).start()
                whole.append(copied)
                given.append(target)
            else:
                given.append(copied)
        for copied in given:
            if isinstance(copied, Copied):
                for c in range(copied.sems.shape[0]):
                    copied.copy(c).start()
        for copied in whole:
            copied.copy(0).wait()
        if not far_outs:
            body(meta_ref, *given, *out_refs, *own_refs)
            return
        buffers, sems = extra[:-1], extra[-1]
        copies = [
            pltpu.make_async_copy(source, target, sems.at[index])
            for index, (source, target) in enumerate(zip(buffers, out_refs))
        ]
        body(lambda index: copies[index].start(), meta_ref, *given, *buffers, *own_refs)
        for copy in copies:
            copy.wait()

    vmem = sum(size(x.shape, x.dtype) for x in scratch if getattr(x, "memory_space", None) == pltpu.VMEM) + (room << 20)
    return pl.pallas_call(
        wrapped,
        out_shape=[pltpu.HBM(*o) if k in hbm else jax.ShapeDtypeStruct(*o) for k, o in enumerate(outs)],
        in_specs=[pl.BlockSpec(memory_space=pltpu.SMEM)]
        + [pl.BlockSpec(memory_space=pltpu.HBM if a or h else pltpu.VMEM) for a, h in zip(far, held)],
        out_specs=[pl.BlockSpec(memory_space=pltpu.HBM if k in hbm else pltpu.VMEM) for k in range(len(outs))],
        scratch_shapes=scratch,
        compiler_params=pltpu.CompilerParams(vmem_limit_bytes=min(vmem, 63 << 20)),
        cost_estimate=pl.CostEstimate(flops=us * 1000000000, bytes_accessed=1000, transcendentals=0),
    )(meta, *arrays)


def prep_body(z, leave, meta, flat, tail, big, second, third, coarse, merge, final, b_second, b_third,
              b_coarse, b_merge, b_final, gate, gate_t, head, head_t, gains, shifts, stage, stage_b):
    def unroll(row, taps_out, width):
        count = taps_out * width // 128
        if width == 192:
            rows = count // 3
            one, two, three = (flat[pl.ds(row + j, rows, stride=3), :] for j in range(3))
            left = lanes(rows) < 64
            turned = roll(three, 64)
            stage[pl.ds(0, rows, stride=2), :] = one
            stage_b[pl.ds(0, rows, stride=2), :] = two
            stage[pl.ds(1, rows, stride=2), :] = jnp.where(left, roll(two, 64), turned)
            stage_b[pl.ds(1, rows, stride=2), :] = turned
        else:
            pack = 128 // width
            block = flat[row : row + count, :]
            for j in range(pack):
                stage[pl.ds(j, count, stride=pack), :] = roll(block, -j * width) if j else block

    def staged(at, count, width):
        if width <= 128:
            return stage[at : at + count, :width]
        return jnp.concatenate([stage[at : at + count, :], stage_b[at : at + count, : width - 128]], axis=1)

    def forward(out_c, in_c):
        return [
            jnp.concatenate(
                [staged((9 * a + t) * out_c, out_c, in_c) for t in range(9)],
                axis=1,
            )
            for a in range(3)
        ]

    def backward_plane(out_c, in_c, a):
        at = 26 - 9 * a
        return jnp.concatenate(
            [staged((at - t) * out_c, out_c, in_c) for t in range(9)], axis=0
        ).T

    def backward(out_c, in_c):
        return jnp.concatenate(
            [staged((26 - t) * out_c, out_c, in_c) for t in range(27)], axis=0
        ).T

    def double(ref, full, copies, step):
        rows, width = full.shape
        for r in range(copies):
            parts = []
            if r:
                parts.append(jnp.zeros((rows, r * step), F32))
            parts.append(full)
            if r < copies - 1:
                parts.append(jnp.zeros((rows, (copies - 1 - r) * step), F32))
            ref[r * rows : (r + 1) * rows, :] = jnp.concatenate(parts, axis=1).astype(BF)

    block = flat[0:8, :]
    for j in range(4):
        stage[pl.ds(j, 8, stride=4), :] = roll(block, -j * 32) if j else block
    taps = stage[0:32, :32].T.astype(BF)
    tall = jnp.concatenate([taps] * (z.Z + 2), axis=0)
    shape = ((z.Z + 2) * C1, 9 * z.ZP)
    source = lax.broadcasted_iota(jnp.int32, (32, 9 * z.ZP), 0)
    target = lax.broadcasted_iota(jnp.int32, (32, 9 * z.ZP), 1) // z.ZP
    gap = lax.rem(lax.broadcasted_iota(jnp.int32, shape, 1), z.ZP) - (
        lax.broadcasted_iota(jnp.int32, shape, 0) // C1
    )
    total = jnp.zeros(shape, F32)
    for a in range(3):
        spread = dot(tall, jnp.where(source == target + 5 + 9 * a, 1.0, 0.0).astype(BF))
        total = total + jnp.where(gap == a, spread, 0.0)
    big[...] = total.astype(BF)
    leave(0)

    for index, row, ref, b_ref, width in (
        (1, ROW_SECOND, second, b_second, C1),
        (2, ROW_THIRD, third, b_third, C2),
        (5, ROW_FINAL, final, b_final, C2),
    ):
        unroll(row, 27 * C2, width)
        ref[...] = jnp.concatenate(forward(C2, width), axis=0).astype(BF)
        for a in range(3):
            b_ref[a * width : (a + 1) * width, :] = backward_plane(C2, width, a).astype(BF)
        leave(index)
        leave(10 if index == 5 else index + 5)
    unroll(ROW_COARSE, 27 * C3, C2)
    coarse[...] = jnp.concatenate(forward(C3, C2), axis=1).astype(BF)
    double(b_coarse, backward(C3, C2), 2, 9 * C3)
    leave(3)
    leave(8)
    unroll(ROW_MERGE, 27 * C2, C2 + C3)
    merge[...] = jnp.concatenate(forward(C2, C2 + C3), axis=0).astype(BF)
    b_merge[...] = backward(C2, C2 + C3).astype(BF)
    leave(4)
    leave(9)

    unroll(ROW_GATE_SKIP, CG, C2)
    gate_skip = stage[:CG, :C2]
    gate_coarse = flat[ROW_GATE_COARSE : ROW_GATE_COARSE + CG, :]
    lane = lanes(C3)

    def columns(at, channels):
        value = jnp.zeros((channels, 128), F32)
        for k in range(CLS):
            piece = tail[at + k * channels : at + (k + 1) * channels, :]
            value = jnp.where(lane[:channels] == k, piece, value)
        return value

    fine_cols = columns(T_HEAD_FINE, C2)
    coarse_cols = columns(T_HEAD_COARSE, C3)
    head_t[...] = fine_cols[:, :16].astype(BF)
    head[...] = fine_cols.T[:16, :].astype(BF)
    rows = jnp.concatenate(
        [
            jnp.concatenate([gate_skip, gate_coarse], axis=1),
            jnp.concatenate([jnp.zeros((16, C2), F32), coarse_cols.T[:16, :]], axis=1),
        ],
        axis=0,
    )
    gate[...] = rows.astype(BF)
    gate_t[...] = rows.T.astype(BF)
    gains[...] = tail[T_GAINS : T_GAINS + 416, :]
    shifts[...] = tail[T_SHIFTS : T_SHIFTS + 416, :]
    for index in range(11, 17):
        leave(index)


def prepare(z, meta, flat, tail):
    outs = [
        (((z.Z + 2) * C1, 9 * z.ZP), BF),
        ((192, 9 * C1), BF),
        ((192, 9 * C2), BF),
        ((128, 27 * C2), BF),
        ((192, 9 * 192), BF),
        ((192, 9 * C2), BF),
        ((96, 9 * C2), BF),
        ((192, 9 * C2), BF),
        ((128, 36 * C3), BF),
        ((192, 27 * C2), BF),
        ((192, 9 * C2), BF),
        ((48, 192), BF),
        ((192, 48), BF),
        ((16, C2), BF),
        ((C2, 16), BF),
        ((416, 128), F32),
        ((416, 128), F32),
    ]
    names = (
        "big", "second", "third", "coarse", "merge", "final", "b_second", "b_third", "b_coarse",
        "b_merge", "b_final", "gate", "gate_t", "head", "head_t", "gains", "shifts",
    )
    out = kernel_call(
        lambda *refs: prep_body(z, *refs), meta, [flat, tail], outs,
        [pltpu.VMEM((27 * C3, 128), F32), pltpu.VMEM((27 * C2, 128), F32)], far_outs=True,
    )
    return dict(zip(names, out))


def layer_gain(gains, layer):
    return gains[NORM_AT[layer] : NORM_AT[layer] + WIDTHS[layer], :]


def send_planes(z, meta, h_refs, source, count, planes):
    if z.two:
        start = jnp.where(meta[0] == 0, planes - count, 0)
        for j in range(count):
            h_refs[0][j] = source(start + j).astype(BF)
    else:
        for j in range(count):
            h_refs[0][j] = source(j).astype(BF)
            h_refs[1][j] = source(planes - count + j).astype(BF)


UNROLL = CHUNK


def flow(z, build, consume, ratio, fetch=(), leave=None):
    run(build(0, 0, 0))

    def body(t, carry):
        need(t, *fetch)
        for r in range(UNROLL):
            zp = UNROLL * t + r
            interleave(consume(zp, r % 2), build(zp + 1, (r + 1) % 2, None), ratio)
        if leave:
            leave(t)
        return carry

    lax.fori_loop(0, z.Z // UNROLL, body, 0)
    interleave(consume(z.Z, 0), build(z.Z + 1, 1, 1), ratio)
    run(consume(z.Z + 1, 1))


def scatter(zp, weight, window, width, parts, nb, finish):
    part_one, part_two = parts
    at = zp - 2 if isinstance(zp, int) else jnp.maximum(zp - 2, 0)
    for n in range(nb // 2):
        result = dot(weight[...], window[:, 256 * n : 256 * (n + 1)])
        for k in (2 * n, 2 * n + 1):
            piece = result[:, cols(k - 2 * n)]
            finish(at, k, part_one[:, cols(k)] + piece[2 * width :])
            part_one[:, cols(k)] = part_two[:, cols(k)] + piece[width : 2 * width]
            part_two[:, cols(k)] = piece[:width]
        yield


def add_sums(zp, st_ref, channels, first, second):
    first, second = fold_sums(first), fold_sums(second)
    if not isinstance(zp, int):
        first, second = jnp.where(zp >= 2, first, 0.0), jnp.where(zp >= 2, second, 0.0)
    st_ref[:channels, :] += first
    st_ref[channels : 2 * channels, :] += second


def convolve(z, weight, p_ref, parts, rows, channels, y_ref, st_ref, build, leave=None, ratio=3):
    st_ref[...] = jnp.zeros(st_ref.shape, F32)
    for part in parts:
        part[...] = jnp.zeros(part.shape, F32)

    def consume(zp, slot):
        values = []

        def finish(at, k, value):
            y_ref[at, :, cols(k)] = value
            values.append(value)

        window = p_ref.at[slot * rows : (slot + 1) * rows, :]
        yield from scatter(zp, weight, window, channels, parts, z.nb, finish)
        add_sums(zp, st_ref, channels, values, [v * v for v in values])

    flow(z, build, consume, ratio, leave=leave)


def mine_body(z, meta, images, labels, out, rows):
    for i in range(z.lz):
        rows[i * z.ly : (i + 1) * z.ly, :] = jnp.concatenate(
            [images[0, i], labels[0, i].astype(F32)], axis=1
        )
    value = rows[...].astype(BF)
    for i in range(out.shape[0]):
        out[i] = value


def first_body(z, meta, recv, big, y_ref, st_ref, p_ref, lab_ref, wide, rows):
    wide[...] = recv[...].astype(F32)
    rows[...] = jnp.zeros(rows.shape, F32)
    per = z.lz * z.ly
    for hh in range(z.H):
        for yy in range(z.ly):
            for zz in range(z.lz):
                rows[pl.ds((hh * z.ly + yy) * z.DP + 2 + zz, z.D, stride=z.lz), :] = wide[
                    pl.ds(hh * per + zz * z.ly + yy, z.D, stride=z.H * per), :
                ]
    lane = lanes(z.ZP)
    start = pl.multiple_of(meta[0] * z.Z // 8 * 8, 8)

    def source(y):
        if z.Z % 8 == 0:
            return rows[pl.ds(pl.multiple_of(y * z.DP + start, 8), z.ZP), :]
        block = rows[pl.ds(pl.multiple_of(y * z.DP + start, 8), z.ZP + 8), :]
        return jnp.where(lax.rem(meta[0], 2) == 0, block[: z.ZP], block[4 : z.ZP + 4])

    blocks = []
    hits = [jnp.zeros((1, 128), F32) for unused in range(CLS)]
    for k in range(z.nb):
        one, two = source(k), source(k + z.nb)
        blocks.append(jnp.where(lane < 64, one, roll(two, 64)))
        label = jnp.where(lane < 64, roll(one, 64), two)[2 : 2 + z.Z]
        for i in range(z.Z):
            lab_ref[i, :, cols(k)] = jnp.broadcast_to(label[i : i + 1], (8, 128))
        for c in range(CLS):
            hits[c] = hits[c] + jnp.sum(
                jnp.where(label == float(c), 1.0, 0.0), axis=0, keepdims=True
            )
    place_windows(p_ref, (0,), z.ZP, 0, blocks, 64)
    y_ref[...] = dot(big[...], p_ref[...])
    st_ref[...] = jnp.zeros(st_ref.shape, F32)

    def step(i):
        values = [y_ref[ds(C1 + i * C1, C1), cols(k)] for k in range(z.nb)]
        st_ref[:C1, :] += fold_sums(values)
        st_ref[C1 : 2 * C1, :] += fold_sums([v * v for v in values])

    unrolled(z.Z, 4, step)
    row = lax.broadcasted_iota(jnp.int32, (8, 128), 0)
    counts = jnp.zeros((8, 128), F32)
    for c in range(CLS):
        counts = jnp.where(row == c, hits[c], counts)
    st_ref[2 * C1 : 2 * C1 + 8, :] = counts


def second_body(z, meta, y1, sa, sb, gains, shifts, weight, y_ref, st_ref, *rest):
    h_refs, p_ref, parts = rest[:-3], rest[-3], rest[-2:]
    unused, unused, factor, level = norm_coefs(
        sa[...] + sb[...], layer_gain(gains, 0), layer_gain(shifts, 0), C1, z.total
    )

    def build(zp, slot, edge):
        blocks = []
        for k in range(z.nb):
            value = y1[ds(zp * C1, C1), cols(k)] * factor + level
            value = value * sigmoid(value)
            blocks.append(value if edge is None else jnp.where(meta[1 + edge] > 0, value, 0.0))
            if k % 2:
                yield
        yield from window_steps(p_ref, (slot * 9 * C1,), C1, 0, blocks, 64)

    convolve(z, weight, p_ref, parts, 9 * C1, C2, y_ref, st_ref, build)
    send_planes(z, meta, h_refs, lambda i: y_ref[i], 1, z.Z)


def middle_body(z, layer, send, meta, y_in, lo, hi, sa, sb, gains, shifts, weight, y_ref, st_ref, *rest):
    h_refs, p_ref, parts = rest[:-3], rest[-3], rest[-2:]
    unused, unused, factor, level = norm_coefs(
        sa[...] + sb[...], layer_gain(gains, layer), layer_gain(shifts, layer), C2, z.total
    )

    def build(zp, slot, edge):
        if edge is None:
            get = lambda k: y_in[zp - 1, :, cols(k)]
        else:
            get = lambda k: (lo, hi)[edge][0, :, cols(k)].astype(F32)
        blocks = []
        for k in range(z.nb):
            value = get(k) * factor + level
            value = value * sigmoid(value)
            blocks.append(value if edge is None else jnp.where(meta[1 + edge] > 0, value, 0.0))
            if k % 2:
                yield
        yield from window_steps(p_ref, (slot * 9 * C2,), C2, 0, blocks, 64)

    convolve(z, weight, p_ref, parts, 9 * C2, C2, y_ref, st_ref, build)
    send_planes(z, meta, h_refs, lambda i: y_ref[i], send, z.Z)


def pool_matrix(entries):
    row = lax.broadcasted_iota(jnp.int32, (256, 128), 0)
    col = lax.broadcasted_iota(jnp.int32, (256, 128), 1)
    same = (col // 32) == 2 * (lax.rem(row, 128) // 64) + row // 128
    return jnp.where(same, entries(lax.rem(row, 64), lax.rem(col, 32)), 0.0).astype(BF)


def mean_entries(fine, coarse):
    return jnp.where(fine // 2 == coarse, 0.125, 0.0)


def lift_entries(fine, coarse):
    near = fine // 2
    other = jnp.clip(jnp.where(lax.rem(fine, 2) == 0, near - 1, near + 1), 0, 31)
    return jnp.where(coarse == near, 0.75, 0.0) + jnp.where(coarse == other, 0.25, 0.0)


def coarse_body(z, meta, y3, lo, hi, sa, sb, gains, shifts, weight, skip, pooled, y_ref, st_ref, *rest):
    h_refs, p_ref = rest[:-1], rest[-1]
    unused, unused, factor, level = norm_coefs(
        sa[...] + sb[...], layer_gain(gains, 2), layer_gain(shifts, 2), C2, z.total
    )
    matrix = pool_matrix(mean_entries)

    def plane(jp, gets, valid, skip_at):
        sums = []
        for i in range(z.half):
            parts = []
            for index, get in enumerate(gets):
                for k in (2 * i, 2 * i + 1):
                    value = get(k) * factor + level
                    value = value * sigmoid(value)
                    if valid is not None:
                        value = jnp.where(valid > 0, value, 0.0)
                    if skip_at[index] is not None:
                        skip[skip_at[index], :, cols(k)] = value.astype(BF)
                    parts.append(value)
            sums.append(fold_sums(parts))
        blocks = []
        for kc in range(z.nbc):
            pair = jnp.concatenate([sums[kc], sums[kc + z.nbc]], axis=1)
            blocks.append(split_dot(pair, matrix))
        for kc in range(z.nbc):
            pooled[jp, :, cols(kc)] = blocks[kc].astype(BF)
        place_windows(p_ref, (jp * (9 * C2),), C2, 0, blocks, 32)

    plane(0, [lambda k: lo[0, :, cols(k)].astype(F32), lambda k: lo[1, :, cols(k)].astype(F32)],
          meta[1], (None, 0))
    plane(z.Zc + 1, [lambda k: hi[0, :, cols(k)].astype(F32), lambda k: hi[1, :, cols(k)].astype(F32)],
          meta[2], (z.Z + 1, None))

    def step(j):
        plane(j + 1, [lambda k: y3[2 * j, :, cols(k)], lambda k: y3[2 * j + 1, :, cols(k)]],
              None, (2 * j + 1, 2 * j + 2))

    unrolled(z.Zc, 4, step)
    st_ref[...] = jnp.zeros(st_ref.shape, F32)

    def conv(j):
        result = dot(weight[...], p_ref[ds(j * (9 * C2), 27 * C2), :])
        y_ref[j] = result
        values = [result[:, cols(k)] for k in range(z.nbc)]
        st_ref[:C3, :] += fold_sums(values)
        st_ref[C3 : 2 * C3, :] += fold_sums([v * v for v in values])

    unrolled(z.Zc, 8, conv)
    send_planes(z, meta, h_refs, lambda i: y_ref[i], 1, z.Zc)


def merge_body(z, meta, yc, lo, hi, sa, sb, gains, shifts, tail, skip, gate, weight,
               lifted_out, pre_out, logit_out, y_ref, st_ref, *rest):
    h_refs = rest[:-10]
    p_ref, t_ref, act, mixed, part_one, part_two, lifted, pre_ref, logit_ref, sems = rest[-10:]
    unused, unused, factor, level = norm_coefs(
        sa[...] + sb[...], layer_gain(gains, 3), layer_gain(shifts, 3), C3, z.total // 8
    )
    matrix = pool_matrix(lift_entries).astype(F32).T.astype(BF)
    n = z.half

    def coarse_act(get):
        out = []
        for k in range(z.nbc):
            value = get(k) * factor + level
            out.append((value * sigmoid(value)).astype(BF))
        return out

    for k, value in enumerate(coarse_act(lambda k: lo[0, :, cols(k)].astype(F32))):
        act[0, :, cols(k)] = value
    for k, value in enumerate(coarse_act(lambda k: hi[0, :, cols(k)].astype(F32))):
        act[z.Zc + 1, :, cols(k)] = value

    def own(j, carry):
        for k, value in enumerate(coarse_act(lambda k: yc[j, :, cols(k)])):
            act[j + 1, :, cols(k)] = value
        return carry

    lax.fori_loop(0, z.Zc, own, 0)

    @pl.when(meta[1] == 0)
    def low_edge():
        act[0] = act[1]

    @pl.when(meta[2] == 0)
    def high_edge():
        act[z.Zc + 1] = act[z.Zc]

    def spread(jp, slot):
        rows = [None] * n
        for k in range(z.nbc):
            both = dot(act[jp, :, cols(k)], matrix)
            rows[k], rows[k + z.nbc] = both[:, :128], both[:, 128:]
        lane = lanes(C3)
        first, last = rows[0], rows[n - 1]
        before = jnp.where(lane < 64, first, roll(last, 64))
        after = jnp.where(lane < 64, roll(first, 64), last)
        extended = [before] + rows + [after]
        for i in range(n):
            t_ref[slot, :, cols(2 * i)] = 0.25 * extended[i] + 0.75 * extended[i + 1]
            t_ref[slot, :, cols(2 * i + 1)] = 0.75 * extended[i + 1] + 0.25 * extended[i + 2]
            if i % 2:
                yield

    run(spread(0, 0))
    bias = tail[T_GATE_BIAS : T_GATE_BIAS + CG, :]
    score = tail[T_SCORE : T_SCORE + CG, :]
    score_bias = tail[T_SCORE_BIAS : T_SCORE_BIAS + 1, :]

    def build(zp, slot, edge):
        turn = zp % 2 if isinstance(zp, int) else 1 - (slot + 1) % 2
        wa, wb = (0.75, 0.25) if turn == 0 else (0.25, 0.75)
        old = (zp // 2) % 2 if isinstance(zp, int) else lax.rem(zp // 2, 2)
        new = 1 - old
        if turn == 0:
            yield from spread(zp // 2 + 1, new)
        valid = None if edge is None else meta[1 + edge]
        base, row = slot * 9 * 192, slot * 192
        mixed[row : row + C2, :] = skip[zp]
        wide = []
        for k in range(z.nb):
            value = (wa * t_ref[old, :, cols(k)] + wb * t_ref[new, :, cols(k)]).astype(BF)
            mixed[row + C2 : row + 192, cols(k)] = value
            lifted[zp, :, cols(k)] = value
            value = value.astype(F32)
            wide.append(value if valid is None else jnp.where(valid > 0, value, 0.0))
            if k % 2:
                yield
        gated = []
        for n in range(z.half):
            rows = dot(gate[...], mixed[row : row + 192, 256 * n : 256 * (n + 1)])
            logit_ref[zp, :, 256 * n : 256 * (n + 1)] = rows[CG:]
            for k in (2 * n, 2 * n + 1):
                pre = rows[:CG, cols(k - 2 * n)] + bias
                pre_ref[zp, :, cols(k)] = pre
                inner = pre * sigmoid(pre)
                alpha = sigmoid(jnp.sum(score * inner, axis=0, keepdims=True) + score_bias)
                if valid is not None:
                    alpha = jnp.where(valid > 0, alpha, 0.0)
                gated.append(mixed[row : row + C2, cols(k)].astype(F32) * alpha)
            yield
        yield from window_steps(p_ref, (base,), 192, C2, wide, 64)
        yield from window_steps(p_ref, (base,), 192, 0, gated, 64)

    pairs = ((lifted, lifted_out), (pre_ref, pre_out), (logit_ref, logit_out))

    def leaving(t):
        span = pl.ds(4 * t + 1, 4)
        return [
            pltpu.make_async_copy(a.at[span], b.at[span], sems.at[n, t]) for n, (a, b) in enumerate(pairs)
        ]

    def leave(t):
        for copy in leaving(t):
            copy.start()

    convolve(z, weight, p_ref, (part_one, part_two), 9 * 192, C2, y_ref, st_ref, build, leave, ratio=5)
    send_planes(z, meta, h_refs, lambda i: y_ref[i], 1, z.Z)
    for t in range(z.Z // 4):
        for copy in leaving(t):
            copy.wait()


def heads_body(z, meta, yf, sa, sb, ca, cb, lab, logit_ref, gains, shifts, tail, head, head_t,
               d_ref, bs_ref, small, gc_ref, *rest):
    h_refs, acts = rest[:-1], rest[-1]
    mean, inv, factor, level = norm_coefs(
        sa[...] + sb[...], layer_gain(gains, 5), layer_gain(shifts, 5), C2, z.total
    )
    counts = jnp.sum(ca[2 * C1 :] + cb[2 * C1 :], axis=1, keepdims=True)
    row = lax.broadcasted_iota(jnp.int32, (8, 1), 0)
    everything = jnp.sum(jnp.where(row < CLS, counts, 0.0), axis=0, keepdims=True)
    class_weight = jnp.where(row < CLS, 2.0 * everything / (3.0 * counts + everything), 0.0)
    weight_total = jnp.sum(counts * class_weight, axis=0, keepdims=True)
    scaled = class_weight / weight_total
    scaled = jnp.concatenate([scaled, jnp.zeros((8, 1), F32)], axis=0)
    rows16 = lax.broadcasted_iota(jnp.int32, (16, 128), 0)
    pad13 = jnp.zeros((13, 128), F32)
    bias_fine = jnp.concatenate([tail[T_BIAS_FINE : T_BIAS_FINE + 3, :], pad13], axis=0)
    bias_coarse = jnp.concatenate([tail[T_BIAS_COARSE : T_BIAS_COARSE + 3, :], pad13], axis=0)
    bs_ref[...] = jnp.zeros(bs_ref.shape, F32)
    small[...] = jnp.zeros(small.shape, F32)

    def logit_grad(logits, label, times):
        logits = jnp.where(rows16 < CLS, logits, -1e30)
        top = jnp.max(logits, axis=0, keepdims=True)
        terms = jnp.where(rows16 < CLS, jnp.exp(logits - top), 0.0)
        soft = terms / jnp.sum(terms, axis=0, keepdims=True)
        onehot = jnp.where(rows16.astype(F32) == label, 1.0, 0.0)
        weight = jnp.sum(scaled * onehot, axis=0, keepdims=True)
        return ((soft - onehot) * (weight * times)).astype(BF)

    def step(i, slot):
        act = acts.at[slot * C2 : (slot + 1) * C2, :]
        for k in range(z.nb):
            value = yf[i, :, cols(k)] * factor + level
            act[:, cols(k)] = (value * sigmoid(value)).astype(BF)
        logits = dot(head[...], act[...])
        fine, bias_sum, coarse_sum = [], [], []
        for k in range(z.nb):
            label = lab[i, 0:1, cols(k)]
            grad = logit_grad(logits[:, cols(k)] + bias_fine, label, 1.0)
            fine.append(grad)
            bias_sum.append(grad.astype(F32))
            grad = logit_grad(logit_ref[i + 1, :, cols(k)] + bias_coarse, label, 0.5)
            gc_ref[i, :, cols(k)] = grad
            coarse_sum.append(grad.astype(F32))
        fine = jnp.concatenate(fine, axis=1)
        small[:C2, :16] += dot_nt(act[...], fine)
        small[C2 : C2 + 16, :] += fold_sums(bias_sum)
        small[C2 + 16 : C2 + 32, :] += fold_sums(coarse_sum)
        back = dot(head_t[...], fine)
        parts, cross = [], []
        for k in range(z.nb):
            y = yf[i, :, cols(k)]
            pre = y * factor + level
            sig = sigmoid(pre)
            grad = back[:, cols(k)] * (sig * (1.0 + pre * (1.0 - sig)))
            d_ref[i, :, cols(k)] = grad
            parts.append(grad)
            cross.append(grad * ((y - mean) * inv))
        bs_ref[:C2, :] += fold_sums(parts)
        bs_ref[C2:, :] += fold_sums(cross)

    def four(t, carry):
        for r in range(4):
            step(4 * t + r, r)
        return carry

    lax.fori_loop(0, z.Z // 4, four, 0)
    send_planes(z, meta, h_refs, lambda i: d_ref[i], 1, z.Z)


def dy_builder(z, meta, layer, count, refs, p_ref, q_ref, share):
    d, d_lo, d_hi, y, y_lo, y_hi, sums, back, gains, shifts = refs
    channels = WIDTHS[layer]
    mean, inv, factor, unused = norm_coefs(
        sums, layer_gain(gains, layer), layer_gain(shifts, layer), channels, count
    )
    slope, level = grad_coefs(back, mean, inv, factor, channels, count)

    def build(zp, bases, edge):
        get_d, get_y = (lambda k: d[zp - 1, :, cols(k)]), (lambda k: y[zp - 1, :, cols(k)])
        if edge is not None:
            get_d = lambda k: (d_lo, d_hi)[edge][0, :, cols(k)].astype(F32)
            get_y = lambda k: (y_lo[y_lo.shape[0] - 1, :, cols(k)], y_hi[0, :, cols(k)])[edge].astype(F32)
        out = []
        for k in range(z.nb):
            value = factor * get_d(k) - slope * get_y(k) + level
            out.append(value if edge is None else jnp.where(meta[1 + edge] > 0, value, 0.0))
            if k % 2:
                yield
        yield from window_steps(p_ref, bases, channels, 0, out, 64)
        yield from share_steps(q_ref, bases, share, meta[3], out, 64)

    def build_or_edge(zp, bases, last):
        out = []
        own = jnp.minimum(zp - 1, z.Z - 1)
        for k in range(z.nb):
            near_d = jnp.where(last, d_hi[0, :, cols(k)].astype(F32), d[own, :, cols(k)])
            near_y = jnp.where(last, y_hi[0, :, cols(k)].astype(F32), y[own, :, cols(k)])
            value = factor * near_d - slope * near_y + level
            out.append(jnp.where(jnp.logical_and(last, meta[2] == 0), 0.0, value))
            if k % 2:
                yield
        yield from window_steps(p_ref, bases, channels, 0, out, 64)
        yield from share_steps(q_ref, bases, share, meta[3], out, 64)

    build.or_edge = build_or_edge
    return build


def back_body(z, layer, below, y_base, share, meta, d, d_lo, d_hi, y, y_lo, y_hi, sa, sb, ba, bb,
              yb, ua, ub, gains, shifts, weight, *rest):
    d_ref, bs_ref, dk_out = rest[:3]
    h_refs, (p_ref, q_ref, x_ref, dk_ref), parts = rest[3:-6], rest[-6:-2], rest[-2:]
    make = dy_builder(z, meta, layer, z.total,
                       (d, d_lo, d_hi, y, y_lo, y_hi, sa[...] + sb[...], ba[...] + bb[...], gains, shifts),
                      p_ref, q_ref, share)
    width = WIDTHS[below]
    mean, inv, factor, level = norm_coefs(
        ua[...] + ub[...], layer_gain(gains, below), layer_gain(shifts, below), width, z.total
    )
    edge = jnp.zeros((2 * width, z.V), BF)
    x_ref[: 2 * width, :] = edge
    x_ref[(z.Z + 2) * width :, :] = edge
    bs_ref[...] = jnp.zeros(bs_ref.shape, F32)
    rows = 9 * WIDTHS[layer]
    part = rows // share
    dk_ref[...] = jnp.zeros(dk_ref.shape, F32)

    for part_ref in parts:
        part_ref[...] = jnp.zeros(part_ref.shape, F32)

    def build(zp, slot, edge):
        return make(zp, (slot * rows,), edge)

    def consume(zp, slot):
        if not isinstance(zp, int):
            for k in range(z.nb):
                pre = yb[zp + y_base, :, cols(k)] * factor + level
                x_ref[ds((zp + 2) * width, width), cols(k)] = (pre * sigmoid(pre)).astype(BF)
        sums, cross = [], []

        def finish(at, k, value):
            y_value = yb[at + y_base, :, cols(k)]
            pre = y_value * factor + level
            sig = sigmoid(pre)
            grad = value * (sig * (1.0 + pre * (1.0 - sig)))
            d_ref[at, :, cols(k)] = grad
            sums.append(grad)
            cross.append(grad * ((y_value - mean) * inv))

        yield from scatter(zp, weight, p_ref.at[slot * rows : (slot + 1) * rows, :], width, parts, z.nb, finish)
        add_sums(zp, bs_ref, width, sums, cross)
        if share == 1:
            window = p_ref[slot * rows : (slot + 1) * rows, :]
        else:
            window = q_ref[slot * part : (slot + 1) * part, :]
        dk_ref[...] += dot_nt(window, x_ref[ds(zp * width, 3 * width), :])

    flow(z, build, consume, 3, (d, y, yb))
    if width == C2:
        pack_wide(dk_out, dk_ref, part)
    else:
        dk_out[:, : 3 * width] = dk_ref[...]
    if h_refs:
        send_planes(z, meta, h_refs, lambda i: d_ref[i], 1, z.Z)


def merge_back_body(z, share, meta, d, d_lo, d_hi, y, y_lo, y_hi, sa, sb, ba, bb, skip, lifted, pre_ref, gc_ref,
                    yc, yc_lo, yc_hi, ua, ub, gains, shifts, tail, weight, gate_t,
                    gskip_out, gcoarse, bs_ref, dk_out, small, *rest):
    h_refs, (p_ref, q_ref, eg, x_ref, acc, dk_ref, gskip, sems) = rest[:-8], rest[-8:]
    build = dy_builder(z, meta, 4, z.total,
                       (d, d_lo, d_hi, y, y_lo, y_hi, sa[...] + sb[...], ba[...] + bb[...], gains, shifts),
                       p_ref, q_ref, share)
    score = tail[T_SCORE : T_SCORE + CG, :]
    score_bias = tail[T_SCORE_BIAS : T_SCORE_BIAS + 1, :]
    small[...] = jnp.zeros(small.shape, F32)
    dk_ref[...] = jnp.zeros(dk_ref.shape, F32)
    acc[...] = jnp.zeros(acc.shape, F32)
    n = z.half
    lane = lanes(C3)
    rows = 9 * C2
    part = 27 * C2 // share

    def plane(i, r4):
        start = r4 * rows
        turn = (r4 % 2) * 256
        side = (r4 % 2) * 48
        eg[side + CG : side + 48, :] = gc_ref[i]
        x_ref[turn + C2 : turn + 192, :] = lifted[i + 1]
        x_ref[turn + 192 : turn + 256, :] = skip[i + 1]
        wide, e_sum, s_sum, r_sum = [], [], [], []
        for q in range(z.half):
            span = slice(256 * q, 256 * (q + 1))
            result = dot(weight[...], p_ref[start : start + 3 * rows, span])
            alphas = []
            for k in (2 * q, 2 * q + 1):
                piece = result[:C2, cols(k - 2 * q)]
                pre = pre_ref[i + 1, :, cols(k)]
                sig = sigmoid(pre)
                inner = pre * sig
                alpha = sigmoid(jnp.sum(score * inner, axis=0, keepdims=True) + score_bias)
                near = skip[i + 1, :, cols(k)].astype(F32)
                grad = jnp.sum(piece * near, axis=0, keepdims=True)
                grad = grad * alpha * (1.0 - alpha)
                e = (score * grad * (sig * (1.0 + pre * (1.0 - sig)))).astype(BF)
                eg[side : side + CG, cols(k)] = e
                x_ref[turn : turn + C2, cols(k)] = (near * alpha).astype(BF)
                alphas.append(alpha)
                e_sum.append(e.astype(F32))
                s_sum.append(grad * inner)
                r_sum.append(grad)
            extra = dot(gate_t[...], eg[side : side + 48, span])
            for k in (2 * q, 2 * q + 1):
                at = cols(k - 2 * q)
                gskip[i, :, cols(k)] = result[:C2, at] * alphas[k - 2 * q] + extra[:C2, at]
                wide.append(result[C2:, at] + extra[C2:, at])
            yield
        small[192:224, :] += fold_sums(e_sum)
        small[224:256, :] += fold_sums(s_sum)
        small[256:257, :] += fold_sums(r_sum)
        low = [
            0.75 * (wide[2 * m] + wide[2 * m + 1])
            + (0.25 * wide[2 * m + 2] if m < n - 1 else 0.0)
            + (0.25 * wide[2 * m - 1] if m > 0 else 0.0)
            for m in range(n)
        ]
        before, after = 0.25 * wide[0], 0.25 * wide[-1]
        low[0] = low[0] + jnp.where(lane < 64, before, roll(after, 64))
        low[n - 1] = low[n - 1] + jnp.where(lane < 64, roll(before, 64), after)
        j, r = i // 2, r4 % 2
        for m in range(n):
            acc[j + 1, :, cols(m)] += 0.75 * low[m]
            acc[j + 2 * r, :, cols(m)] += 0.25 * low[m]
        yield
        if share == 1:
            window = p_ref[start : start + 3 * rows, :]
        else:
            window = q_ref[start // share : start // share + part, :]
        tall = jnp.concatenate([window, eg[side : side + 48, :]], axis=0)
        dk_ref[...] += dot_nt(tall, x_ref[turn : turn + 256, :])

    need(0, d, y)
    for zp in range(3):
        run(build(zp, (zp * rows,), 0 if zp == 0 else None))

    def four(t, carry):
        need(t, skip, lifted, pre_ref, gc_ref)
        for r in range(4):
            if r == 2:

                @pl.when(t + 1 < z.Z // 4)
                def fetch():
                    need(t + 1, d, y)

            at = (r + 3) % 4
            bases = (at * rows, (at + 4) * rows) if at < 2 else (at * rows,)
            zp = 4 * t + r + 3
            if r < 2:
                steps = build(zp, bases, None)
            else:
                steps = build.or_edge(zp, bases, zp == z.Z + 1)
            interleave(plane(4 * t + r, r), steps, 2)
        leaving(t).start()
        return carry

    def leaving(t):
        span = pl.ds(4 * t, 4)
        return pltpu.make_async_copy(gskip.at[span], gskip_out.at[span], sems.at[t])

    lax.fori_loop(0, z.Z // 4, four, 0)
    pack_wide(dk_out, dk_ref[:part, :192], part)
    tall = dk_ref[part:, :].T
    small[:C2, :48] = tall[192:]
    small[C2:192, :48] = tall[C2:192]

    matrix = pool_matrix(lift_entries)

    def shrink(jp, carry):
        for k in range(z.nbc):
            pair = jnp.concatenate([acc[jp, :, cols(k)], acc[jp, :, cols(k + z.nbc)]], axis=1)
            gcoarse[jp, :, cols(k)] = split_dot(pair, matrix)
        return carry

    lax.fori_loop(0, z.Zc + 2, shrink, 0)

    @pl.when(meta[1] == 0)
    def low_edge():
        gcoarse[1] += gcoarse[0]
        gcoarse[0] = jnp.zeros((C3, z.Vc), F32)

    @pl.when(meta[2] == 0)
    def high_edge():
        gcoarse[z.Zc] += gcoarse[z.Zc + 1]
        gcoarse[z.Zc + 1] = jnp.zeros((C3, z.Vc), F32)

    mean, inv, factor, level = norm_coefs(
        ua[...] + ub[...], layer_gain(gains, 3), layer_gain(shifts, 3), C3, z.total // 8
    )
    bs_ref[...] = jnp.zeros(bs_ref.shape, F32)

    def sums(jp, get):
        for k in range(z.nbc):
            value = get(k)
            pre = value * factor + level
            sig = sigmoid(pre)
            grad = gcoarse[jp, :, cols(k)] * (sig * (1.0 + pre * (1.0 - sig)))
            bs_ref[:C3, :] += grad
            bs_ref[C3:, :] += grad * ((value - mean) * inv)

    sums(0, lambda k: yc_lo[0, :, cols(k)].astype(F32))
    sums(z.Zc + 1, lambda k: yc_hi[0, :, cols(k)].astype(F32))

    def own(j, carry):
        sums(j + 1, lambda k: yc[j, :, cols(k)])
        return carry

    lax.fori_loop(0, z.Zc, own, 0)
    if z.two:
        start = jnp.where(meta[0] == 0, z.Zc, 0)
        for m in range(2):
            h_refs[0][m] = gcoarse[start + m].astype(BF)
    else:
        for m in range(2):
            h_refs[0][m] = gcoarse[m].astype(BF)
            h_refs[1][m] = gcoarse[z.Zc + m].astype(BF)
    for t in range(z.Z // 4):
        leaving(t).wait()


def coarse_back_body(z, share, meta, gcoarse, g_lo, g_hi, yc, yc_lo, yc_hi, sa, sb, ba, bb, pooled, gskip, y3,
                     ua, ub, gains, shifts, weight, d_ref, bs_ref, dk_out, *rest):
    h_refs, (p_ref, x_ref, dk_ref) = rest[:-3], rest[-3:]
    mean, inv, factor, level = norm_coefs(
        sa[...] + sb[...], layer_gain(gains, 3), layer_gain(shifts, 3), C3, z.total // 8
    )
    slope, offset = grad_coefs(ba[...] + bb[...], mean, inv, factor, C3, z.total // 8)

    def plane(jp, get_y, extra, valid):
        out = []
        for k in range(z.nbc):
            value = get_y(k)
            pre = value * factor + level
            sig = sigmoid(pre)
            grad = gcoarse[jp, :, cols(k)] + extra(k)
            grad = grad * (sig * (1.0 + pre * (1.0 - sig)))
            grad = factor * grad - slope * value + offset
            out.append(grad if valid is None else jnp.where(valid > 0, grad, 0.0))
        place_windows(p_ref, (jp * (9 * C3),), C3, 0, out, 32)

    def from_lo(m):
        return lambda k: jnp.where(meta[1] > 0, g_lo[m, :, cols(k)].astype(F32), 0.0)

    def from_hi(m):
        return lambda k: jnp.where(meta[2] > 0, g_hi[m, :, cols(k)].astype(F32), 0.0)

    plane(0, lambda k: yc_lo[0, :, cols(k)].astype(F32), from_lo(0), meta[1])
    plane(1, lambda k: yc[0, :, cols(k)], from_lo(1), None)

    def inner(j):
        plane(j + 2, lambda k: yc[j + 1, :, cols(k)], lambda k: 0.0, None)

    if z.Zc > 2:
        unrolled(z.Zc - 2, 3, inner)
    plane(z.Zc, lambda k: yc[z.Zc - 1, :, cols(k)], from_hi(0), None)
    plane(z.Zc + 1, lambda k: yc_hi[0, :, cols(k)].astype(F32), from_hi(1), meta[2])

    edge = jnp.zeros((2 * C2, z.Vc), BF)
    x_ref[: 2 * C2, :] = edge
    x_ref[(z.Zc + 2) * C2 :, :] = edge

    for j in range(z.Zc):
        x_ref[(j + 2) * C2 : (j + 3) * C2, :] = pooled[j + 1]
    mean, inv, factor, level = norm_coefs(
        ua[...] + ub[...], layer_gain(gains, 2), layer_gain(shifts, 2), C2, z.total
    )
    matrix = pool_matrix(mean_entries).astype(F32).T.astype(BF)
    bs_ref[...] = jnp.zeros(bs_ref.shape, F32)
    rows = 9 * C3

    def step(s, carry):
        need(s, y3, gskip)
        result = dot(weight[...], p_ref[ds(s * (2 * rows), 4 * rows), :])
        parts, cross = [], []
        for r in range(2):
            low = result[r * C2 : (r + 1) * C2]
            spread = [None] * z.half
            for k in range(z.nbc):
                both = split_dot(low[:, cols(k)], matrix)
                spread[k], spread[k + z.nbc] = both[:, :128], both[:, 128:]
            for q in range(2):
                at = 4 * s + 2 * r + q
                for k in range(z.nb):
                    value = y3[at, :, cols(k)]
                    pre = value * factor + level
                    sig = sigmoid(pre)
                    grad = spread[k // 2] + gskip[at, :, cols(k)]
                    grad = grad * (sig * (1.0 + pre * (1.0 - sig)))
                    d_ref[at, :, cols(k)] = grad
                    parts.append(grad)
                    cross.append(grad * ((value - mean) * inv))
        bs_ref[:C2, :] += fold_sums(parts)
        bs_ref[C2:, :] += fold_sums(cross)
        return carry

    lax.fori_loop(0, z.Zc // 2, step, 0)
    part = rows // share

    def kernel_grad(zp):
        window = p_ref[ds(zp * rows + meta[3] * part, part), :]
        return dot_nt(window, x_ref[zp * C2 : (zp + 3) * C2, :])

    dk_ref[...] = fold_sums([kernel_grad(zp) for zp in range(z.Zc + 2)])
    pack_wide(dk_out, dk_ref, part)
    send_planes(z, meta, h_refs, lambda i: d_ref[i], 1, z.Z)


def first_back_body(z, meta, d, y1, p_img, sa, sb, ba, bb, gains, shifts, dk_ref, low):
    mean, inv, factor, unused = norm_coefs(
        sa[...] + sb[...], layer_gain(gains, 0), layer_gain(shifts, 0), C1, z.total
    )
    slope, level = grad_coefs(ba[...] + bb[...], mean, inv, factor, C1, z.total)

    def step(i):
        for k in range(z.nb):
            value = factor * d[i, :, cols(k)] - slope * y1[i + 1, :, cols(k)] + level
            low[ds(i * C1, C1), cols(k)] = value.astype(BF)

    unrolled(z.Z, 4, step)
    table = dot_nt(p_img[...], low[...])
    shape = (9 * z.ZP, z.Z * C1)
    gap = lax.rem(lax.broadcasted_iota(jnp.int32, shape, 0), z.ZP) - (
        lax.broadcasted_iota(jnp.int32, shape, 1) // C1
    )
    dk_ref[...] = jnp.zeros(dk_ref.shape, F32)
    for a in range(3):
        kept = jnp.where(gap == a + 1, table, 0.0)
        folded = fold_sums([kept[:, cols(k)] for k in range(z.Z * C1 // 128)])
        folded = folded + roll(folded, 64)
        folded = folded + roll(folded, 32)
        for t in range(9):
            dk_ref[9 * a + t : 9 * a + t + 1, :] = jnp.sum(
                folded[t * z.ZP : (t + 1) * z.ZP], axis=0, keepdims=True
            )


def gather_body(z, meta, *refs):
    ins, (out, norm), (stage, stage_b, flat, column, quarters, full, full_b) = refs[:-9], refs[-9:-7], refs[-7:]
    shared, ins = ins[: z.share], ins[z.share :]
    pairs = [(ins[2 * j], ins[2 * j + 1]) for j in range(len(ins) // 2)]
    (first, second, small_head, small_gate, b_first, b_second, b_third, b_coarse, b_merge, b_final) = pairs
    for k in range(z.share):
        quarters[jnp.bitwise_xor(meta[3], k)] = shared[k][...].astype(F32)

    def unpack(start, count, taps_out):
        part = count // z.share
        width = part if taps_out == C3 else taps_out // z.share
        for k in range(z.share):
            unpack_wide(full, full_b, k, width, taps_out, quarters.at[k], start, part)

    def total(pair):
        return pair[0][...] + pair[1][...]

    def pack(row, taps_out, width):
        count = taps_out * width // 128
        fold = 128 // width
        lane = lanes(count)
        value = stage[pl.ds(0, count, stride=fold), :]
        for j in range(1, fold):
            part = roll(stage[pl.ds(j, count, stride=fold), :], j * width)
            value = jnp.where(lane < j * width, value, part)
        flat[row : row + count, :] = value

    flat[ROWS : ROWS + 8, :] = jnp.zeros((8, 128), F32)
    stage[0:5, :32] = jnp.zeros((5, 32), F32)
    stage[5:32, :32] = (first[0][...] + first[1][...])[:27, :32]
    pack(ROW_FIRST, 32, 32)
    wide_at = 27 * C2 // z.share * 3 // 2
    for row, out_c, in_c, source in (
        (ROW_SECOND, C2, C1, second),
        (ROW_THIRD, C2, C2, 2 * wide_at),
        (ROW_COARSE, C3, C2, wide_at + wide_at // 3),
        (ROW_FINAL, C2, C2, wide_at),
    ):
        count = 9 * out_c
        if source is second:
            full[:count, :] = total(second)
        else:
            unpack(source, count, out_c)
        for t in range(9):
            span = slice(t * out_c, (t + 1) * out_c)
            for a in range(3):
                at = (9 * a + 8 - t) * out_c
                if a * in_c < 128:
                    stage[at : at + out_c, :in_c] = full[span, a * in_c : (a + 1) * in_c]
                else:
                    stage[at : at + out_c, :in_c] = full_b[span, :in_c]
        pack(row, 27 * out_c, in_c)
    unpack(0, 27 * C2, C2)
    for t in range(27):
        at = (26 - t) * C2
        stage[at : at + C2, :] = full[t * C2 : (t + 1) * C2, :]
        stage_b[at : at + C2, :64] = full_b[t * C2 : (t + 1) * C2, :64]
    half = 27 * C2 // 2
    even, even_b = stage[pl.ds(0, half, stride=2), :], stage_b[pl.ds(0, half, stride=2), :]
    odd, odd_b = stage[pl.ds(1, half, stride=2), :], stage_b[pl.ds(1, half, stride=2), :]
    left = lanes(half) < 64
    odd = roll(odd, 64)
    flat[pl.ds(ROW_MERGE, half, stride=3), :] = even
    flat[pl.ds(ROW_MERGE + 1, half, stride=3), :] = jnp.where(left, even_b, odd)
    flat[pl.ds(ROW_MERGE + 2, half, stride=3), :] = jnp.where(left, odd, roll(odd_b, 64))

    gate = total(small_gate)
    turned = gate[:192].T
    stage[:CG, :C2] = turned[:CG, :C2]
    pack(ROW_GATE_SKIP, CG, C2)
    flat[ROW_GATE_COARSE : ROW_GATE_COARSE + CG, :] = turned[:CG, C2:]
    heads = total(small_head)
    lane = lanes(C3)
    column[TAIL_LEN - 7 :, :] = jnp.zeros((2048 - TAIL_LEN + 7, 128), F32)
    column[T_GATE_BIAS : T_GATE_BIAS + CG, :] = gate[192:224]
    column[T_SCORE : T_SCORE + CG, :] = gate[224:256]
    column[T_SCORE_BIAS : T_SCORE_BIAS + 1, :] = gate[256:257]
    for k in range(CLS):
        at = T_HEAD_FINE + k * C2
        column[at : at + C2, :] = jnp.where(lane[:C2] == k, heads[:C2], 0.0)
        at = T_HEAD_COARSE + k * C3
        column[at : at + C3, :] = jnp.where(lane == CG + k, gate[C2:192], 0.0)
    column[T_BIAS_FINE : T_BIAS_FINE + 3, :] = heads[C2 : C2 + 3]
    column[T_BIAS_COARSE : T_BIAS_COARSE + 3, :] = heads[C2 + 16 : C2 + 19]
    for layer, pair in enumerate((b_first, b_second, b_third, b_coarse, b_merge, b_final)):
        sums = total(pair)
        width = WIDTHS[layer]
        at = T_GAINS + NORM_AT[layer]
        column[at : at + width, :] = sums[width : 2 * width]
        at = T_SHIFTS + NORM_AT[layer]
        column[at : at + width, :] = sums[:width]
    for k in range(16):
        flat[ROW_TAIL + k : ROW_TAIL + k + 1, :] = jnp.sum(
            column[k * 128 : (k + 1) * 128, :].T, axis=0, keepdims=True
        )
    chunk = ROWS // 21
    mask = lanes(chunk) < 96

    def finish(i, acc):
        base = pl.multiple_of(i * chunk, 8)
        block = roll(flat[pl.ds(base, chunk + 8), :], 96)
        out[pl.ds(base, chunk), :] = jnp.where(mask, block[1 : chunk + 1], block[2 : chunk + 2])
        return acc + fold_sums([block[8 * m : 8 * m + 8] * block[8 * m : 8 * m + 8] for m in range(chunk // 8)])

    acc = lax.fori_loop(0, 21, finish, jnp.zeros((8, 128), F32))
    sq = jnp.sum(jnp.sum(acc, axis=1, keepdims=True), axis=0, keepdims=True)
    norm[...] = jnp.broadcast_to(jnp.sqrt(sq), (8, 128))


def local(z, images, labels, weights, first_moment, second_moment):
    devices = z.D * z.H
    linear = lax.axis_index("depth") * z.H + lax.axis_index("height")
    position = lax.rem(linear, z.G)
    meta = jnp.stack(
        [position, (position > 0).astype(jnp.int32), (position < z.G - 1).astype(jnp.int32),
         lax.rem(linear // z.G, z.share)]
    ).astype(jnp.int32)

    call = functools.partial(kernel_call, room=12 if z.V <= 1024 else 18)

    def partner(value, step):
        return lax.ppermute(value, AXES, [(i, i ^ step) for i in range(devices)])

    def both(value):
        step = 1
        while step * 2 < z.G:
            value = value + partner(value, step)
            step *= 2
        return value, partner(value, step)

    def neighbours(sent):
        if z.two:
            got = partner(sent[0], 1)
            return got, got
        up = [(i, i + 1) for i in range(devices) if i % z.G != z.G - 1]
        return (
            lax.ppermute(sent[1], AXES, up),
            lax.ppermute(sent[0], AXES, [(j, i) for i, j in up]),
        )

    def shares(values):
        value = jnp.concatenate([one + two for one, two in values], axis=0).astype(BF)
        return [value] + [
            lax.ppermute(value, AXES, [(i, (i // z.G ^ k) * z.G + i % z.G) for i in range(devices)])
            for k in range(1, z.share)
        ]

    def sent(count, channels, lanes_):
        return [((count, channels, lanes_), BF)] * (1 if z.two else 2)

    V, Vc, Z, Zc = z.V, z.Vc, z.Z, z.Zc
    local_rows = z.lz * z.ly
    (mine,) = call(
        lambda *r: mine_body(z, *r), meta, [images, labels], [((devices, local_rows, 128), BF)],
        [pltpu.VMEM((local_rows, 128), F32)],
    )
    everyone = lax.all_to_all(
        mine, AXES, 0, 0
    ).reshape(devices * local_rows, 128)
    flat = jnp.pad(weights, (PAD, ROWS * 128 - PAD - weights.shape[0])).reshape(ROWS, 128)
    tail = jnp.broadcast_to(
        jnp.pad(weights[TAIL_AT:], (0, 1))[:, None], (TAIL_LEN + 1, 128)
    )
    w = prepare(z, meta, flat, tail)
    gains, shifts = w["gains"], w["shifts"]

    def fars(values, base=None):
        return [Far(value, base) for value in values]

    y1, st1, p_img, lab = call(
        lambda *r: first_body(z, *r), meta, [Far(everyone), Far(w["big"])],
        [(((Z + 2) * C1, V), F32), ((72, 128), F32), ((9 * z.ZP, V), BF), ((Z, 8, V), F32)],
        [pltpu.VMEM((devices * local_rows, 128), F32), pltpu.VMEM((z.PY * z.DP, 128), F32)],
    )
    st1 = both(st1)
    parts = [pltpu.VMEM((C2, V), F32), pltpu.VMEM((C2, V), F32)]
    y2, st2, *h2 = call(
        lambda *r: second_body(z, *r), meta, [y1, *st1, gains, shifts, w["second"]],
        [((Z, C2, V), F32), ((2 * C2, 128), F32)] + sent(1, C2, V),
        [pltpu.VMEM((2 * 9 * C1, V), BF), *parts],
    )
    st2, h2 = both(st2), neighbours(h2)
    wide_p = pltpu.VMEM((2 * 9 * C2, V), BF)
    share_p = pltpu.VMEM((2 * 9 * C2 // z.share, V), BF)
    y3, st3, *h3 = call(
        lambda *r: middle_body(z, 1, 2, *r), meta, [y2, *h2, *st2, gains, shifts, w["third"]],
        [((Z, C2, V), F32), ((2 * C2, 128), F32)] + sent(2, C2, V), [wide_p, *parts],
    )
    st3, h3 = both(st3), neighbours(h3)
    skip, pooled, yc, stc, *hc = call(
        lambda *r: coarse_body(z, *r), meta, [y3, *h3, *st3, gains, shifts, w["coarse"]],
        [((Z + 2, C2, V), BF), ((Zc + 2, C2, Vc), BF), ((Zc, C3, Vc), F32), ((2 * C3, 128), F32)]
        + sent(1, C3, Vc),
        [pltpu.VMEM(((Zc + 2) * 9 * C2, Vc), BF)],
    )
    stc, hc = both(stc), neighbours(hc)
    lifted, pre, logits, ym, stm, *hm = call(
        lambda *r: merge_body(z, *r), meta,
        [yc, *hc, *stc, gains, shifts, tail, skip, w["gate"], w["merge"]],
        [((Z + 2, C3, V), BF), ((Z + 2, CG, V), F32), ((Z + 2, 16, V), F32), ((Z, C2, V), F32),
         ((2 * C2, 128), F32)] + sent(1, C2, V),
        [pltpu.VMEM((2 * 9 * 192, V), BF), pltpu.VMEM((2, C3, V), F32), pltpu.VMEM((Zc + 2, C3, Vc), BF),
         pltpu.VMEM((384, V), BF), *parts, pltpu.VMEM((Z + 2, C3, V), BF), pltpu.VMEM((Z + 2, CG, V), F32),
         pltpu.VMEM((Z + 2, 16, V), F32), pltpu.SemaphoreType.DMA((3, Z // 4))],
        hbm_outs=(0, 1, 2),
    )
    stm, hm = both(stm), neighbours(hm)
    yf, stf, *hf = call(
        lambda *r: middle_body(z, 4, 1, *r), meta, [ym, *hm, *stm, gains, shifts, w["final"]],
        [((Z, C2, V), F32), ((2 * C2, 128), F32)] + sent(1, C2, V), [wide_p, *parts],
    )
    stf, hf = both(stf), neighbours(hf)
    counts = fars(st1)
    df, bf, small_head, gc, *hdf = call(
        lambda *r: heads_body(z, *r), meta,
        [yf, *stf, *counts, Far(lab), Far(logits), gains, shifts, tail, w["head"], w["head_t"]],
        [((Z, C2, V), F32), ((2 * C2, 128), F32), ((C2 + 32, 128), F32), ((Z, 16, V), BF)] + sent(1, C2, V),
        [pltpu.VMEM((4 * C2, V), BF)],
    )
    bf, hdf, small_head = both(bf), neighbours(hdf), both(small_head)
    x_wide = pltpu.VMEM(((Z + 4) * C2, V), BF)
    part_rows = 9 * C2 // z.share
    packed = 3 * part_rows // 2
    dk_wide = pltpu.VMEM((part_rows, 192), F32)
    dm, bm, kf, *hdm = call(
        lambda *r: back_body(z, 5, 4, 0, z.share, *r), meta,
        [df, *hdf, yf, *hf, *stf, *bf, ym, *stm, gains, shifts, w["b_final"]],
        [((Z, C2, V), F32), ((2 * C2, 128), F32), ((packed, 128), F32)] + sent(1, C2, V),
        [wide_p, share_p, x_wide, dk_wide, *parts],
    )
    bm, hdm, kf = both(bm), neighbours(hdm), both(kf)
    gskip, gcoarse, bc, km, small_gate, *hg = call(
        lambda *r: merge_back_body(z, z.share, *r), meta,
        [dm, *hdm, ym, *hm, *stm, *bm, Far(skip, 1), Far(lifted, 1), Far(pre, 1), Far(gc, 0),
         yc, *hc, *stc, gains, shifts, tail, w["b_merge"], w["gate_t"]],
        [((Z, C2, V), F32), ((Zc + 2, C3, Vc), F32), ((2 * C3, 128), F32), ((3 * packed, 128), F32),
         ((264, 128), F32)] + sent(2, C3, Vc),
        [pltpu.VMEM((6 * 9 * C2, V), BF), pltpu.VMEM((6 * 9 * C2 // z.share, V), BF), pltpu.VMEM((96, V), BF), pltpu.VMEM((512, V), BF),
         pltpu.VMEM((Zc + 2, C3, V // 2), F32), pltpu.VMEM((3 * part_rows + 48, 256), F32),
         pltpu.VMEM((Z, C2, V), F32), pltpu.SemaphoreType.DMA((Z // 4,))],
        hbm_outs=(0,),
    )
    bc, hg, km, small_gate = both(bc), neighbours(hg), both(km), both(small_gate)
    d3, b3, kc, *hd3 = call(
        lambda *r: coarse_back_body(z, z.share, *r), meta,
        [gcoarse, *hg, yc, *hc, *stc, *bc, pooled, Far(gskip, 0), Far(y3, 0), *st3,
         gains, shifts, w["b_coarse"]],
        [((Z, C2, V), F32), ((2 * C2, 128), F32), ((2 * packed, 128), F32)] + sent(1, C2, V),
        [pltpu.VMEM(((Zc + 2) * 9 * C3, Vc), BF), pltpu.VMEM(((Zc + 4) * C2, Vc), BF),
         pltpu.VMEM((2 * part_rows, 192), F32)],
    )
    b3, hd3, kc = both(b3), neighbours(hd3), both(kc)
    d2, b2, k3, *hd2 = call(
        lambda *r: back_body(z, 2, 1, 0, z.share, *r), meta,
        [d3, *hd3, Far(y3, 0), *h3, *st3, *b3, Far(y2, 0), *st2, gains, shifts, w["b_third"]],
        [((Z, C2, V), F32), ((2 * C2, 128), F32), ((packed, 128), F32)] + sent(1, C2, V),
        [wide_p, share_p, x_wide, dk_wide, *parts],
    )
    b2, hd2, shared = both(b2), neighbours(hd2), shares([km, kf, kc, both(k3)])
    y1_planes = y1.reshape(Z + 2, C1, V)
    d1, b1, k2 = call(
        lambda *r: back_body(z, 1, 0, 1, 1, *r), meta,
        [d2, *hd2, Far(y2, 0), *h2, *st2, *b2, Far(y1_planes, 1), *st1, gains, shifts,
         w["b_second"], ],
        [((Z, C1, V), F32), ((2 * C1, 128), F32), ((9 * C2, 128), F32)],
        [wide_p, share_p, pltpu.VMEM(((Z + 4) * C1, V), BF), pltpu.VMEM((9 * C2, 3 * C1), F32), pltpu.VMEM((C1, V), F32), pltpu.VMEM((C1, V), F32)],
    )
    b1, k2 = both(b1), both(k2)
    (k1,) = call(
        lambda *r: first_back_body(z, *r), meta,
        [d1, Far(y1_planes), Far(p_img), *fars(st1), *b1, gains, shifts, *[Held(part) for part in shared]],
        [((32, 128), F32)], [pltpu.VMEM((Z * C1, V), BF)],
    )
    k1 = both(k1)
    pieces = (k1, k2, small_head, small_gate, b1, b2, b3, bc, bm, bf)
    grad, norm = call(
        lambda *r: gather_body(z, *r), meta,
        fars(shared) + [Far(part) for pair in pieces for part in pair],
        [((ROWS, 128), F32), ((8, 128), F32)],
        [pltpu.VMEM((27 * C3, 128), F32), pltpu.VMEM((27 * C2, 128), F32),
         pltpu.VMEM((ROWS + 8, 128), F32), pltpu.VMEM((2048, 128), F32)]
        + [pltpu.VMEM((z.share, 7 * packed, 128), F32)] + [pltpu.VMEM((27 * C2, 128), F32)] * 2,
    )
    gradient = grad.reshape(ROWS * 128)[: weights.shape[0]]
    grad_norm = norm[0, 0]
    clipped = gradient * jnp.minimum(1.0, CLIP_NORM / (grad_norm + 1e-06))
    moment_one = BETA_ONE * first_moment + (1.0 - BETA_ONE) * clipped
    moment_two = BETA_TWO * second_moment + (1.0 - BETA_TWO) * clipped * clipped
    corrected_one = moment_one / (1.0 - BETA_ONE**STEP)
    corrected_two = moment_two / (1.0 - BETA_TWO**STEP)
    updated = weights - LEARN_RATE * (
        corrected_one / (jnp.sqrt(corrected_two) + ADAM_EPS) + DECAY_RATE * weights
    )
    return (grad_norm, moment_one, moment_two, updated, updated.astype(BF))


def solution(mesh):
    depth, height = mesh.shape["depth"], mesh.shape["height"]

    def step(images, labels, weights, first_moment, second_moment):
        z = Sizes(depth, height, images.shape[1] // depth, images.shape[2] // height, images.shape[3])
        placed = (P(None, "depth", "height", None), P(None, "depth", "height", None), P(), P(), P())
        return jax.shard_map(
            lambda *arrays: local(z, *arrays), mesh=mesh, in_specs=placed,
            out_specs=(P(), P(), P(), P(), P()), check_vma=False,
        )(images, labels, weights, first_moment, second_moment)

    return step
```
